32 devices in a mesh: depth: 2 (over x), sky: 16 (over z, y, core).
Axes of the slice: x: 2, y: 2, z: 4, core: 2. Of those that a mesh axis runs over, the one named last changes fastest.
Arguments:
- potential: float32 [24, 512, 2048], P('depth', 'sky'), may hold values from -6 to 6
- widths: int32 [24], P('depth'), may hold values from 1 to 8, as said below
- plane_slot: int32 [24], P('depth'), may hold values from 0 to 15
- ratio_near: float32 [16], replicated, may hold values from 1 to 1.6
- ratio_lens: float32 [16], replicated, may hold values from 0.5 to 1.5
Outputs:
- convergence: float32 [24, 512, 2048], P('depth', 'sky')
The draws below stay inside these ranges and needn't reach their ends.
Inputs may be any that keep to these rules, and one draw needn't show every extreme that they name: `widths`: some plane has half-width 8.
All inputs are finite; a program needn't handle non-finite values.
Results may differ from the reference program's by a relative error of at most 0.0003.
Values sent between devices are 32-bit elements; how exact they have to be, the bound alone decides.
No kernel may reach another device: no remote copies, remote signals or barrier semaphores. Data moves between devices by JAX's collectives and lax.ppermute only.
A program may use at most 64 MiB of HBM per device.

```python
import jax
import jax.numpy as jnp
from jax import lax

PL_DEV = 12
COLS = 2048
WMAX = 8
TABLE = 16
PLANES = 24
ROWS = 512


def draw_widths(key, part):
    first_key = jax.random.fold_in(key, 11)
    second_key = jax.random.fold_in(key, 23)
    base_widths = jax.random.randint(first_key, (PLANES,), 1, WMAX + 1)
    block_count = PLANES // PL_DEV
    position = jax.random.randint(second_key, (block_count,), 0, PL_DEV)
    lanes = jnp.arange(PLANES, dtype=jnp.int32) % PL_DEV
    blocks = jnp.arange(PLANES, dtype=jnp.int32) // PL_DEV
    return jnp.where(lanes == position[blocks], WMAX, base_widths).astype(jnp.int32)


def place_ends(entries, own_key, least, top_value):
    spot = [jax.random.randint(jax.random.fold_in(own_key, axis), (), 0, length) for axis, length in enumerate(entries.shape)]
    main_axis = entries.shape.index(max(entries.shape))
    next_to = spot[:main_axis] + [(spot[main_axis] + 1) % entries.shape[main_axis]] + spot[main_axis + 1:]
    return entries.at[tuple(spot)].set(least).at[tuple(next_to)].set(top_value)


def levels(own_key, dims, shards, low, high):
    factor_of, own = 1.0, jax.random.fold_in(own_key, 6)
    for dim, parts in shards:
        draws = jnp.exp(jax.random.uniform(jax.random.fold_in(own, dim), (parts,), jnp.float32, low / len(shards), high / len(shards)))
        factor_of = factor_of * jnp.repeat(draws, dims[dim] // parts).reshape([-1 if axis == dim else 1 for axis in range(len(dims))])
    return factor_of


def bell_draw(own_key, shape, scale, most, pieces=(), kind=jnp.bfloat16):
    values = scale * jax.random.normal(own_key, shape, jnp.float32)
    if pieces:
        values = values * levels(own_key, shape, pieces, -0.22, 0.18)
    return jnp.clip(values, -most, most).astype(kind)


def setup_inputs(seed: int = 0) -> dict:
    keys = jax.random.split(jax.random.key(seed), 6)
    return {
        "potential": bell_draw(keys[0], (PLANES, ROWS, COLS), 0.5, 6.0, ((0, 2), (1, 16)), jnp.float32),
        "widths": draw_widths(jax.random.fold_in(keys[5], 71), 0),
        "plane_slot": place_ends(jax.random.randint(keys[2], (PLANES,), 0, TABLE), jax.random.fold_in(keys[2], 1), 0, TABLE - 1).astype(jnp.int32),
        "ratio_near": jnp.clip(jax.random.uniform(keys[3], (TABLE,), jnp.float32, 1.0, 1.6), 1.0, 1.6),
        "ratio_lens": jnp.clip(jax.random.uniform(keys[4], (TABLE,), jnp.float32, 0.5, 1.5), 0.5, 1.5),
    }


def box_filter(values, half_width, axis_index, length):
    summed = None
    for displace in range(-WMAX, WMAX + 1):
        window = lax.slice_in_dim(values, WMAX + displace, WMAX + displace + length, axis=axis_index)
        active = jnp.where(abs(displace) <= half_width, 1.0, 0.0).astype(jnp.float32)
        term = active * window
        summed = term if summed is None else summed + term
    return summed / (2.0 * half_width.astype(jnp.float32) + 1.0)


def hessian(padded, half_width, row_count, col_count):
    along = box_filter(padded, half_width, 0, row_count + 2)
    smooth = box_filter(along, half_width, 1, col_count + 2)
    centre = smooth[1:-1, 1:-1]
    along_cols = smooth[1:-1, 2:] - 2.0 * centre + smooth[1:-1, :-2]
    along_rows = smooth[2:, 1:-1] - 2.0 * centre + smooth[:-2, 1:-1]
    mixed_term = 0.25 * (smooth[2:, 2:] - smooth[2:, :-2] - smooth[:-2, 2:] + smooth[:-2, :-2])
    return along_cols, along_rows, mixed_term


def advance(carried, along_cols, along_rows, mixed_term, near_factor, lens_factor):
    entry_xx = near_factor - lens_factor * along_cols
    entry_yy = near_factor - lens_factor * along_rows
    entry_xy = -lens_factor * mixed_term
    retained = 1.0 - near_factor
    upper = carried[0:2]
    lower = carried[2:4]
    row_first = entry_xx * upper[0] + entry_xy * upper[1] + retained * lower[0]
    row_second = entry_xy * upper[0] + entry_yy * upper[1] + retained * lower[1]
    advanced = jnp.stack([row_first, row_second, upper[0], upper[1]])
    convergence = 1.0 - 0.5 * (row_first[0] + row_second[1])
    return advanced, convergence


def identity_state(row_count, col_count):
    pattern = jnp.array([[1.0, 0.0], [0.0, 1.0], [1.0, 0.0], [0.0, 1.0]], dtype=jnp.float32)
    return jnp.broadcast_to(pattern[:, :, None, None], (4, 2, row_count, col_count)).astype(jnp.float32)


def reference(potential, widths, plane_slot, ratio_near, ratio_lens):
    row_count = potential.shape[1]
    col_count = potential.shape[2]
    table_ids = jnp.arange(ratio_near.shape[0], dtype=jnp.int32)

    def plane(carried, inputs):
        plane_map, half_width, slot_id = inputs
        chosen = (slot_id == table_ids).astype(jnp.float32)
        near_factor = jnp.sum(chosen * ratio_near)
        lens_factor = jnp.sum(chosen * ratio_lens)
        padded = jnp.pad(plane_map, WMAX + 1)
        along_cols, along_rows, mixed_term = hessian(padded, half_width, row_count, col_count)
        return advance(carried, along_cols, along_rows, mixed_term, near_factor, lens_factor)

    initial = identity_state(row_count, col_count)
    final_state, convergence = lax.scan(plane, initial, (potential, widths, plane_slot))
    return convergence
```

```python
import functools

import jax
import jax.numpy as jnp
from jax import lax
from jax.experimental import pallas as pl
from jax.experimental.pallas import tpu as pltpu
from jax.sharding import PartitionSpec as P

WMAX = 8
RIM = WMAX + 1
LANES = 128
SUB = 8
EDGES = (RIM, 5, 0)
VMEM_LIMIT = 16 * 1024 * 1024
F32 = jnp.float32


def row_groups(row_count):
    groups = [((RIM, row_count - RIM),)]
    for outer, inner in zip(EDGES[:-1], EDGES[1:]):
        groups.append(((inner, outer), (row_count - outer, row_count - inner)))
    return groups


def rows_in(group):
    return sum(stop - start for start, stop in group)


class ShiftLeft:
    def __init__(self, lane, distance):
        self.lane, self.distance, self.held = lane, distance, None

    def __call__(self, block):
        zero = jnp.zeros((SUB, LANES), F32)
        rolled = zero if block is None else pltpu.roll(block, LANES - self.distance, 1)
        held = zero if self.held is None else self.held
        self.held = rolled
        return jnp.where(self.lane < LANES - self.distance, rolled, held)


class ShiftRight:
    def __init__(self, lane, distance):
        self.lane, self.distance, self.held = lane, distance, None

    def __call__(self, block):
        rolled = pltpu.roll(block, self.distance, 1) if self.distance else block
        held, self.held = self.held, rolled
        if held is None:
            return None
        return jnp.where(self.lane >= self.distance, held, rolled) if self.distance else held


def window_sums(lane, half_width):
    shift = lambda distance: ShiftLeft(lane, distance)
    plus = lambda a, b: b if a is None else a + b
    s = [shift(d) for d in {1: (1, 2), 2: (1, 2, 4), 3: (1, 2, 3, 6), 4: (1, 2, 3, 6), 5: (1, 2, 4, 2, 8),
                            6: (1, 2, 3, 6, 12), 7: (1, 2, 3, 5, 10), 8: (1, 2, 4, 8, 16)}[half_width]]

    def sums(x):
        p2 = plus(x, s[0](x))
        if half_width in (2, 5, 8):
            p4 = p2 + s[1](p2)
            if half_width == 2:
                return p4 + s[2](x)
            p8 = p4 + s[2](p4)
            if half_width == 5:
                return p8 + s[4](p2 + s[3](x))
            return p8 + s[3](p8) + s[4](x)
        p3 = p2 + s[1](x)
        if half_width == 1:
            return p3
        if half_width == 7:
            p5 = p3 + s[2](p2)
            return p5 + s[3](p5) + s[4](p5)
        p6 = p3 + s[2](p3)
        if half_width == 3:
            return p6 + s[3](x)
        if half_width == 4:
            return p6 + s[3](p3)
        return p6 + s[3](p6) + s[4](x)

    return sums


def column_stage(blocks, half_width, load, store):
    lane = lax.broadcasted_iota(jnp.int32, (SUB, LANES), 1)
    sums = window_sums(lane, half_width)
    right = [ShiftRight(lane, half_width + step) for step in (0, -1, 1)]
    for block in range(blocks - 1, -2, -1):
        total = sums(load(block) if block >= 0 else None)
        centre, after, before = [shift(total) for shift in right]
        if centre is not None:
            store(block + 1, (centre, after + before - 2.0 * centre, after - before))


def for_each_width(half_width, body):
    for candidate in range(1, WMAX + 1):

        @pl.when(half_width == candidate)
        def _(candidate=candidate):
            body(candidate)


def own_columns(k, half_width, rows, blocks, x_ref, field_ref):
    def with_width(static_width):
        def tile(index, carry):
            base = index * (SUB * blocks)

            def load(block):
                return x_ref[k, pl.ds(pl.multiple_of(base + block * SUB, SUB), SUB), :]

            def store(block, values):
                start = base + RIM * blocks + block
                for field, value in enumerate(values):
                    field_ref[k, field, pl.ds(start, SUB, stride=blocks), :] = value

            column_stage(blocks, static_width, load, store)
            return carry

        lax.fori_loop(0, rows // SUB, tile, 0)

    for_each_width(half_width, with_width)


def halo_columns(k, half_width, rows, blocks, sides, tile_ref, stage_ref, field_ref):
    places = []
    for ref, first, count in sides:
        for i in range(count):
            slot = len(places)
            places.append(first + i)
            for half in range(blocks // SUB):
                start = (slot // SUB) * SUB * blocks + half * SUB * SUB + slot % SUB
                tile_ref[pl.ds(start, SUB, stride=SUB), :] = ref[k, pl.ds(i * blocks + half * SUB, SUB), :]
    tiles = -(-len(places) // SUB)

    def with_width(static_width):
        for index in range(tiles):
            base = index * (SUB * blocks)

            def load(block):
                return tile_ref[pl.ds(base + block * SUB, SUB), :]

            def store(block, values):
                for field, value in enumerate(values):
                    stage_ref[field, pl.ds(base + block, SUB, stride=blocks), :] = value

            column_stage(blocks, static_width, load, store)

    for_each_width(half_width, with_width)
    for slot, row in enumerate(places):
        for field in range(3):
            field_ref[k, field, pl.ds((row + RIM) * blocks, blocks), :] = stage_ref[
                field, pl.ds(slot * blocks, blocks), :
            ]


def row_stage(k, half_width, near, scale, group, blocks, field_ref, entry_ref):
    def row(field, index):
        return field_ref[k, field, pl.ds(pl.multiple_of(index * blocks, blocks), blocks), :]

    place = 0
    for start, stop in group:
        first = start + RIM
        along = lax.fori_loop(
            0, 2 * half_width + 1, lambda i, total: total + row(1, first - half_width + i),
            jnp.zeros((blocks, LANES), F32),
        )
        for at in range(first, stop + RIM):
            high, low = at + half_width, at - half_width
            across = (row(0, high + 1) - row(0, high)) - (row(0, low) - row(0, low - 1))
            mixed = (row(2, high + 1) + row(2, high)) - (row(2, low) + row(2, low - 1))
            where = pl.ds(place * blocks, blocks)
            entry_ref[k, 0, where, :] = near - scale * along
            entry_ref[k, 1, where, :] = near - scale * across
            entry_ref[k, 2, where, :] = (-0.25 * scale) * mixed
            if at + 1 < stop + RIM:
                along = along + (row(1, high + 1) - row(1, low))
            place += 1


def sweep(planes, length, near_of, entry_ref, conv_ref, start, finish):
    step = 4 * SUB if length % (4 * SUB) == 0 else SUB

    def part(index, carry):
        where = pl.ds(pl.multiple_of(index * step, step), step)
        state = start(where, (step, LANES))
        now, then = state[:4], state[4:]
        for k in range(planes):
            xx, yy, xy = [entry_ref[k, i, where, :] for i in range(3)]
            kept = 1.0 - near_of(k)
            new = [
                xx * now[0] + xy * now[2] + kept * then[0],
                xx * now[1] + xy * now[3] + kept * then[1],
                xy * now[0] + yy * now[2] + kept * then[2],
                xy * now[1] + yy * now[3] + kept * then[3],
            ]
            now, then = new, now
            conv_ref[k, where, :] = 1.0 - 0.5 * (new[0] + new[3])
        finish(where, now + then)
        return carry

    lax.fori_loop(0, length // step, part, 0)


def identity_state(where, shape):
    one, zero = jnp.ones(shape, F32), jnp.zeros(shape, F32)
    return [one, zero, zero, one] * 2


def writer(state_ref):
    def finish(where, state):
        for i, value in enumerate(state):
            state_ref[i, where, :] = value

    return finish


def scalars_of(k, widths, slots, near, lens):
    half_width = widths[k]
    count = (2 * half_width + 1).astype(F32)
    return half_width, near[slots[k]], lens[slots[k]] / (count * count)


def first_kernel(sizes, widths, slots, near, lens, x_hbm, field_ref, entry_ref, conv_ref, state_ref, *rest):
    planes, rows, blocks, groups = sizes
    sends, (x_ref, sems) = rest[:-2], rest[-2:]
    copies = [pltpu.make_async_copy(x_hbm.at[k], x_ref.at[k], sems.at[k]) for k in range(planes)]
    for copy in copies:
        copy.start()
    group = groups[0]

    def plane(k, carry):
        pltpu.make_async_copy(x_hbm.at[k], x_ref.at[k], sems.at[k]).wait()
        half_width, near_k, scale = scalars_of(k, widths, slots, near, lens)
        own_columns(k, half_width, rows, blocks, x_ref, field_ref)
        row_stage(k, half_width, near_k, scale, group, blocks, field_ref, entry_ref)
        for part, (outer, inner) in enumerate(zip(EDGES[:-1], EDGES[1:])):
            begin, count = RIM - outer, outer - inner
            for ref, first in ((sends[2 * part], rows - begin - count), (sends[2 * part + 1], begin)):
                for i in range(count):
                    row = first + i
                    for half in range(blocks // SUB):
                        start = (row // SUB) * SUB * blocks + half * SUB * SUB + row % SUB
                        ref[k, pl.ds(i * blocks + half * SUB, SUB), :] = x_ref[k, pl.ds(start, SUB, stride=SUB), :]
        return carry

    lax.fori_loop(0, planes, plane, 0)

    @pl.when(lax.axis_index("depth") == 0)
    def _():
        sweep(planes, rows_in(group) * blocks, lambda k: near[slots[k]], entry_ref, conv_ref, identity_state,
              writer(state_ref))


def later_kernel(sizes, part, widths, slots, near, lens, field_in, before, after, field_ref, entry_ref, conv_ref,
                 state_ref, tile_ref, stage_ref):
    planes, rows, blocks, groups = sizes
    group = groups[part + 1]
    outer, inner = EDGES[part], EDGES[part + 1]
    begin, count = RIM - outer, outer - inner

    def plane(k, carry):
        half_width, near_k, scale = scalars_of(k, widths, slots, near, lens)
        sides = ((before, -begin - count, count), (after, rows + begin, count))
        halo_columns(k, half_width, rows, blocks, sides, tile_ref, stage_ref, field_ref)
        row_stage(k, half_width, near_k, scale, group, blocks, field_ref, entry_ref)
        return carry

    lax.fori_loop(0, planes, plane, 0)

    @pl.when(lax.axis_index("depth") == 0)
    def _():
        sweep(planes, rows_in(group) * blocks, lambda k: near[slots[k]], entry_ref, conv_ref, identity_state,
              writer(state_ref))


def resume_kernel(sizes, part, turn, slots, near, entry_ref, incoming, conv_in, conv_ref, *state_ref):
    planes, rows, blocks, groups = sizes

    @pl.when(lax.axis_index("depth") == turn)
    def _():
        sweep(planes, rows_in(groups[part]) * blocks, lambda k: near[slots[k]], entry_ref, conv_ref,
              lambda where, shape: [incoming[i, where, :] for i in range(8)],
              writer(state_ref[0]) if state_ref else lambda where, state: None)


def gather_kernel(sizes, *refs):
    planes, rows, blocks, groups = sizes
    out_ref = refs[-1]
    k = pl.program_id(0)
    for group, conv_ref in zip(groups, refs):
        place = 0
        for start, stop in group:
            for row in range(start, stop):
                for half in range(blocks // SUB):
                    to = (row // SUB) * SUB * blocks + half * SUB * SUB + row % SUB
                    out_ref[0, pl.ds(to, SUB, stride=SUB), :] = conv_ref[k, pl.ds(place * blocks + half * SUB, SUB), :]
                place += 1


def per_device(potential, widths, plane_slot, ratio_near, ratio_lens):
    planes, rows, cols = potential.shape
    blocks = cols // LANES
    groups = row_groups(rows)
    sizes = (planes, rows, blocks, groups)
    depth_count, sky_count = lax.axis_size("depth"), lax.axis_size("sky")
    up = [(i, i + 1) for i in range(sky_count - 1)]
    down = [(j, i) for i, j in up]
    ahead = [(i, i + 1) for i in range(depth_count - 1)]
    tiled = potential.reshape(planes, rows // SUB, SUB, blocks, LANES).transpose(0, 1, 3, 2, 4)
    tiled = tiled.reshape(planes, rows * blocks, LANES)
    smem = pl.BlockSpec(memory_space=pltpu.SMEM)
    vmem = pl.BlockSpec(memory_space=pltpu.VMEM)
    params = pltpu.CompilerParams(vmem_limit_bytes=VMEM_LIMIT)
    scalars = (widths, plane_slot, ratio_near, ratio_lens)

    def held(*shape):
        return pltpu.VMEM(shape, F32)

    def moved(*shape):
        return jax.ShapeDtypeStruct(shape, F32)

    field_shape = held(planes, 3, (rows + 2 * RIM) * blocks, LANES)

    def group_shapes(part):
        length = rows_in(groups[part]) * blocks
        return [held(planes, 3, length, LANES), held(planes, length, LANES), moved(8, length, LANES)]

    sends = []
    for outer, inner in zip(EDGES[:-1], EDGES[1:]):
        sends += [moved(planes, (outer - inner) * blocks, LANES)] * 2
    field, entry, conv, state, *packed = pl.pallas_call(
        functools.partial(first_kernel, sizes),
        out_shape=[field_shape, *group_shapes(0), *sends],
        in_specs=[smem] * 4 + [pl.BlockSpec(memory_space=pl.ANY)],
        out_specs=[vmem] * (4 + len(sends)),
        scratch_shapes=[pltpu.VMEM((planes, rows * blocks, LANES), F32), pltpu.SemaphoreType.DMA((planes,))],
        compiler_params=params,
        name="interior",
    )(*scalars, tiled)
    entries, convs, states = [entry], [conv], [state]
    for part, (outer, inner) in enumerate(zip(EDGES[:-1], EDGES[1:])):
        before = lax.ppermute(packed[2 * part], "sky", up)
        after = lax.ppermute(packed[2 * part + 1], "sky", down)
        slots = -(-2 * (outer - inner) // SUB) * SUB
        field, entry, conv, state = pl.pallas_call(
            functools.partial(later_kernel, sizes, part),
            out_shape=[field_shape, *group_shapes(part + 1)],
            in_specs=[smem] * 4 + [vmem] * 3,
            out_specs=[vmem] * 4,
            scratch_shapes=[held(slots * blocks, LANES), held(3, slots * blocks, LANES)],
            input_output_aliases={4: 0},
            compiler_params=params,
            name="border",
        )(*scalars, pltpu.with_memory_space_constraint(field, pltpu.VMEM), before, after)
        entries.append(entry)
        convs.append(conv)
        states.append(state)

    for turn in range(1, depth_count):
        last = turn == depth_count - 1
        for part in range(len(groups)):
            incoming = lax.ppermute(states[part], "depth", ahead)
            conv, *state = pl.pallas_call(
                functools.partial(resume_kernel, sizes, part, turn),
                out_shape=group_shapes(part)[1:2] + ([] if last else group_shapes(part)[2:3]),
                in_specs=[smem] * 2 + [vmem] * 3,
                out_specs=[vmem] * (1 if last else 2),
                input_output_aliases={4: 0},
                compiler_params=params,
                name="resume",
            )(plane_slot, ratio_near, pltpu.with_memory_space_constraint(entries[part], pltpu.VMEM), incoming,
              pltpu.with_memory_space_constraint(convs[part], pltpu.VMEM))
            convs[part] = conv
            if state:
                states[part] = state[0]

    out = pl.pallas_call(
        functools.partial(gather_kernel, sizes),
        grid=(planes,),
        out_shape=moved(planes, rows * blocks, LANES),
        in_specs=[vmem] * len(groups),
        out_specs=pl.BlockSpec((1, rows * blocks, LANES), lambda k: (k, 0, 0)),
        compiler_params=params,
        name="gather",
    )(*[pltpu.with_memory_space_constraint(conv, pltpu.VMEM) for conv in convs])
    out = out.reshape(planes, rows // SUB, blocks, SUB, LANES).transpose(0, 1, 3, 2, 4)
    return out.reshape(planes, rows, cols)


def solution(mesh):
    return jax.shard_map(
        per_device,
        mesh=mesh,
        in_specs=(P("depth", "sky", None), P("depth"), P("depth"), P(), P()),
        out_specs=P("depth", "sky", None),
        check_vma=False,
    )
```

```python
import functools

import jax
import jax.numpy as jnp
from jax import lax
from jax.experimental import pallas as pl
from jax.experimental.pallas import tpu as pltpu
from jax.sharding import PartitionSpec as P

WMAX = 8
RIM = WMAX + 1
LANES = 128
SUB = 8
EDGES = (RIM, 4, 0)
VMEM_LIMIT = 16 * 1024 * 1024
PACK = 16
INNER = 2
F32, BF16 = jnp.float32, jnp.bfloat16


def row_groups(row_count):
    middle = row_count // 2 + 2
    groups = [((RIM, middle),), ((middle, row_count - RIM),)]
    for outer, inner in zip(EDGES[:-1], EDGES[1:]):
        groups.append(((inner, outer), (row_count - outer, row_count - inner)))
    return groups


def rows_in(group):
    return sum(stop - start for start, stop in group)


def split(value):
    high = value.astype(BF16)
    rest = value - high.astype(F32)
    middle = rest.astype(BF16)
    return high, middle, (rest - middle.astype(F32)).astype(BF16)


def band(half_width, band_ref):
    source = lax.broadcasted_iota(jnp.int32, (2 * LANES, LANES), 0)
    target = lax.broadcasted_iota(jnp.int32, (2 * LANES, LANES), 1)
    offset = jnp.where(source >= LANES + LANES // 2, source - 2 * LANES, source) - target
    distance = jnp.abs(offset)
    rim = (distance == half_width + 1).astype(F32)
    edge = (distance == half_width).astype(F32)
    inside = (distance <= half_width).astype(F32)
    both = rim + edge
    fields = (inside, rim - edge, jnp.where(offset > 0, both, -both))
    for field, value in enumerate(fields):
        value = value.astype(BF16)
        for part in range(3):
            band_ref[part * 2 * LANES:(part + 1) * 2 * LANES, field * LANES:(field + 1) * LANES] = value


def clear_ends(blocks, height, left_ref):
    zero = jnp.zeros((height, LANES // 2), BF16)
    for part in range(3):
        at = part * 2 * LANES + LANES
        left_ref[(blocks - 1) * height:blocks * height, at:at + LANES // 2] = zero
        left_ref[0:height, at + LANES // 2:at + LANES] = zero


def column_stage(half_width, blocks, height, load, left_ref, band_ref):
    half = LANES // 2
    band(half_width, band_ref)
    for block in range(blocks):
        here = slice(block * height, (block + 1) * height)
        for part, value in enumerate(split(load(block))):
            at = part * 2 * LANES
            left_ref[here, at:at + LANES] = value
            if block > 0:
                left_ref[(block - 1) * height:block * height, at + LANES:at + LANES + half] = value[:, :half]
            if block < blocks - 1:
                left_ref[(block + 1) * height:(block + 2) * height, at + LANES + half:at + 2 * LANES] = value[:, half:]
    return jnp.dot(left_ref[...], band_ref[...], preferred_element_type=F32)


def own_columns(k, half_width, rows, blocks, x_ref, field_ref, left_ref, band_ref):
    tiles = rows // SUB

    def load(block):
        return jnp.concatenate(
            [x_ref[k, pl.ds((tile * blocks + block) * SUB, SUB), :] for tile in range(tiles)], axis=0)

    result = column_stage(half_width, blocks, rows, load, left_ref, band_ref)
    for block in range(blocks):
        for tile in range(tiles):
            from_row = block * rows + tile * SUB
            start = (tile * SUB + RIM) * blocks + block
            for field in range(3):
                field_ref[k, field, pl.ds(start, SUB, stride=blocks), :] = result[
                    from_row:from_row + SUB, field * LANES:(field + 1) * LANES]


def halo_height(count):
    return -(-2 * count // PACK) * PACK


def halo_columns(k, half_width, blocks, sides, tile_ref, stage_ref, field_ref, left_ref, band_ref):
    places = []
    height = halo_height(sides[0][2])
    for ref, first, count in sides:
        for i in range(count):
            slot = len(places)
            places.append(first + i)
            for half in range(blocks // SUB):
                tile_ref[pl.ds(half * SUB * height + slot, SUB, stride=height), :] = ref[
                    k, pl.ds(i * blocks + half * SUB, SUB), :]

    def load(block):
        return tile_ref[pl.ds(block * height, height), :]

    result = column_stage(half_width, blocks, height, load, left_ref, band_ref)
    for block in range(blocks):
        for first in range(0, len(places), SUB):
            from_row = block * height + first
            for field in range(3):
                stage_ref[field, pl.ds(first * blocks + block, SUB, stride=blocks), :] = result[
                    from_row:from_row + SUB, field * LANES:(field + 1) * LANES]
    for slot, row in enumerate(places):
        for field in range(3):
            field_ref[k, field, pl.ds((row + RIM) * blocks, blocks), :] = stage_ref[
                field, pl.ds(slot * blocks, blocks), :]


def row_stage(k, half_width, near, scale, group, blocks, field_ref, entry_ref):
    def row(field, index):
        return field_ref[k, field, pl.ds(pl.multiple_of(index * blocks, blocks), blocks), :]

    place = 0
    for start, stop in group:
        first = start + RIM
        along = row(1, first)
        for step in range(1, WMAX + 1):
            pair = row(1, first - step) + row(1, first + step)
            along = along + jnp.where(step <= half_width, pair, 0.0)
        for at in range(first, stop + RIM):
            high, low = at + half_width, at - half_width
            across = (row(0, high + 1) - row(0, high)) - (row(0, low) - row(0, low - 1))
            mixed = (row(2, high + 1) + row(2, high)) - (row(2, low) + row(2, low - 1))
            where = pl.ds(place * blocks, blocks)
            entry_ref[k, 0, where, :] = near - scale * along
            entry_ref[k, 1, where, :] = near - scale * across
            entry_ref[k, 2, where, :] = (-0.25 * scale) * mixed
            if at + 1 < stop + RIM:
                along = along + (row(1, high + 1) - row(1, low))
            place += 1


def sweep(planes, length, near_of, entry_ref, conv_ref, start, finish):
    step = next(count * SUB for count in (4, 3, 2, 1) if length % (count * SUB) == 0)

    def part(index, carry):
        where = pl.ds(pl.multiple_of(index * step, step), step)
        state = start(where, (step, LANES))
        now, then = state[:4], state[4:]
        for k in range(planes):
            xx, yy, xy = [entry_ref[k, i, where, :] for i in range(3)]
            kept = 1.0 - near_of(k)
            new = [
                xx * now[0] + xy * now[2] + kept * then[0],
                xx * now[1] + xy * now[3] + kept * then[1],
                xy * now[0] + yy * now[2] + kept * then[2],
                xy * now[1] + yy * now[3] + kept * then[3],
            ]
            now, then = new, now
            conv_ref[k, where, :] = 1.0 - 0.5 * (new[0] + new[3])
        finish(where, now + then)
        return carry

    lax.fori_loop(0, length // step, part, 0)


def identity_state(where, shape):
    one, zero = jnp.ones(shape, F32), jnp.zeros(shape, F32)
    return [one, zero, zero, one] * 2


def writer(state_ref):
    def finish(where, state):
        for i, value in enumerate(state):
            state_ref[i, where, :] = value

    return finish


def scalars_of(k, widths, slots, near, lens):
    half_width = widths[k]
    count = (2 * half_width + 1).astype(F32)
    return half_width, near[slots[k]], lens[slots[k]] / (count * count)


def first_kernel(sizes, widths_hbm, slots_hbm, near_hbm, lens_hbm, x_hbm, field_ref, *rest):
    planes, rows, blocks, groups = sizes
    parts, rest = [rest[3 * part:3 * part + 3] for part in range(INNER)], rest[3 * INNER:]
    sends, (x_ref, widths, slots, near, lens, left_ref, band_ref, plane_sems, table_sems) = rest[:-9], rest[-9:]
    tables = ((widths_hbm, widths), (slots_hbm, slots), (near_hbm, near), (lens_hbm, lens))
    copies = [pltpu.make_async_copy(*pair, table_sems.at[i]) for i, pair in enumerate(tables)]
    for copy in copies:
        copy.start()

    def plane_copy(k):
        return pltpu.make_async_copy(x_hbm.at[k], x_ref.at[k], plane_sems.at[k])

    for k in range(planes):
        plane_copy(k).start()
    clear_ends(blocks, rows, left_ref)
    for copy in copies:
        copy.wait()

    def plane(k, carry):
        plane_copy(k).wait()
        half_width, near_k, scale = scalars_of(k, widths, slots, near, lens)
        own_columns(k, half_width, rows, blocks, x_ref, field_ref, left_ref, band_ref)
        for group, (entry_ref, _, _) in zip(groups, parts):
            row_stage(k, half_width, near_k, scale, group, blocks, field_ref, entry_ref)
        for part, (outer, inner) in enumerate(zip(EDGES[:-1], EDGES[1:])):
            begin, count = RIM - outer, outer - inner
            for ref, first in ((sends[2 * part], rows - begin - count), (sends[2 * part + 1], begin)):
                for i in range(count):
                    row = first + i
                    for half in range(blocks // SUB):
                        start = (row // SUB) * SUB * blocks + half * SUB * SUB + row % SUB
                        ref[k, pl.ds(i * blocks + half * SUB, SUB), :] = x_ref[k, pl.ds(start, SUB, stride=SUB), :]
        return carry

    lax.fori_loop(0, planes, plane, 0)

    @pl.when(lax.axis_index("depth") == 0)
    def _():
        for group, (entry_ref, conv_ref, state_ref) in zip(groups, parts):
            sweep(planes, rows_in(group) * blocks, lambda k: near[slots[k]], entry_ref, conv_ref, identity_state,
                  writer(state_ref))


def later_kernel(sizes, part, widths, slots, near, lens, field_in, before, after, behind, field_ref, entry_ref, conv_ref,
                 state_ref, tile_ref, stage_ref, left_ref, band_ref):
    planes, rows, blocks, groups = sizes
    group = groups[INNER + part]
    outer, inner = EDGES[part], EDGES[part + 1]
    begin, count = RIM - outer, outer - inner
    height = halo_height(count)
    clear_ends(blocks, height, left_ref)
    tile_ref[...] = jnp.zeros(tile_ref.shape, F32)

    def plane(k, carry):
        half_width, near_k, scale = scalars_of(k, widths, slots, near, lens)
        sides = ((before, -begin - count, count), (after, rows + begin, count))
        halo_columns(k, half_width, blocks, sides, tile_ref, stage_ref, field_ref, left_ref, band_ref)
        row_stage(k, half_width, near_k, scale, group, blocks, field_ref, entry_ref)
        return carry

    lax.fori_loop(0, planes, plane, 0)

    @pl.when(lax.axis_index("depth") == 0)
    def _():
        sweep(planes, rows_in(group) * blocks, lambda k: near[slots[k]], entry_ref, conv_ref, identity_state,
              writer(state_ref))


def resume(sizes, part, turn, slots, near, entry_ref, incoming, conv_ref, finish):
    planes, rows, blocks, groups = sizes

    @pl.when(lax.axis_index("depth") == turn)
    def _():
        sweep(planes, rows_in(groups[part]) * blocks, lambda k: near[slots[k]], entry_ref, conv_ref,
              lambda where, shape: [incoming[i, where, :] for i in range(8)], finish)


def resume_kernel(sizes, part, turn, slots, near, entry_ref, incoming, conv_in, conv_ref, *state_ref):
    finish = writer(state_ref[0]) if state_ref else lambda where, state: None
    resume(sizes, part, turn, slots, near, entry_ref, incoming, conv_ref, finish)


def last_kernel(sizes, turn, slots, near, entry_ref, incoming, conv_in, *refs):
    planes, rows, blocks, groups = sizes
    others, (conv_ref, out_hbm, tiles_ref, sems) = refs[:-4], refs[-4:]
    part = len(groups) - 1
    resume(sizes, part, turn, slots, near, entry_ref, incoming, conv_ref, lambda where, state: None)

    def plane_copy(k):
        return pltpu.make_async_copy(tiles_ref.at[k], out_hbm.at[k], sems.at[k])

    def plane(k, carry):
        for group, ref in zip(groups, (*others, conv_ref)):
            place = 0
            for start, stop in group:
                for row in range(start, stop):
                    for half in range(blocks // SUB):
                        to = (row // SUB) * SUB * blocks + half * SUB * SUB + row % SUB
                        tiles_ref[k, pl.ds(to, SUB, stride=SUB), :] = ref[k, pl.ds(place * blocks + half * SUB, SUB), :]
                    place += 1
        plane_copy(k).start()
        return carry

    lax.fori_loop(0, planes, plane, 0)
    for k in range(planes):
        plane_copy(k).wait()


def per_device(potential, widths, plane_slot, ratio_near, ratio_lens):
    planes, rows, cols = potential.shape
    blocks = cols // LANES
    groups = row_groups(rows)
    sizes = (planes, rows, blocks, groups)
    depth_count, sky_count = lax.axis_size("depth"), lax.axis_size("sky")
    up = [(i, i + 1) for i in range(sky_count - 1)]
    down = [(j, i) for i, j in up]
    ahead = [(i, i + 1) for i in range(depth_count - 1)]
    tiled = potential.reshape(planes, rows // SUB, SUB, blocks, LANES).transpose(0, 1, 3, 2, 4)
    tiled = tiled.reshape(planes, rows * blocks, LANES)
    smem = pl.BlockSpec(memory_space=pltpu.SMEM)
    vmem = pl.BlockSpec(memory_space=pltpu.VMEM)
    anywhere = pl.BlockSpec(memory_space=pl.ANY)
    params = pltpu.CompilerParams(vmem_limit_bytes=VMEM_LIMIT)
    scalars = (widths, plane_slot, ratio_near, ratio_lens)
    dma = pltpu.SemaphoreType.DMA
    cost = pl.CostEstimate(flops=1, transcendentals=0, bytes_accessed=1)

    def held(*shape, dtype=F32):
        return pltpu.VMEM(shape, dtype)

    def moved(*shape):
        return jax.ShapeDtypeStruct(shape, F32)

    def in_vmem(array):
        return pltpu.with_memory_space_constraint(array, pltpu.VMEM)

    def in_hbm(array):
        return pltpu.with_memory_space_constraint(array, pltpu.HBM)

    field_shape = held(planes, 3, (rows + 2 * RIM) * blocks, LANES)

    def group_shapes(part):
        length = rows_in(groups[part]) * blocks
        return [held(planes, 3, length, LANES), held(planes, length, LANES), moved(8, length, LANES)]

    def matrix_scratch(height):
        return [held(blocks * height, 6 * LANES, dtype=BF16), held(6 * LANES, 3 * LANES, dtype=BF16)]

    sends = []
    for outer, inner in zip(EDGES[:-1], EDGES[1:]):
        sends += [held(planes, (outer - inner) * blocks, LANES)] * 2
    field, *made = pl.pallas_call(
        functools.partial(first_kernel, sizes),
        out_shape=[field_shape, *sum((group_shapes(part) for part in range(INNER)), []), *sends],
        in_specs=[anywhere] * 5,
        out_specs=[vmem] * (1 + 3 * INNER + len(sends)),
        scratch_shapes=[
            held(planes, rows * blocks, LANES), *[pltpu.SMEM(array.shape, array.dtype) for array in scalars],
            *matrix_scratch(rows), dma((planes,)), dma((len(scalars),))],
        compiler_params=params,
        cost_estimate=cost,
        name="interior",
    )(*[in_hbm(array) for array in (*scalars, tiled)])
    entries, convs, states = [made[i:3 * INNER:3] for i in range(3)]
    packed = made[3 * INNER:]
    arriving = [lax.ppermute(state, "depth", ahead) for state in states]
    for part, (outer, inner) in enumerate(zip(EDGES[:-1], EDGES[1:])):
        before = lax.ppermute(packed[2 * part], "sky", up)
        after = lax.ppermute(packed[2 * part + 1], "sky", down)
        height = halo_height(outer - inner)
        field, entry, conv, state = pl.pallas_call(
            functools.partial(later_kernel, sizes, part),
            out_shape=[field_shape, *group_shapes(INNER + part)],
            in_specs=[smem] * 4 + [vmem] * 3 + [anywhere],
            out_specs=[vmem] * 4,
            scratch_shapes=[held(height * blocks, LANES), held(3, height * blocks, LANES), *matrix_scratch(height)],
            input_output_aliases={4: 0},
            compiler_params=params,
            cost_estimate=cost,
            name="border",
        )(*scalars, in_vmem(field), before, after, arriving[part])
        entries.append(entry)
        convs.append(conv)
        arriving.append(lax.ppermute(state, "depth", ahead))

    for turn in range(1, depth_count):
        last = turn == depth_count - 1
        for part in range(len(groups) - last):
            convs[part], *state = pl.pallas_call(
                functools.partial(resume_kernel, sizes, part, turn),
                out_shape=group_shapes(part)[1:2] + ([] if last else group_shapes(part)[2:3]),
                in_specs=[smem] * 2 + [vmem] * 3,
                out_specs=[vmem] * (1 if last else 2),
                input_output_aliases={4: 0},
                compiler_params=params,
                cost_estimate=cost,
                name="resume",
            )(plane_slot, ratio_near, in_vmem(entries[part]), arriving[part], in_vmem(convs[part]))
            if state:
                arriving[part] = lax.ppermute(state[0], "depth", ahead)

    conv, out = pl.pallas_call(
        functools.partial(last_kernel, sizes, depth_count - 1),
        out_shape=[group_shapes(len(groups) - 1)[1], moved(planes, rows * blocks, LANES)],
        in_specs=[smem] * 2 + [vmem] * (3 + len(groups) - 1),
        out_specs=[vmem, anywhere],
        scratch_shapes=[held(planes, rows * blocks, LANES), dma((planes,))],
        input_output_aliases={4: 0},
        compiler_params=params,
        cost_estimate=cost,
        name="last",
    )(plane_slot, ratio_near, in_vmem(entries[-1]), arriving[-1], in_vmem(convs[-1]),
      *[in_vmem(conv) for conv in convs[:-1]])
    out = out.reshape(planes, rows // SUB, blocks, SUB, LANES).transpose(0, 1, 3, 2, 4)
    return out.reshape(planes, rows, cols)


def solution(mesh):
    return jax.shard_map(
        per_device,
        mesh=mesh,
        in_specs=(P("depth", "sky", None), P("depth"), P("depth"), P(), P()),
        out_specs=P("depth", "sky", None),
        check_vma=False,
    )
```

```python
import functools

import jax
import jax.numpy as jnp
from jax import lax
from jax.experimental import pallas as pl
from jax.experimental.pallas import tpu as pltpu
from jax.sharding import PartitionSpec as P

WMAX = 8
RIM = WMAX + 1
LANES = 128
SUB = 8
EDGES = (RIM, 4, 0)
INNER_ROWS = 4
PARTS = (3, 2, 2)
VMEM_LIMIT = 16 * 1024 * 1024
INNER = 2
F32, BF16 = jnp.float32, jnp.bfloat16


def row_groups(row_count):
    first = (row_count - INNER_ROWS) // 2
    groups = [((first, first + INNER_ROWS),), ((RIM, first), (first + INNER_ROWS, row_count - RIM))]
    for outer, inner in zip(EDGES[:-1], EDGES[1:]):
        groups.append(((inner, outer), (row_count - outer, row_count - inner)))
    return groups


def rows_in(group):
    return sum(stop - start for start, stop in group)


def split(value, parts):
    found = []
    for part in range(parts):
        found.append(value.astype(BF16))
        if part + 1 < parts:
            value = value - found[-1].astype(F32)
    return found


def make_bands(planes, widths, band_ref):
    source = lax.broadcasted_iota(jnp.int32, (LANES, 2 * LANES), 0)
    target = lax.broadcasted_iota(jnp.int32, (LANES, 2 * LANES), 1)
    across = jnp.where(target >= LANES + LANES // 2, source + 2 * LANES, source)
    offset = across - target
    distance = jnp.abs(offset)

    def plane(k, carry):
        half_width = widths[k]
        rim = (distance == half_width + 1).astype(F32)
        edge = (distance == half_width).astype(F32)
        inside = (distance <= half_width).astype(F32)
        both = rim + edge
        for field, value in enumerate((rim - edge, jnp.where(offset > 0, both, -both), inside)):
            band_ref[k, field] = value.astype(BF16)
        return carry

    lax.fori_loop(0, planes, plane, 0)


def entries_of(k, half_width, near, scale, group, blocks, x_ref, band_ref, left_ref, beside_ref, entry_ref):
    def row(index):
        return x_ref[k, pl.ds(pl.multiple_of(index * blocks, blocks), blocks), :]

    place = 0
    for start, stop in group:
        first = start + RIM
        total = row(first)
        for step in range(1, WMAX + 1):
            total = total + jnp.where(step <= half_width, row(first - step) + row(first + step), 0.0)
        for at in range(first, stop + RIM):
            high, low = at + half_width, at - half_width
            rim_high, edge_high, edge_low, rim_low = row(high + 1), row(high), row(low), row(low - 1)
            values = (total, (rim_high + edge_high) - (edge_low + rim_low),
                      (rim_high - edge_high) - (edge_low - rim_low))
            total = total + (rim_high - edge_low)
            here = slice(place * blocks, (place + 1) * blocks)
            for field, value in enumerate(values):
                for part, piece in enumerate(split(value, PARTS[field])):
                    left_ref[field, here, part * LANES:(part + 1) * LANES] = piece
            place += 1
    length = place * blocks
    pitch = blocks + SUB
    left_lane = lax.broadcasted_iota(jnp.int32, (blocks, LANES), 1) < LANES // 2
    factors = (-scale, -0.25 * scale, -scale)
    added = (near, 0.0, near)
    for field in range(3):
        weight = jnp.concatenate([band_ref[k, field]] * PARTS[field], axis=0)
        product = jnp.dot(left_ref[field, :length, :PARTS[field] * LANES], weight, preferred_element_type=F32)
        for at in range(place):
            beside_ref[field, pl.ds(at * pitch + SUB, blocks), :] = product[at * blocks:(at + 1) * blocks, LANES:]
        for at in range(place):
            beside = jnp.where(left_lane, beside_ref[field, pl.ds(at * pitch + SUB - 1, blocks), :],
                               beside_ref[field, pl.ds(at * pitch + SUB + 1, blocks), :])
            value = factors[field] * (product[at * blocks:(at + 1) * blocks, :LANES] + beside)
            entry_ref[k, field, pl.ds(at * blocks, blocks), :] = value + added[field] if field != 1 else value


def sweep(planes, length, near_of, entry_ref, conv_ref, start, finish):
    step = next(count * SUB for count in (4, 3, 2, 1) if length % (count * SUB) == 0)

    def part(index, carry):
        where = pl.ds(pl.multiple_of(index * step, step), step)
        state = start(where, (step, LANES))
        now, then = state[:4], state[4:]
        for k in range(planes):
            xx, xy, yy = [entry_ref[k, i, where, :] for i in range(3)]
            kept = 1.0 - near_of(k)
            new = [
                xx * now[0] + xy * now[2] + kept * then[0],
                xx * now[1] + xy * now[3] + kept * then[1],
                xy * now[0] + yy * now[2] + kept * then[2],
                xy * now[1] + yy * now[3] + kept * then[3],
            ]
            now, then = new, now
            conv_ref[k, where, :] = 1.0 - 0.5 * (new[0] + new[3])
        finish(where, now + then)
        return carry

    lax.fori_loop(0, length // step, part, 0)


def identity_state(where, shape):
    one, zero = jnp.ones(shape, F32), jnp.zeros(shape, F32)
    return [one, zero, zero, one] * 2


def writer(state_ref):
    def finish(where, state):
        for i, value in enumerate(state):
            state_ref[i, where, :] = value

    return finish


def group_stage(sizes, part, scalars, x_ref, band_ref, left_ref, beside_ref, entry_ref, conv_ref, state_ref,
                before_plane=lambda k: None):
    planes, rows, blocks, groups = sizes
    widths, slots, near, lens = scalars
    beside_ref[...] = jnp.zeros(beside_ref.shape, F32)

    def plane(k, carry):
        before_plane(k)
        half_width = widths[k]
        count = (2 * half_width + 1).astype(F32)
        entries_of(k, half_width, near[slots[k]], lens[slots[k]] / (count * count), groups[part], blocks, x_ref,
                   band_ref, left_ref, beside_ref, entry_ref)
        return carry

    lax.fori_loop(0, planes, plane, 0)

    @pl.when(lax.axis_index("depth") == 0)
    def _():
        sweep(planes, rows_in(groups[part]) * blocks, lambda k: near[slots[k]], entry_ref, conv_ref, identity_state,
              writer(state_ref))


def first_kernel(sizes, widths_hbm, slots_hbm, near_hbm, lens_hbm, potential_hbm, x_ref, band_ref, entry_ref, conv_ref,
                 state_ref, left_ref, beside_ref, tiles_ref, widths, slots, near, lens, plane_sems, table_sems):
    planes, rows, blocks, groups = sizes
    tables = ((widths_hbm, widths), (slots_hbm, slots), (near_hbm, near), (lens_hbm, lens))
    copies = [pltpu.make_async_copy(*pair, table_sems.at[i]) for i, pair in enumerate(tables)]
    for copy in copies:
        copy.start()

    def plane_copy(k):
        return pltpu.make_async_copy(potential_hbm.at[k], tiles_ref.at[k], plane_sems.at[k])

    for k in range(planes):
        plane_copy(k).start()
    for copy in copies:
        copy.wait()
    make_bands(planes, widths, band_ref)

    def arrive(k):
        plane_copy(k).wait()
        for row in range(rows):
            for half in range(blocks // SUB):
                start = (row // SUB) * SUB * blocks + half * SUB * SUB + row % SUB
                x_ref[k, pl.ds((row + RIM) * blocks + half * SUB, SUB), :] = tiles_ref[
                    k, pl.ds(start, SUB, stride=SUB), :]

    group_stage(sizes, 0, (widths, slots, near, lens), x_ref, band_ref, left_ref, beside_ref, entry_ref, conv_ref,
                state_ref, arrive)


def second_kernel(sizes, widths, slots, near, lens, x_ref, band_ref, entry_ref, conv_ref, state_ref, *rest):
    planes, rows, blocks, groups = sizes
    sends, (left_ref, beside_ref) = rest[:-2], rest[-2:]

    def leave(k):
        for part, (outer, inner) in enumerate(zip(EDGES[:-1], EDGES[1:])):
            begin, count = RIM - outer, outer - inner
            for ref, first in ((sends[2 * part], rows - begin - count), (sends[2 * part + 1], begin)):
                ref[k] = x_ref[k, pl.ds((first + RIM) * blocks, count * blocks), :]

    group_stage(sizes, 1, (widths, slots, near, lens), x_ref, band_ref, left_ref, beside_ref, entry_ref, conv_ref,
                state_ref, leave)


def border_kernel(sizes, part, widths, slots, near, lens, x_in, band_ref, before, after, behind, x_ref, entry_ref,
                  conv_ref, state_ref, left_ref, beside_ref):
    planes, rows, blocks, groups = sizes
    outer, inner = EDGES[part], EDGES[part + 1]
    begin, count = RIM - outer, outer - inner

    def arrive(k):
        x_ref[k, pl.ds((RIM - begin - count) * blocks, count * blocks), :] = before[k]
        x_ref[k, pl.ds((RIM + rows + begin) * blocks, count * blocks), :] = after[k]

    group_stage(sizes, INNER + part, (widths, slots, near, lens), x_ref, band_ref, left_ref, beside_ref, entry_ref,
                conv_ref, state_ref, arrive)


def resume(sizes, part, turn, slots, near, entry_ref, incoming, conv_ref, finish):
    planes, rows, blocks, groups = sizes

    @pl.when(lax.axis_index("depth") == turn)
    def _():
        sweep(planes, rows_in(groups[part]) * blocks, lambda k: near[slots[k]], entry_ref, conv_ref,
              lambda where, shape: [incoming[i, where, :] for i in range(8)], finish)


def resume_kernel(sizes, part, turn, slots, near, entry_ref, incoming, conv_in, conv_ref, *state_ref):
    finish = writer(state_ref[0]) if state_ref else lambda where, state: None
    resume(sizes, part, turn, slots, near, entry_ref, incoming, conv_ref, finish)


def last_kernel(sizes, turn, slots, near, entry_ref, incoming, conv_in, *refs):
    planes, rows, blocks, groups = sizes
    others, (conv_ref, out_hbm, tiles_ref, sems) = refs[:-4], refs[-4:]
    part = len(groups) - 1
    resume(sizes, part, turn, slots, near, entry_ref, incoming, conv_ref, lambda where, state: None)

    def plane_copy(k):
        return pltpu.make_async_copy(tiles_ref.at[k], out_hbm.at[k], sems.at[k])

    def plane(k, carry):
        for group, ref in zip(groups, (*others, conv_ref)):
            place = 0
            for start, stop in group:
                for row in range(start, stop):
                    for half in range(blocks // SUB):
                        to = (row // SUB) * SUB * blocks + half * SUB * SUB + row % SUB
                        tiles_ref[k, pl.ds(to, SUB, stride=SUB), :] = ref[k, pl.ds(place * blocks + half * SUB, SUB), :]
                    place += 1
        plane_copy(k).start()
        return carry

    lax.fori_loop(0, planes, plane, 0)
    for k in range(planes):
        plane_copy(k).wait()


def per_device(potential, widths, plane_slot, ratio_near, ratio_lens):
    planes, rows, cols = potential.shape
    blocks = cols // LANES
    groups = row_groups(rows)
    sizes = (planes, rows, blocks, groups)
    depth_count, sky_count = lax.axis_size("depth"), lax.axis_size("sky")
    up = [(i, i + 1) for i in range(sky_count - 1)]
    down = [(j, i) for i, j in up]
    ahead = [(i, i + 1) for i in range(depth_count - 1)]
    tiled = potential.reshape(planes, rows // SUB, SUB, blocks, LANES).transpose(0, 1, 3, 2, 4)
    tiled = tiled.reshape(planes, rows * blocks, LANES)
    smem = pl.BlockSpec(memory_space=pltpu.SMEM)
    vmem = pl.BlockSpec(memory_space=pltpu.VMEM)
    anywhere = pl.BlockSpec(memory_space=pl.ANY)
    params = pltpu.CompilerParams(vmem_limit_bytes=VMEM_LIMIT)
    scalars = (widths, plane_slot, ratio_near, ratio_lens)
    dma = pltpu.SemaphoreType.DMA
    cost = pl.CostEstimate(flops=1, transcendentals=0, bytes_accessed=1)

    def held(*shape, dtype=F32):
        return pltpu.VMEM(shape, dtype)

    def moved(*shape):
        return jax.ShapeDtypeStruct(shape, F32)

    def in_vmem(array):
        return pltpu.with_memory_space_constraint(array, pltpu.VMEM)

    def in_hbm(array):
        return pltpu.with_memory_space_constraint(array, pltpu.HBM)

    x_shape = held(planes, (rows + 2 * RIM) * blocks, LANES)
    band_shape = held(planes, 3, LANES, 2 * LANES, dtype=BF16)

    def group_shapes(part):
        length = rows_in(groups[part]) * blocks
        return [held(planes, 3, length, LANES), held(planes, length, LANES), moved(8, length, LANES)]

    def group_scratch(part):
        count = rows_in(groups[part])
        return [held(3, count * blocks, max(PARTS) * LANES, dtype=BF16),
                held(3, (count + 1) * (blocks + SUB), LANES)]

    sends = []
    for outer, inner in zip(EDGES[:-1], EDGES[1:]):
        sends += [moved(planes, (outer - inner) * blocks, LANES)] * 2
    x, bands, *group = pl.pallas_call(
        functools.partial(first_kernel, sizes),
        out_shape=[x_shape, band_shape, *group_shapes(0)],
        in_specs=[anywhere] * 5,
        out_specs=[vmem] * 5,
        scratch_shapes=[
            *group_scratch(0), held(planes, rows * blocks, LANES),
            *[pltpu.SMEM(array.shape, array.dtype) for array in scalars], dma((planes,)), dma((len(scalars),))],
        compiler_params=params,
        cost_estimate=cost,
        name="first",
    )(*[in_hbm(array) for array in (*scalars, tiled)])
    made = [group]
    arriving = [lax.ppermute(group[2], "depth", ahead)]
    *group, = pl.pallas_call(
        functools.partial(second_kernel, sizes),
        out_shape=[*group_shapes(1), *sends],
        in_specs=[smem] * 4 + [vmem] * 2,
        out_specs=[vmem] * (3 + len(sends)),
        scratch_shapes=group_scratch(1),
        compiler_params=params,
        cost_estimate=cost,
        name="second",
    )(*scalars, in_vmem(x), in_vmem(bands))
    group, packed = group[:3], group[3:]
    made.append(group)
    arriving.append(lax.ppermute(group[2], "depth", ahead))
    for part, (outer, inner) in enumerate(zip(EDGES[:-1], EDGES[1:])):
        before = lax.ppermute(packed[2 * part], "sky", up)
        after = lax.ppermute(packed[2 * part + 1], "sky", down)
        x, *group = pl.pallas_call(
            functools.partial(border_kernel, sizes, part),
            out_shape=[x_shape, *group_shapes(INNER + part)],
            in_specs=[smem] * 4 + [vmem] * 4 + [anywhere],
            out_specs=[vmem] * 4,
            scratch_shapes=group_scratch(INNER + part),
            input_output_aliases={4: 0},
            compiler_params=params,
            cost_estimate=cost,
            name="border",
        )(*scalars, in_vmem(x), in_vmem(bands), before, after, arriving[part])
        made.append(group)
        arriving.append(lax.ppermute(group[2], "depth", ahead))
    entries, convs = [group[0] for group in made], [group[1] for group in made]

    for turn in range(1, depth_count):
        last = turn == depth_count - 1
        for part in range(len(groups) - last):
            convs[part], *state = pl.pallas_call(
                functools.partial(resume_kernel, sizes, part, turn),
                out_shape=group_shapes(part)[1:2] + ([] if last else group_shapes(part)[2:3]),
                in_specs=[smem] * 2 + [vmem] * 3,
                out_specs=[vmem] * (1 if last else 2),
                input_output_aliases={4: 0},
                compiler_params=params,
                cost_estimate=cost,
                name="resume",
            )(plane_slot, ratio_near, in_vmem(entries[part]), arriving[part], in_vmem(convs[part]))
            if state:
                arriving[part] = lax.ppermute(state[0], "depth", ahead)

    conv, out = pl.pallas_call(
        functools.partial(last_kernel, sizes, depth_count - 1),
        out_shape=[group_shapes(len(groups) - 1)[1], moved(planes, rows * blocks, LANES)],
        in_specs=[smem] * 2 + [vmem] * (3 + len(groups) - 1),
        out_specs=[vmem, anywhere],
        scratch_shapes=[held(planes, rows * blocks, LANES), dma((planes,))],
        input_output_aliases={4: 0},
        compiler_params=params,
        cost_estimate=cost,
        name="last",
    )(plane_slot, ratio_near, in_vmem(entries[-1]), arriving[-1], in_vmem(convs[-1]),
      *[in_vmem(conv) for conv in convs[:-1]])
    out = out.reshape(planes, rows // SUB, blocks, SUB, LANES).transpose(0, 1, 3, 2, 4)
    return out.reshape(planes, rows, cols)


def solution(mesh):
    return jax.shard_map(
        per_device,
        mesh=mesh,
        in_specs=(P("depth", "sky", None), P("depth"), P("depth"), P(), P()),
        out_specs=P("depth", "sky", None),
        check_vma=False,
    )
```

```python
import functools

import jax
import jax.numpy as jnp
from jax import lax
from jax.experimental import pallas as pl
from jax.experimental.pallas import tpu as pltpu
from jax.sharding import PartitionSpec as P

WMAX = 8
RIM = WMAX + 1
LANES = 128
SUB = 8
WEIGHT = 100000000
TOGETHER = 4
PARTS = (3, 2, 2)
VMEM_LIMIT = 16 * 1024 * 1024
F32, BF16 = jnp.float32, jnp.bfloat16


def group_sizes(row_count):
    return (row_count - 2 * RIM, RIM, RIM)


def side_starts(row_count):
    low, high = (0, -RIM), (row_count - RIM, row_count)
    even = lax.rem(lax.axis_index("sky"), 2) == 0
    paired = [jnp.where(even, b, a) for a, b in zip(low, high)]
    other = [jnp.where(even, a, b) for a, b in zip(low, high)]
    return paired, other


def first_row(row_count, part):
    return RIM if part == 0 else side_starts(row_count)[part - 1][0]


def split(value, parts):
    found = []
    for part in range(parts):
        found.append(value.astype(BF16))
        if part + 1 < parts:
            value = value - found[-1].astype(F32)
    return found


def make_bands(planes, widths, band_ref):
    source = lax.broadcasted_iota(jnp.int32, (LANES, 2 * LANES), 0)
    target = lax.broadcasted_iota(jnp.int32, (LANES, 2 * LANES), 1)
    across = jnp.where(target >= LANES + LANES // 2, source + 2 * LANES, source)
    offset = across - target
    distance = jnp.abs(offset)

    def plane(k, carry):
        half_width = widths[k]
        rim = (distance == half_width + 1).astype(F32)
        edge = (distance == half_width).astype(F32)
        inside = (distance <= half_width).astype(F32)
        both = rim + edge
        for field, value in enumerate((rim - edge, jnp.where(offset > 0, both, -both), inside)):
            band_ref[k, field] = value.astype(BF16)
        return carry

    lax.fori_loop(0, planes, plane, 0)


def build(k, half_width, first, count, blocks, x_ref, left_ref):
    def row(index):
        return x_ref[k, pl.ds(pl.multiple_of(index * blocks, blocks), blocks), :]

    total = row(first)
    for step in range(1, WMAX + 1):
        total = total + jnp.where(step <= half_width, row(first - step) + row(first + step), 0.0)
    for i in range(count):
        high, low = first + i + half_width, first + i - half_width
        rim_high, edge_high, edge_low, rim_low = row(high + 1), row(high), row(low), row(low - 1)
        values = (total, (rim_high + edge_high) - (edge_low + rim_low),
                  (rim_high - edge_high) - (edge_low - rim_low))
        total = total + (rim_high - edge_low)
        here = slice(i * blocks, (i + 1) * blocks)
        for field, value in enumerate(values):
            for part, piece in enumerate(split(value, PARTS[field])):
                left_ref[field, here, part * LANES:(part + 1) * LANES] = piece


def multiply(k, field, band_ref, left_ref):
    weight = jnp.concatenate([band_ref[k, field]] * PARTS[field], axis=0)
    return jnp.dot(left_ref[field, :, :PARTS[field] * LANES], weight, preferred_element_type=F32)


def combine(k, field, near, scale, blocks, product, beside_ref, entry_ref):
    pitch = blocks + SUB
    count = product.shape[0] // blocks
    left_lane = lax.broadcasted_iota(jnp.int32, (blocks, LANES), 1) < LANES // 2
    factor = -0.25 * scale if field == 1 else -scale
    for at in range(count):
        beside_ref[field, pl.ds(at * pitch + SUB, blocks), :] = product[at * blocks:(at + 1) * blocks, LANES:]
    for at in range(count):
        beside = jnp.where(left_lane, beside_ref[field, pl.ds(at * pitch + SUB - 1, blocks), :],
                           beside_ref[field, pl.ds(at * pitch + SUB + 1, blocks), :])
        value = factor * (product[at * blocks:(at + 1) * blocks, :LANES] + beside)
        entry_ref[k, field, pl.ds(at * blocks, blocks), :] = value if field == 1 else value + near


def sweep(planes, length, near_of, entry_ref, conv_ref, start, finish):
    step = next(count * SUB for count in (4, 3, 2, 1) if length % (count * SUB) == 0)

    def part(index, carry):
        where = pl.ds(pl.multiple_of(index * step, step), step)
        state = start(where, (step, LANES))
        now, then = state[:4], state[4:]
        for k in range(planes):
            xx, xy, yy = [entry_ref[k, i, where, :] for i in range(3)]
            kept = 1.0 - near_of(k)
            new = [
                xx * now[0] + xy * now[2] + kept * then[0],
                xx * now[1] + xy * now[3] + kept * then[1],
                xy * now[0] + yy * now[2] + kept * then[2],
                xy * now[1] + yy * now[3] + kept * then[3],
            ]
            now, then = new, now
            conv_ref[k, where, :] = 1.0 - 0.5 * (new[0] + new[3])
        finish(where, now + then)
        return carry

    lax.fori_loop(0, length // step, part, 0)


def identity_state(where, shape):
    one, zero = jnp.ones(shape, F32), jnp.zeros(shape, F32)
    return [one, zero, zero, one] * 2


def writer(state_ref):
    def finish(where, state):
        for i, value in enumerate(state):
            state_ref[i, where, :] = value

    return finish


def group_stage(sizes, part, scalars, x_ref, band_ref, left_refs, beside_refs, entry_ref, conv_ref, state_ref,
                before_plane=lambda k: None):
    planes, rows, blocks = sizes
    widths, slots, near, lens = scalars
    first, count = first_row(rows, part) + RIM, group_sizes(rows)[part]
    together = len(left_refs)
    for beside_ref in beside_refs:
        beside_ref[...] = jnp.zeros(beside_ref.shape, F32)

    def step(index, carry):
        ks = [index * together + i for i in range(together)]
        for k in ks:
            before_plane(k)
        for k, left_ref in zip(ks, left_refs):
            build(k, widths[k], first, count, blocks, x_ref, left_ref)
        for field in range(3):
            for k, left_ref, beside_ref in zip(ks, left_refs, beside_refs):
                width = (2 * widths[k] + 1).astype(F32)
                combine(k, field, near[slots[k]], lens[slots[k]] / (width * width), blocks,
                        multiply(k, field, band_ref, left_ref), beside_ref, entry_ref)
        return carry

    lax.fori_loop(0, planes // together, step, 0)

    @pl.when(lax.axis_index("depth") == 0)
    def _():
        sweep(planes, group_sizes(rows)[part] * blocks, lambda k: near[slots[k]], entry_ref, conv_ref, identity_state,
              writer(state_ref))


def first_kernel(sizes, widths_hbm, slots_hbm, near_hbm, lens_hbm, potential_hbm, x_ref, band_ref, entry_ref, conv_ref,
                 state_ref, paired_ref, other_ref, *scratch):
    planes, rows, blocks = sizes
    scratch, (tiles_ref, widths, slots, near, lens, plane_sems, table_sems) = scratch[:-7], scratch[-7:]
    tables = ((widths_hbm, widths), (slots_hbm, slots), (near_hbm, near), (lens_hbm, lens))
    copies = [pltpu.make_async_copy(*pair, table_sems.at[i]) for i, pair in enumerate(tables)]
    for copy in copies:
        copy.start()

    def plane_copy(k):
        return pltpu.make_async_copy(potential_hbm.at[k], tiles_ref.at[k], plane_sems.at[k])

    for k in range(planes):
        plane_copy(k).start()
    for copy in copies:
        copy.wait()
    make_bands(planes, widths, band_ref)
    sides = [(start + RIM) * blocks for start, _ in side_starts(rows)]

    def arrive(k):
        plane_copy(k).wait()
        for row in range(rows):
            for half in range(blocks // SUB):
                start = (row // SUB) * SUB * blocks + half * SUB * SUB + row % SUB
                x_ref[k, pl.ds((row + RIM) * blocks + half * SUB, SUB), :] = tiles_ref[
                    k, pl.ds(start, SUB, stride=SUB), :]
        for ref, side in zip((paired_ref, other_ref), sides):
            ref[k] = x_ref[k, pl.ds(pl.multiple_of(side, blocks), RIM * blocks), :]

    group_stage(sizes, 0, (widths, slots, near, lens), x_ref, band_ref, scratch[::2], scratch[1::2], entry_ref, conv_ref,
                state_ref, arrive)


def border_kernel(sizes, part, widths, slots, near, lens, x_in, band_ref, rows_in, *refs):
    planes, rows, blocks = sizes
    x_ref, entry_ref, conv_ref, state_ref, *scratch = refs[part - 1:]
    start = side_starts(rows)[part - 1][1] + RIM

    def arrive(k):
        x_ref[k, pl.ds(pl.multiple_of(start * blocks, blocks), RIM * blocks), :] = rows_in[k]

    group_stage(sizes, part, (widths, slots, near, lens), x_ref, band_ref, scratch[::2], scratch[1::2], entry_ref,
                conv_ref, state_ref, arrive)


def resume(sizes, part, turn, slots, near, entry_ref, incoming, conv_ref, finish):
    planes, rows, blocks = sizes

    @pl.when(lax.axis_index("depth") == turn)
    def _():
        sweep(planes, group_sizes(rows)[part] * blocks, lambda k: near[slots[k]], entry_ref, conv_ref,
              lambda where, shape: [incoming[i, where, :] for i in range(8)], finish)


def resume_kernel(sizes, part, turn, slots, near, entry_ref, incoming, conv_in, conv_ref, *state_ref):
    finish = writer(state_ref[0]) if state_ref else lambda where, state: None
    resume(sizes, part, turn, slots, near, entry_ref, incoming, conv_ref, finish)


def last_kernel(sizes, turn, slots, near, entry_ref, incoming, conv_in, *refs):
    planes, rows, blocks = sizes
    others, (conv_ref, out_hbm, tiles_ref, sems) = refs[:-4], refs[-4:]
    part = len(others)
    resume(sizes, part, turn, slots, near, entry_ref, incoming, conv_ref, lambda where, state: None)

    def plane_copy(k):
        return pltpu.make_async_copy(tiles_ref.at[k], out_hbm.at[k], sems.at[k])

    def plane(k, carry):
        for part, ref in enumerate((*others, conv_ref)):
            start = first_row(rows, part)
            for i in range(group_sizes(rows)[part]):
                row = start + i
                for half in range(blocks // SUB):
                    to = (row // SUB) * SUB * blocks + half * SUB * SUB + row % SUB
                    tiles_ref[k, pl.ds(to, SUB, stride=SUB), :] = ref[k, pl.ds(i * blocks + half * SUB, SUB), :]
        plane_copy(k).start()
        return carry

    lax.fori_loop(0, planes, plane, 0)
    for k in range(planes):
        plane_copy(k).wait()


def per_device(potential, widths, plane_slot, ratio_near, ratio_lens):
    planes, rows, cols = potential.shape
    blocks = cols // LANES
    sizes = (planes, rows, blocks)
    parts = len(group_sizes(rows))
    together = next(count for count in range(TOGETHER, 0, -1) if planes % count == 0)
    depth_count, sky_count = lax.axis_size("depth"), lax.axis_size("sky")
    swaps = [[pair for i in range(first, sky_count - 1, 2) for pair in ((i, i + 1), (i + 1, i))] for first in (0, 1)]
    ahead = [(i, i + 1) for i in range(depth_count - 1)]
    tiled = potential.reshape(planes, rows // SUB, SUB, blocks, LANES).transpose(0, 1, 3, 2, 4)
    tiled = tiled.reshape(planes, rows * blocks, LANES)
    smem = pl.BlockSpec(memory_space=pltpu.SMEM)
    vmem = pl.BlockSpec(memory_space=pltpu.VMEM)
    anywhere = pl.BlockSpec(memory_space=pl.ANY)
    params = pltpu.CompilerParams(vmem_limit_bytes=VMEM_LIMIT)
    scalars = (widths, plane_slot, ratio_near, ratio_lens)
    dma = pltpu.SemaphoreType.DMA
    cost = pl.CostEstimate(flops=1, transcendentals=0, bytes_accessed=1)

    def held(*shape, dtype=F32):
        return pltpu.VMEM(shape, dtype)

    def moved(*shape):
        return jax.ShapeDtypeStruct(shape, F32)

    def in_vmem(array):
        return pltpu.with_memory_space_constraint(array, pltpu.VMEM)

    def in_hbm(array):
        return pltpu.with_memory_space_constraint(array, pltpu.HBM)

    x_shape = held(planes, (rows + 2 * RIM) * blocks, LANES)
    band_shape = held(planes, 3, LANES, 2 * LANES, dtype=BF16)

    def group_shapes(part):
        length = group_sizes(rows)[part] * blocks
        return [held(planes, 3, length, LANES), held(planes, length, LANES), moved(8, length, LANES)]

    def group_scratch(part):
        count = group_sizes(rows)[part]
        return [held(3, count * blocks, max(PARTS) * LANES, dtype=BF16),
                held(3, (count + 1) * (blocks + SUB), LANES)] * together

    side = moved(planes, RIM * blocks, LANES)
    x, bands, *group, paired, other = pl.pallas_call(
        functools.partial(first_kernel, sizes),
        out_shape=[x_shape, band_shape, *group_shapes(0), side, side],
        in_specs=[anywhere] * 5,
        out_specs=[vmem] * 7,
        scratch_shapes=[
            *group_scratch(0), held(planes, rows * blocks, LANES),
            *[pltpu.SMEM(array.shape, array.dtype) for array in scalars], dma((planes,)), dma((len(scalars),))],
        compiler_params=params,
        cost_estimate=cost,
        name="first",
    )(*[in_hbm(array) for array in (*scalars, tiled)])
    made = [group]
    arriving = [lax.ppermute(group[2], "depth", ahead)]
    swapped = [lax.ppermute(paired, "sky", swaps[0]), lax.ppermute(other, "sky", swaps[1])]
    entries, convs = [group[0] for group in made], [group[1] for group in made]

    def resumed(part, turn):
        last = turn == depth_count - 1
        convs[part], *state = pl.pallas_call(
            functools.partial(resume_kernel, sizes, part, turn),
            out_shape=group_shapes(part)[1:2] + ([] if last else group_shapes(part)[2:3]),
            in_specs=[smem] * 2 + [vmem] * 3,
            out_specs=[vmem] * (1 if last else 2),
            input_output_aliases={4: 0},
            compiler_params=params,
            cost_estimate=cost,
            name="resume",
        )(plane_slot, ratio_near, in_vmem(entries[part]), arriving[part], in_vmem(convs[part]))
        if state:
            arriving[part] = lax.ppermute(state[0], "depth", ahead)

    for part in range(1, parts):
        x, *group = pl.pallas_call(
            functools.partial(border_kernel, sizes, part),
            out_shape=[x_shape, *group_shapes(part)],
            in_specs=[smem] * 4 + [vmem] * 3 + [anywhere] * (part - 1),
            out_specs=[vmem] * 4,
            scratch_shapes=group_scratch(part),
            input_output_aliases={4: 0},
            compiler_params=params,
            cost_estimate=cost,
            name="border",
        )(*scalars, in_vmem(x), in_vmem(bands), swapped[part - 1], *arriving[:part - 1])
        entries.append(group[0])
        convs.append(group[1])
        arriving.append(lax.ppermute(group[2], "depth", ahead))
    for turn in range(1, depth_count):
        for part in range(parts - (turn == depth_count - 1)):
            resumed(part, turn)

    conv, out = pl.pallas_call(
        functools.partial(last_kernel, sizes, depth_count - 1),
        out_shape=[group_shapes(parts - 1)[1], moved(planes, rows * blocks, LANES)],
        in_specs=[smem] * 2 + [vmem] * (3 + parts - 1),
        out_specs=[vmem, anywhere],
        scratch_shapes=[held(planes, rows * blocks, LANES), dma((planes,))],
        input_output_aliases={4: 0},
        compiler_params=params,
        cost_estimate=cost,
        name="last",
    )(plane_slot, ratio_near, in_vmem(entries[-1]), arriving[-1], in_vmem(convs[-1]),
      *[in_vmem(conv) for conv in convs[:-1]])
    out = out.reshape(planes, rows // SUB, blocks, SUB, LANES).transpose(0, 1, 3, 2, 4)
    return out.reshape(planes, rows, cols)


def solution(mesh):
    return jax.shard_map(
        per_device,
        mesh=mesh,
        in_specs=(P("depth", "sky", None), P("depth"), P("depth"), P(), P()),
        out_specs=P("depth", "sky", None),
        check_vma=False,
    )
```

```python
import functools

import jax
import jax.numpy as jnp
from jax import lax
from jax.experimental import pallas as pl
from jax.experimental.pallas import tpu as pltpu
from jax.sharding import PartitionSpec as P

WMAX = 8
RIM = WMAX + 1
LANES = 128
SUB = 8
TOGETHER = 4
PARTS = (3, 2, 2)
SHARES = 2
SENT = 7
TINY, POLE, FAR = 1e-30, 1e-20, 1e10
VMEM_LIMIT = 16 * 1024 * 1024
F32, BF16 = jnp.float32, jnp.bfloat16


def group_sizes(row_count):
    return (row_count - 2 * RIM, RIM, RIM)


def side_starts(row_count):
    low, high = (0, -RIM), (row_count - RIM, row_count)
    even = lax.rem(lax.axis_index("sky"), 2) == 0
    paired = [jnp.where(even, b, a) for a, b in zip(low, high)]
    other = [jnp.where(even, a, b) for a, b in zip(low, high)]
    return paired, other


def first_row(row_count, part):
    return RIM if part == 0 else side_starts(row_count)[part - 1][0]


def split(value, parts):
    found = []
    for part in range(parts):
        found.append(value.astype(BF16))
        if part + 1 < parts:
            value = value - found[-1].astype(F32)
    return found


def make_bands(planes, widths, band_ref):
    source = lax.broadcasted_iota(jnp.int32, (LANES, 2 * LANES), 0)
    target = lax.broadcasted_iota(jnp.int32, (LANES, 2 * LANES), 1)
    across = jnp.where(target >= LANES + LANES // 2, source + 2 * LANES, source)
    offset = across - target
    distance = jnp.abs(offset)

    def plane(k, carry):
        half_width = widths[k]
        rim = (distance == half_width + 1).astype(F32)
        edge = (distance == half_width).astype(F32)
        inside = (distance <= half_width).astype(F32)
        both = rim + edge
        for field, value in enumerate((rim - edge, jnp.where(offset > 0, both, -both), inside)):
            band_ref[k, field] = value.astype(BF16)
        return carry

    lax.fori_loop(0, planes, plane, 0)


def build(k, half_width, first, count, blocks, x_ref, left_ref):
    def row(index):
        return x_ref[k, pl.ds(pl.multiple_of(index * blocks, blocks), blocks), :]

    total = row(first)
    for step in range(1, WMAX + 1):
        total = total + jnp.where(step <= half_width, row(first - step) + row(first + step), 0.0)
    for i in range(count):
        high, low = first + i + half_width, first + i - half_width
        rim_high, edge_high, edge_low, rim_low = row(high + 1), row(high), row(low), row(low - 1)
        values = (total, (rim_high + edge_high) - (edge_low + rim_low),
                  (rim_high - edge_high) - (edge_low - rim_low))
        total = total + (rim_high - edge_low)
        here = slice(i * blocks, (i + 1) * blocks)
        for field, value in enumerate(values):
            for part, piece in enumerate(split(value, PARTS[field])):
                left_ref[field, here, part * LANES:(part + 1) * LANES] = piece


def multiply(k, field, band_ref, left_ref):
    weight = jnp.concatenate([band_ref[k, field]] * PARTS[field], axis=0)
    return jnp.dot(left_ref[field, :, :PARTS[field] * LANES], weight, preferred_element_type=F32)


def combine(k, field, near, scale, blocks, product, beside_ref, entry_ref):
    pitch = blocks + SUB
    count = product.shape[0] // blocks
    left_lane = lax.broadcasted_iota(jnp.int32, (blocks, LANES), 1) < LANES // 2
    factor = -0.25 * scale if field == 1 else -scale
    for at in range(count):
        beside_ref[field, pl.ds(at * pitch + SUB, blocks), :] = product[at * blocks:(at + 1) * blocks, LANES:]
    for at in range(count):
        beside = jnp.where(left_lane, beside_ref[field, pl.ds(at * pitch + SUB - 1, blocks), :],
                           beside_ref[field, pl.ds(at * pitch + SUB + 1, blocks), :])
        value = factor * (product[at * blocks:(at + 1) * blocks, :LANES] + beside)
        entry_ref[k, field, pl.ds(at * blocks, blocks), :] = value if field == 1 else value + near


def sweep(planes, length, near_of, entry_ref, conv_ref, start, finish):
    step = next(count * SUB for count in (4, 3, 2, 1) if length % (count * SUB) == 0)

    def part(index, carry):
        where = pl.ds(pl.multiple_of(index * step, step), step)
        state = start(where, (step, LANES))
        now, then = state[:4], state[4:]
        for k in range(planes):
            xx, xy, yy = [entry_ref[k, i, where, :] for i in range(3)]
            kept = 1.0 - near_of(k)
            new = [
                xx * now[0] + xy * now[2] + kept * then[0],
                xx * now[1] + xy * now[3] + kept * then[1],
                xy * now[0] + yy * now[2] + kept * then[2],
                xy * now[1] + yy * now[3] + kept * then[3],
            ]
            now, then = new, now
            conv_ref[k, where, :] = 1.0 - 0.5 * (new[0] + new[3])
        finish(where, now + then)
        return carry

    lax.fori_loop(0, length // step, part, 0)


def packed_state(state):
    a00, a01, a10, a11, b00, b01, b10, b11 = state
    p = [a00 + b01, a10 + b11, a01 - b00, a11 - b10]
    q = [a00 - b01, a10 - b11, a01 + b00, a11 + b10]
    most = jnp.maximum(jnp.maximum(jnp.abs(q[0]), jnp.abs(q[1])), jnp.maximum(jnp.abs(q[2]), jnp.abs(q[3])))
    scale = 1.0 / jnp.maximum(most, TINY)
    q = [value * scale for value in q]
    side = q[0] * q[0] + q[1] * q[1] + q[2] * q[2]
    reach = jnp.sqrt(side + q[3] * q[3]) + jnp.abs(q[3])
    ahead = q[3] >= 0.0
    factor = jnp.where(ahead, 1.0, reach) / jnp.where(ahead, jnp.maximum(reach, TINY), jnp.maximum(side, POLE))
    at_pole = jnp.logical_and(jnp.logical_not(ahead), side < POLE)
    u = [value * factor for value in q[:3]]
    return p + [jnp.where(at_pole, FAR, u[0]), u[1], u[2]]


def unpacked_state(values):
    p, u = values[:4], values[4:]
    most = jnp.maximum(jnp.maximum(jnp.abs(p[0]), jnp.abs(p[1])), jnp.maximum(jnp.abs(p[2]), jnp.abs(p[3])))
    bound = jnp.maximum(most, TINY)
    scale = 1.0 / bound
    unit = [value * scale for value in p]
    norm = bound * jnp.sqrt((unit[0] * unit[0] + unit[1] * unit[1]) + (unit[2] * unit[2] + unit[3] * unit[3]))
    square = u[0] * u[0] + u[1] * u[1] + u[2] * u[2]
    share = 1.0 / (1.0 + square)
    q = [norm * (2.0 * share * value) for value in u] + [norm * ((1.0 - square) * share)]
    half = lambda a, b: 0.5 * (a + b)
    return [half(p[0], q[0]), half(p[2], q[2]), half(p[1], q[1]), half(p[3], q[3]),
            half(q[2], -p[2]), half(p[0], -q[0]), half(q[3], -p[3]), half(p[1], -q[1])]


def identity_state(where, shape):
    one, zero = jnp.ones(shape, F32), jnp.zeros(shape, F32)
    return [one, zero, zero, one] * 2


def writer(state_ref):
    def finish(where, state):
        for i, value in enumerate(packed_state(state)):
            state_ref[i, where, :] = value

    return finish


def group_stage(sizes, part, scalars, x_ref, band_ref, left_refs, beside_refs, entry_ref, conv_ref, state_ref,
                before_plane=lambda k: None):
    planes, rows, blocks = sizes
    widths, slots, near, lens = scalars
    first, count = first_row(rows, part) + RIM, group_sizes(rows)[part]
    together = len(left_refs)
    for beside_ref in beside_refs:
        beside_ref[...] = jnp.zeros(beside_ref.shape, F32)

    def step(index, carry):
        ks = [index * together + i for i in range(together)]
        for k in ks:
            before_plane(k)
        for k, left_ref in zip(ks, left_refs):
            build(k, widths[k], first, count, blocks, x_ref, left_ref)
        for field in range(3):
            for k, left_ref, beside_ref in zip(ks, left_refs, beside_refs):
                width = (2 * widths[k] + 1).astype(F32)
                combine(k, field, near[slots[k]], lens[slots[k]] / (width * width), blocks,
                        multiply(k, field, band_ref, left_ref), beside_ref, entry_ref)
        return carry

    lax.fori_loop(0, planes // together, step, 0)

    @pl.when(lax.axis_index("depth") == 0)
    def _():
        sweep(planes, group_sizes(rows)[part] * blocks, lambda k: near[slots[k]], entry_ref, conv_ref, identity_state,
              writer(state_ref))


def first_kernel(sizes, widths_hbm, slots_hbm, near_hbm, lens_hbm, potential_hbm, x_ref, band_ref, entry_ref, conv_ref,
                 state_ref, *refs):
    planes, rows, blocks = sizes
    sends, scratch = refs[:2 * SHARES], refs[2 * SHARES:]
    scratch, (tiles_ref, widths, slots, near, lens, plane_sems, table_sems) = scratch[:-7], scratch[-7:]
    share = planes // SHARES
    tables = ((widths_hbm, widths), (slots_hbm, slots), (near_hbm, near), (lens_hbm, lens))
    copies = [pltpu.make_async_copy(*pair, table_sems.at[i]) for i, pair in enumerate(tables)]
    for copy in copies:
        copy.start()

    def plane_copy(k):
        return pltpu.make_async_copy(potential_hbm.at[k], tiles_ref.at[k], plane_sems.at[k])

    for k in range(planes):
        plane_copy(k).start()
    for copy in copies:
        copy.wait()
    make_bands(planes, widths, band_ref)
    sides = [(start + RIM) * blocks for start, _ in side_starts(rows)]

    def arrive(k):
        plane_copy(k).wait()
        for row in range(rows):
            for half in range(blocks // SUB):
                start = (row // SUB) * SUB * blocks + half * SUB * SUB + row % SUB
                x_ref[k, pl.ds((row + RIM) * blocks + half * SUB, SUB), :] = tiles_ref[
                    k, pl.ds(start, SUB, stride=SUB), :]
        for i, side in enumerate(sides):
            rows_out = x_ref[k, pl.ds(pl.multiple_of(side, blocks), RIM * blocks), :]
            for piece in range(SHARES):

                @pl.when(lax.div(k, share) == piece)
                def _(ref=sends[i * SHARES + piece]):
                    ref[lax.rem(k, share)] = rows_out

    group_stage(sizes, 0, (widths, slots, near, lens), x_ref, band_ref, scratch[::2], scratch[1::2], entry_ref, conv_ref,
                state_ref, arrive)


def border_kernel(sizes, part, widths, slots, near, lens, x_in, band_ref, *refs):
    planes, rows, blocks = sizes
    arrived, refs = refs[:SHARES], refs[SHARES:]
    share = planes // SHARES
    x_ref, entry_ref, conv_ref, state_ref, *scratch = refs[part - 1:]
    start = side_starts(rows)[part - 1][1] + RIM

    def arrive(k):
        for piece, ref in enumerate(arrived):

            @pl.when(lax.div(k, share) == piece)
            def _(ref=ref):
                x_ref[k, pl.ds(pl.multiple_of(start * blocks, blocks), RIM * blocks), :] = ref[lax.rem(k, share)]

    group_stage(sizes, part, (widths, slots, near, lens), x_ref, band_ref, scratch[::2], scratch[1::2], entry_ref,
                conv_ref, state_ref, arrive)


def resume(sizes, part, turn, slots, near, entry_ref, incoming, conv_ref, finish):
    planes, rows, blocks = sizes

    @pl.when(lax.axis_index("depth") == turn)
    def _():
        sweep(planes, group_sizes(rows)[part] * blocks, lambda k: near[slots[k]], entry_ref, conv_ref,
              lambda where, shape: unpacked_state([incoming[i, where, :] for i in range(SENT)]), finish)


def resume_kernel(sizes, part, turn, slots, near, entry_ref, incoming, conv_in, conv_ref, *state_ref):
    finish = writer(state_ref[0]) if state_ref else lambda where, state: None
    resume(sizes, part, turn, slots, near, entry_ref, incoming, conv_ref, finish)


def last_kernel(sizes, turn, slots, near, entry_ref, incoming, conv_in, *refs):
    planes, rows, blocks = sizes
    others, (conv_ref, out_hbm, tiles_ref, sems) = refs[:-4], refs[-4:]
    part = len(others)
    resume(sizes, part, turn, slots, near, entry_ref, incoming, conv_ref, lambda where, state: None)

    def plane_copy(k):
        return pltpu.make_async_copy(tiles_ref.at[k], out_hbm.at[k], sems.at[k])

    def plane(k, carry):
        for part, ref in enumerate((*others, conv_ref)):
            start = first_row(rows, part)
            for i in range(group_sizes(rows)[part]):
                row = start + i
                for half in range(blocks // SUB):
                    to = (row // SUB) * SUB * blocks + half * SUB * SUB + row % SUB
                    tiles_ref[k, pl.ds(to, SUB, stride=SUB), :] = ref[k, pl.ds(i * blocks + half * SUB, SUB), :]
        plane_copy(k).start()
        return carry

    lax.fori_loop(0, planes, plane, 0)
    for k in range(planes):
        plane_copy(k).wait()


def per_device(potential, widths, plane_slot, ratio_near, ratio_lens):
    planes, rows, cols = potential.shape
    blocks = cols // LANES
    sizes = (planes, rows, blocks)
    parts = len(group_sizes(rows))
    together = next(count for count in range(TOGETHER, 0, -1) if planes % count == 0)
    depth_count, sky_count = lax.axis_size("depth"), lax.axis_size("sky")
    swaps = [[pair for i in range(first, sky_count - 1, 2) for pair in ((i, i + 1), (i + 1, i))] for first in (0, 1)]
    ahead = [(i, i + 1) for i in range(depth_count - 1)]
    tiled = potential.reshape(planes, rows // SUB, SUB, blocks, LANES).transpose(0, 1, 3, 2, 4)
    tiled = tiled.reshape(planes, rows * blocks, LANES)
    smem = pl.BlockSpec(memory_space=pltpu.SMEM)
    vmem = pl.BlockSpec(memory_space=pltpu.VMEM)
    anywhere = pl.BlockSpec(memory_space=pl.ANY)
    params = pltpu.CompilerParams(vmem_limit_bytes=VMEM_LIMIT)
    scalars = (widths, plane_slot, ratio_near, ratio_lens)
    dma = pltpu.SemaphoreType.DMA
    cost = pl.CostEstimate(flops=1, transcendentals=0, bytes_accessed=1)

    def held(*shape, dtype=F32):
        return pltpu.VMEM(shape, dtype)

    def moved(*shape):
        return jax.ShapeDtypeStruct(shape, F32)

    def in_vmem(array):
        return pltpu.with_memory_space_constraint(array, pltpu.VMEM)

    def in_hbm(array):
        return pltpu.with_memory_space_constraint(array, pltpu.HBM)

    x_shape = held(planes, (rows + 2 * RIM) * blocks, LANES)
    band_shape = held(planes, 3, LANES, 2 * LANES, dtype=BF16)

    def group_shapes(part):
        length = group_sizes(rows)[part] * blocks
        return [held(planes, 3, length, LANES), held(planes, length, LANES), moved(SENT, length, LANES)]

    def group_scratch(part):
        count = group_sizes(rows)[part]
        return [held(3, count * blocks, max(PARTS) * LANES, dtype=BF16),
                held(3, (count + 1) * (blocks + SUB), LANES)] * together

    side = moved(planes // SHARES, RIM * blocks, LANES)
    x, bands, *rest = pl.pallas_call(
        functools.partial(first_kernel, sizes),
        out_shape=[x_shape, band_shape, *group_shapes(0), *[side] * (2 * SHARES)],
        in_specs=[anywhere] * 5,
        out_specs=[vmem] * (5 + 2 * SHARES),
        scratch_shapes=[
            *group_scratch(0), held(planes, rows * blocks, LANES),
            *[pltpu.SMEM(array.shape, array.dtype) for array in scalars], dma((planes,)), dma((len(scalars),))],
        compiler_params=params,
        cost_estimate=cost,
        name="first",
    )(*[in_hbm(array) for array in (*scalars, tiled)])
    group, sends = rest[:3], rest[3:]
    made = [group]
    arriving = [lax.ppermute(group[2], "depth", ahead)]
    swapped = [[lax.ppermute(piece, "sky", swap) for piece in sends[i * SHARES:(i + 1) * SHARES]]
               for i, swap in enumerate(swaps)]
    entries, convs = [group[0] for group in made], [group[1] for group in made]

    def resumed(part, turn):
        last = turn == depth_count - 1
        convs[part], *state = pl.pallas_call(
            functools.partial(resume_kernel, sizes, part, turn),
            out_shape=group_shapes(part)[1:2] + ([] if last else group_shapes(part)[2:3]),
            in_specs=[smem] * 2 + [vmem] * 3,
            out_specs=[vmem] * (1 if last else 2),
            input_output_aliases={4: 0},
            compiler_params=params,
            cost_estimate=cost,
            name="resume",
        )(plane_slot, ratio_near, in_vmem(entries[part]), arriving[part], in_vmem(convs[part]))
        if state:
            arriving[part] = lax.ppermute(state[0], "depth", ahead)

    for part in range(1, parts):
        x, *group = pl.pallas_call(
            functools.partial(border_kernel, sizes, part),
            out_shape=[x_shape, *group_shapes(part)],
            in_specs=[smem] * 4 + [vmem] * (2 + SHARES) + [anywhere] * (part - 1),
            out_specs=[vmem] * 4,
            scratch_shapes=group_scratch(part),
            input_output_aliases={4: 0},
            compiler_params=params,
            cost_estimate=cost,
            name="border",
        )(*scalars, in_vmem(x), in_vmem(bands), *swapped[part - 1], *arriving[:part - 1])
        entries.append(group[0])
        convs.append(group[1])
        arriving.append(lax.ppermute(group[2], "depth", ahead))
    for turn in range(1, depth_count):
        for part in range(parts - (turn == depth_count - 1)):
            resumed(part, turn)

    conv, out = pl.pallas_call(
        functools.partial(last_kernel, sizes, depth_count - 1),
        out_shape=[group_shapes(parts - 1)[1], moved(planes, rows * blocks, LANES)],
        in_specs=[smem] * 2 + [vmem] * (3 + parts - 1),
        out_specs=[vmem, anywhere],
        scratch_shapes=[held(planes, rows * blocks, LANES), dma((planes,))],
        input_output_aliases={4: 0},
        compiler_params=params,
        cost_estimate=cost,
        name="last",
    )(plane_slot, ratio_near, in_vmem(entries[-1]), arriving[-1], in_vmem(convs[-1]),
      *[in_vmem(conv) for conv in convs[:-1]])
    out = out.reshape(planes, rows // SUB, blocks, SUB, LANES).transpose(0, 1, 3, 2, 4)
    return out.reshape(planes, rows, cols)


def solution(mesh):
    return jax.shard_map(
        per_device,
        mesh=mesh,
        in_specs=(P("depth", "sky", None), P("depth"), P("depth"), P(), P()),
        out_specs=P("depth", "sky", None),
        check_vma=False,
    )
```

```python
import functools

import jax
import jax.numpy as jnp
from jax import lax
from jax.experimental import pallas as pl
from jax.experimental.pallas import tpu as pltpu
from jax.sharding import PartitionSpec as P

WMAX = 8
RIM = WMAX + 1
LANES = 128
SUB = 8
TOGETHER = 4
PARTS = (3, 2, 2)
BORDER_SHARES = (((0, 1),), ((0,), (1,)))
SHARES = 2
SENT = 7
TINY, POLE, FAR = 1e-30, 1e-20, 1e10
VMEM_LIMIT = 16 * 1024 * 1024
F32, BF16 = jnp.float32, jnp.bfloat16


def group_sizes(row_count):
    return (row_count - 2 * RIM, RIM, RIM)


def side_starts(row_count):
    low, high = (0, -RIM), (row_count - RIM, row_count)
    even = lax.rem(lax.axis_index("sky"), 2) == 0
    paired = [jnp.where(even, b, a) for a, b in zip(low, high)]
    other = [jnp.where(even, a, b) for a, b in zip(low, high)]
    return paired, other


def first_row(row_count, part):
    return RIM if part == 0 else side_starts(row_count)[part - 1][0]


def split(value, parts):
    found = []
    for part in range(parts):
        found.append(value.astype(BF16))
        if part + 1 < parts:
            value = value - found[-1].astype(F32)
    return found


def make_bands(band_ref):
    source = lax.broadcasted_iota(jnp.int32, (LANES, 2 * LANES), 0)
    target = lax.broadcasted_iota(jnp.int32, (LANES, 2 * LANES), 1)
    across = jnp.where(target >= LANES + LANES // 2, source + 2 * LANES, source)
    offset = across - target
    distance = jnp.abs(offset)

    def width(index, carry):
        half_width = index + 1
        rim = (distance == half_width + 1).astype(F32)
        edge = (distance == half_width).astype(F32)
        inside = (distance <= half_width).astype(F32)
        both = rim + edge
        for field, value in enumerate((rim - edge, jnp.where(offset > 0, both, -both), inside)):
            band_ref[index, field] = value.astype(BF16)
        return carry

    lax.fori_loop(0, WMAX, width, 0)


def build(k, half_width, first, count, blocks, x_ref, left_ref):
    def row(index):
        return x_ref[k, pl.ds(pl.multiple_of(index * blocks, blocks), blocks), :]

    total = row(first)
    for step in range(1, WMAX + 1):
        total = total + jnp.where(step <= half_width, row(first - step) + row(first + step), 0.0)
    for i in range(count):
        high, low = first + i + half_width, first + i - half_width
        rim_high, edge_high, edge_low, rim_low = row(high + 1), row(high), row(low), row(low - 1)
        values = (total, (rim_high + edge_high) - (edge_low + rim_low),
                  (rim_high - edge_high) - (edge_low - rim_low))
        total = total + (rim_high - edge_low)
        here = slice(i * blocks, (i + 1) * blocks)
        for field, value in enumerate(values):
            for part, piece in enumerate(split(value, PARTS[field])):
                left_ref[field, here, part * LANES:(part + 1) * LANES] = piece


def multiply(half_width, field, band_ref, left_ref):
    weight = jnp.concatenate([band_ref[half_width - 1, field]] * PARTS[field], axis=0)
    return jnp.dot(left_ref[field, :, :PARTS[field] * LANES], weight, preferred_element_type=F32)


def combine(k, field, near, scale, blocks, product, beside_ref, entry_ref):
    pitch = blocks + SUB
    count = product.shape[0] // blocks
    left_lane = lax.broadcasted_iota(jnp.int32, (blocks, LANES), 1) < LANES // 2
    factor = -0.25 * scale if field == 1 else -scale
    for at in range(count):
        beside_ref[field, pl.ds(at * pitch + SUB, blocks), :] = product[at * blocks:(at + 1) * blocks, LANES:]
    for at in range(count):
        beside = jnp.where(left_lane, beside_ref[field, pl.ds(at * pitch + SUB - 1, blocks), :],
                           beside_ref[field, pl.ds(at * pitch + SUB + 1, blocks), :])
        value = factor * (product[at * blocks:(at + 1) * blocks, :LANES] + beside)
        entry_ref[k, field, pl.ds(at * blocks, blocks), :] = value if field == 1 else value + near


def sweep(planes, length, near_of, entry_ref, conv_ref, start, finish):
    step = next(count * SUB for count in (4, 3, 2, 1) if length % (count * SUB) == 0)

    def part(index, carry):
        where = pl.ds(pl.multiple_of(index * step, step), step)
        now, then = (None, None) if start is None else start(where)
        for k in range(planes):
            xx, xy, yy = [entry_ref[k, i, where, :] for i in range(3)]
            kept = 1.0 - near_of(k)
            if now is None:
                one, zero = jnp.ones((step, LANES), F32), jnp.zeros((step, LANES), F32)
                now, new = [one, zero, zero, one], [xx + kept, xy, xy, yy + kept]
            else:
                new = [
                    xx * now[0] + xy * now[2],
                    xx * now[1] + xy * now[3],
                    xy * now[0] + yy * now[2],
                    xy * now[1] + yy * now[3],
                ]
                if then is None:
                    new = [new[0] + kept, new[1], new[2], new[3] + kept]
                else:
                    new = [value + kept * old for value, old in zip(new, then)]
            then = now if k or start is not None else None
            now = new
            conv_ref[k, where, :] = 1.0 - 0.5 * (new[0] + new[3])
        if finish is not None:
            finish(where, now + then)
        return carry

    lax.fori_loop(0, length // step, part, 0)


def packed_state(state):
    a00, a01, a10, a11, b00, b01, b10, b11 = state
    p = [a00 + b01, a10 + b11, a01 - b00, a11 - b10]
    q = [a00 - b01, a10 - b11, a01 + b00, a11 + b10]
    most = jnp.maximum(jnp.maximum(jnp.abs(q[0]), jnp.abs(q[1])), jnp.maximum(jnp.abs(q[2]), jnp.abs(q[3])))
    scale = 1.0 / jnp.maximum(most, TINY)
    q = [value * scale for value in q]
    side = q[0] * q[0] + q[1] * q[1] + q[2] * q[2]
    reach = jnp.sqrt(side + q[3] * q[3]) + jnp.abs(q[3])
    ahead = q[3] >= 0.0
    factor = jnp.where(ahead, 1.0, reach) / jnp.where(ahead, jnp.maximum(reach, TINY), jnp.maximum(side, POLE))
    at_pole = jnp.logical_and(jnp.logical_not(ahead), side < POLE)
    u = [value * factor for value in q[:3]]
    return p + [jnp.where(at_pole, FAR, u[0]), u[1], u[2]]


def unpacked_state(values):
    p, u = values[:4], values[4:]
    most = jnp.maximum(jnp.maximum(jnp.abs(p[0]), jnp.abs(p[1])), jnp.maximum(jnp.abs(p[2]), jnp.abs(p[3])))
    bound = jnp.maximum(most, TINY)
    scale = 1.0 / bound
    unit = [value * scale for value in p]
    norm = bound * jnp.sqrt((unit[0] * unit[0] + unit[1] * unit[1]) + (unit[2] * unit[2] + unit[3] * unit[3]))
    square = u[0] * u[0] + u[1] * u[1] + u[2] * u[2]
    share = 1.0 / (1.0 + square)
    q = [norm * (2.0 * share * value) for value in u] + [norm * ((1.0 - square) * share)]
    half = lambda a, b: 0.5 * (a + b)
    now = [half(p[0], q[0]), half(p[2], q[2]), half(p[1], q[1]), half(p[3], q[3])]
    then = [half(q[2], -p[2]), half(p[0], -q[0]), half(q[3], -p[3]), half(p[1], -q[1])]
    return now, then


def writer(state_ref):
    def finish(where, state):
        for i, value in enumerate(packed_state(state)):
            state_ref[i, where, :] = value

    return finish


def steps_of(planes, shares):
    count = planes // SHARES
    per = next(n for n in range(max(1, TOGETHER // len(shares)), 0, -1) if count % n == 0)
    return count // per, per


def group_stage(sizes, part, scalars, x_ref, band_ref, scratch, entry_ref, conv_ref, state_ref, before_plane,
                shares=tuple(range(SHARES))):
    planes, rows, blocks = sizes
    widths, slots, near, lens = scalars
    left_refs, beside_refs = scratch[::2], scratch[1::2]
    first, count = first_row(rows, part) + RIM, group_sizes(rows)[part]
    steps, per = steps_of(planes, shares)
    for beside_ref in beside_refs:
        beside_ref[...] = jnp.zeros(beside_ref.shape, F32)

    def step(index, carry):
        ks = []
        for i in range(per):
            for share in shares:
                place = index * per + i
                ks.append(place * SHARES + share)
                before_plane(share, place, ks[-1])
        for k, left_ref in zip(ks, left_refs):
            build(k, widths[k], first, count, blocks, x_ref, left_ref)
        for field in range(3):
            for k, left_ref, beside_ref in zip(ks, left_refs, beside_refs):
                width = (2 * widths[k] + 1).astype(F32)
                combine(k, field, near[slots[k]], lens[slots[k]] / (width * width), blocks,
                        multiply(widths[k], field, band_ref, left_ref), beside_ref, entry_ref)
        return carry

    lax.fori_loop(0, steps, step, 0)
    if shares[-1] == SHARES - 1:

        @pl.when(lax.axis_index("depth") == 0)
        def _():
            sweep(planes, group_sizes(rows)[part] * blocks, lambda k: near[slots[k]], entry_ref, conv_ref, None,
                  writer(state_ref))


def first_kernel(sizes, widths_hbm, slots_hbm, near_hbm, lens_hbm, potential_hbm, x_ref, band_ref, entry_ref, conv_ref,
                 state_ref, *refs):
    planes, rows, blocks = sizes
    sends, scratch = refs[:2 * SHARES], refs[2 * SHARES:]
    scratch, (tiles_ref, widths, slots, near, lens, plane_sems, table_sems) = scratch[:-7], scratch[-7:]
    tables = ((widths_hbm, widths), (slots_hbm, slots), (near_hbm, near), (lens_hbm, lens))
    copies = [pltpu.make_async_copy(*pair, table_sems.at[i]) for i, pair in enumerate(tables)]
    for copy in copies:
        copy.start()

    def plane_copy(k):
        return pltpu.make_async_copy(potential_hbm.at[k], tiles_ref.at[k], plane_sems.at[k])

    for k in range(planes):
        plane_copy(k).start()
    make_bands(band_ref)
    for copy in copies:
        copy.wait()
    sides = [(start + RIM) * blocks for start, _ in side_starts(rows)]

    def arrive(share, place, k):
        plane_copy(k).wait()
        for row in range(rows):
            for half in range(blocks // SUB):
                start = (row // SUB) * SUB * blocks + half * SUB * SUB + row % SUB
                x_ref[k, pl.ds((row + RIM) * blocks + half * SUB, SUB), :] = tiles_ref[
                    k, pl.ds(start, SUB, stride=SUB), :]
        for i, side in enumerate(sides):
            sends[i * SHARES + share][place] = x_ref[k, pl.ds(pl.multiple_of(side, blocks), RIM * blocks), :]

    group_stage(sizes, 0, (widths, slots, near, lens), x_ref, band_ref, scratch, entry_ref, conv_ref, state_ref, arrive)


def border_kernel(sizes, part, shares, widths, slots, near, lens, band_ref, x_in, entry_in, *refs):
    planes, rows, blocks = sizes
    arrived, refs = refs[:len(shares)], refs[len(shares):]
    last = shares[-1] == SHARES - 1
    outputs = 4 if last else 2
    scratch_count = 2 * len(shares) * steps_of(planes, shares)[1]
    refs, scratch = refs[-outputs - scratch_count:-scratch_count], refs[-scratch_count:]
    x_ref, entry_ref, conv_ref, state_ref = (*refs, None, None)[:4]
    start = side_starts(rows)[part - 1][1] + RIM

    def arrive(share, place, k):
        x_ref[k, pl.ds(pl.multiple_of(start * blocks, blocks), RIM * blocks), :] = arrived[shares.index(share)][place]

    group_stage(sizes, part, (widths, slots, near, lens), x_ref, band_ref, scratch, entry_ref, conv_ref, state_ref, arrive,
                shares)


def resume(sizes, part, turn, slots, near, entry_ref, incoming, conv_ref, finish):
    planes, rows, blocks = sizes

    @pl.when(lax.axis_index("depth") == turn)
    def _():
        sweep(planes, group_sizes(rows)[part] * blocks, lambda k: near[slots[k]], entry_ref, conv_ref,
              lambda where: unpacked_state([incoming[i, where, :] for i in range(SENT)]), finish)


def resume_kernel(sizes, part, turn, slots, near, entry_ref, incoming, conv_in, conv_ref, *state_ref):
    resume(sizes, part, turn, slots, near, entry_ref, incoming, conv_ref, writer(state_ref[0]) if state_ref else None)


def place_rows(sizes, part, k, conv_ref, tiles_ref):
    planes, rows, blocks = sizes
    start = first_row(rows, part)
    for i in range(group_sizes(rows)[part]):
        row = start + i
        for half in range(blocks // SUB):
            to = lax.div(row, SUB) * SUB * blocks + half * SUB * SUB + lax.rem(row, SUB)
            tiles_ref[k, pl.ds(to, SUB, stride=SUB), :] = conv_ref[k, pl.ds(i * blocks + half * SUB, SUB), :]


def write_out(sizes, late, tiles_ref, out_hbm, sems, before_plane):
    planes, rows, blocks = sizes
    even = lax.rem(lax.axis_index("sky"), 2) == 0
    tail = -(-RIM // SUB) * SUB
    if late:
        start, count = jnp.where(even, 0, rows - tail), tail
    else:
        start, count = jnp.where(even, tail, 0), rows - tail

    def plane_copy(k):
        where = pl.ds(pl.multiple_of(start * blocks, SUB * blocks), count * blocks)
        return pltpu.make_async_copy(tiles_ref.at[k, where], out_hbm.at[k, where], sems.at[k])

    def plane(k, carry):
        before_plane(k)
        plane_copy(k).start()
        return carry

    lax.fori_loop(0, planes, plane, 0)
    for k in range(planes):
        plane_copy(k).wait()


def early_kernel(sizes, *refs):
    *conv_refs, tiles_ref, out_hbm, sems = refs

    def place(k):
        for part, conv_ref in enumerate(conv_refs):
            place_rows(sizes, part, k, conv_ref, tiles_ref)

    write_out(sizes, False, tiles_ref, out_hbm, sems, place)


def last_kernel(sizes, part, turn, slots, near, entry_ref, incoming, conv_in, tiles_in, out_in, conv_ref, tiles_ref,
                out_hbm, sems):
    resume(sizes, part, turn, slots, near, entry_ref, incoming, conv_ref, None)
    write_out(sizes, True, tiles_ref, out_hbm, sems, lambda k: place_rows(sizes, part, k, conv_ref, tiles_ref))


def per_device(potential, widths, plane_slot, ratio_near, ratio_lens):
    planes, rows, cols = potential.shape
    blocks = cols // LANES
    sizes = (planes, rows, blocks)
    parts = len(group_sizes(rows))
    depth_count, sky_count = lax.axis_size("depth"), lax.axis_size("sky")
    swaps = [[pair for i in range(first, sky_count - 1, 2) for pair in ((i, i + 1), (i + 1, i))] for first in (0, 1)]
    ahead = [(i, i + 1) for i in range(depth_count - 1)]
    tiled = potential.reshape(planes, rows // SUB, SUB, blocks, LANES).transpose(0, 1, 3, 2, 4)
    tiled = tiled.reshape(planes, rows * blocks, LANES)
    smem = pl.BlockSpec(memory_space=pltpu.SMEM)
    vmem = pl.BlockSpec(memory_space=pltpu.VMEM)
    anywhere = pl.BlockSpec(memory_space=pl.ANY)
    params = pltpu.CompilerParams(vmem_limit_bytes=VMEM_LIMIT)
    scalars = (widths, plane_slot, ratio_near, ratio_lens)
    dma = pltpu.SemaphoreType.DMA
    cost = pl.CostEstimate(flops=1, transcendentals=0, bytes_accessed=1)

    def held(*shape, dtype=F32):
        return pltpu.VMEM(shape, dtype)

    def moved(*shape):
        return jax.ShapeDtypeStruct(shape, F32)

    def in_vmem(array):
        return pltpu.with_memory_space_constraint(array, pltpu.VMEM)

    def in_hbm(array):
        return pltpu.with_memory_space_constraint(array, pltpu.HBM)

    x_shape = held(planes, (rows + 2 * RIM) * blocks, LANES)
    band_shape = held(WMAX, 3, LANES, 2 * LANES, dtype=BF16)

    def group_shapes(part):
        length = group_sizes(rows)[part] * blocks
        return [held(planes, 3, length, LANES), held(planes, length, LANES), moved(SENT, length, LANES)]

    def group_scratch(part, shares):
        count = group_sizes(rows)[part]
        return [held(3, count * blocks, max(PARTS) * LANES, dtype=BF16),
                held(3, (count + 1) * (blocks + SUB), LANES)] * (len(shares) * steps_of(planes, shares)[1])

    side = moved(planes // SHARES, RIM * blocks, LANES)
    x, bands, *rest = pl.pallas_call(
        functools.partial(first_kernel, sizes),
        out_shape=[x_shape, band_shape, *group_shapes(0), *[side] * (2 * SHARES)],
        in_specs=[anywhere] * 5,
        out_specs=[vmem] * (5 + 2 * SHARES),
        scratch_shapes=[
            *group_scratch(0, range(SHARES)), held(planes, rows * blocks, LANES),
            *[pltpu.SMEM(array.shape, array.dtype) for array in scalars], dma((planes,)), dma((len(scalars),))],
        compiler_params=params,
        cost_estimate=cost,
        name="first",
    )(*[in_hbm(array) for array in (*scalars, tiled)])
    group, sends = rest[:3], rest[3:]
    made = [group]
    arriving = [lax.ppermute(group[2], "depth", ahead)]
    swapped = [[lax.ppermute(piece, "sky", swap) for piece in sends[i * SHARES:(i + 1) * SHARES]]
               for i, swap in enumerate(swaps)]
    entries, convs = [group[0] for group in made], [group[1] for group in made]
    out_shape = moved(planes, rows * blocks, LANES)

    def resumed(part, turn):
        last = turn == depth_count - 1
        convs[part], *state = pl.pallas_call(
            functools.partial(resume_kernel, sizes, part, turn),
            out_shape=group_shapes(part)[1:2] + ([] if last else group_shapes(part)[2:3]),
            in_specs=[smem] * 2 + [vmem] * 3,
            out_specs=[vmem] * (1 if last else 2),
            input_output_aliases={4: 0},
            compiler_params=params,
            cost_estimate=cost,
            name="resume",
        )(plane_slot, ratio_near, in_vmem(entries[part]), arriving[part], in_vmem(convs[part]))
        if state:
            arriving[part] = lax.ppermute(state[0], "depth", ahead)

    for part in range(1, parts):
        entry = None
        for shares in BORDER_SHARES[part - 1]:
            last = shares[-1] == SHARES - 1
            behind = arriving[:1] if last and part > 1 else []
            x, entry, *group = pl.pallas_call(
                functools.partial(border_kernel, sizes, part, shares),
                out_shape=[x_shape, *group_shapes(part)[:3 if last else 1]],
                in_specs=[smem] * 4 + [vmem] * 2 + [anywhere if entry is None else vmem] + [vmem] * len(shares)
                + [anywhere] * len(behind),
                out_specs=[vmem] * (4 if last else 2),
                scratch_shapes=group_scratch(part, shares),
                input_output_aliases={5: 0} if entry is None else {5: 0, 6: 1},
                compiler_params=params,
                cost_estimate=cost,
                name="border",
            )(*scalars, in_vmem(bands), in_vmem(x), plane_slot if entry is None else in_vmem(entry),
              *[swapped[part - 1][share] for share in shares], *behind)
        entries.append(entry)
        convs.append(group[0])
        arriving.append(lax.ppermute(group[1], "depth", ahead))
    for turn in range(1, depth_count):
        for part in range(parts - (turn == depth_count - 1)):
            resumed(part, turn)
    tiles, out = pl.pallas_call(
        functools.partial(early_kernel, sizes),
        out_shape=[held(planes, rows * blocks, LANES), out_shape],
        in_specs=[vmem] * (parts - 1),
        out_specs=[vmem, anywhere],
        scratch_shapes=[dma((planes,))],
        compiler_params=params,
        cost_estimate=cost,
        name="early",
    )(*[in_vmem(conv) for conv in convs[:-1]])
    conv, tiles, out = pl.pallas_call(
        functools.partial(last_kernel, sizes, parts - 1, depth_count - 1),
        out_shape=[group_shapes(parts - 1)[1], held(planes, rows * blocks, LANES), out_shape],
        in_specs=[smem] * 2 + [vmem] * 4 + [anywhere],
        out_specs=[vmem, vmem, anywhere],
        scratch_shapes=[dma((planes,))],
        input_output_aliases={4: 0, 5: 1, 6: 2},
        compiler_params=params,
        cost_estimate=cost,
        name="last",
    )(plane_slot, ratio_near, in_vmem(entries[-1]), arriving[-1], in_vmem(convs[-1]), in_vmem(tiles), out)
    out = out.reshape(planes, rows // SUB, blocks, SUB, LANES).transpose(0, 1, 3, 2, 4)
    return out.reshape(planes, rows, cols)


def solution(mesh):
    return jax.shard_map(
        per_device,
        mesh=mesh,
        in_specs=(P("depth", "sky", None), P("depth"), P("depth"), P(), P()),
        out_specs=P("depth", "sky", None),
        check_vma=False,
    )
```

```python
import functools

import jax
import jax.numpy as jnp
from jax import lax
from jax.experimental import pallas as pl
from jax.experimental.pallas import tpu as pltpu
from jax.sharding import PartitionSpec as P

WMAX = 8
RIM = WMAX + 1
LANES = 128
SUB = 8
INNER_ROWS, FINAL_ROWS = 9, 4
TOGETHER = 4
PARTS = (3, 2, 2)
BORDER_SHARES = (((0, 1),), ((0,), (1,)))
SHARES = 2
SENT = 7
TINY, POLE, FAR = 1e-30, 1e-20, 1e10
VMEM_LIMIT = 16 * 1024 * 1024
F32, BF16 = jnp.float32, jnp.bfloat16


def group_sizes(row_count):
    return (INNER_ROWS, row_count - 2 * RIM - INNER_ROWS, RIM, RIM)


def is_even():
    return lax.rem(lax.axis_index("sky"), 2) == 0


def pieces_of(row_count):
    sizes = group_sizes(row_count)
    even = is_even()
    split_last = [(jnp.where(even, FINAL_ROWS, 0), RIM - FINAL_ROWS), (jnp.where(even, 0, RIM - FINAL_ROWS), FINAL_ROWS)]
    return [(part, 0, count) for part, count in enumerate(sizes[:-1])] + [(len(sizes) - 1, *one) for one in split_last]


def side_starts(row_count):
    low, high = (0, -RIM), (row_count - RIM, row_count)
    even = is_even()
    paired = [jnp.where(even, b, a) for a, b in zip(low, high)]
    other = [jnp.where(even, a, b) for a, b in zip(low, high)]
    return paired, other


def first_row(row_count, part):
    return (RIM, RIM + INNER_ROWS)[part] if part < 2 else side_starts(row_count)[part - 2][0]


def split(value, parts):
    found = []
    for part in range(parts):
        found.append(value.astype(BF16))
        if part + 1 < parts:
            value = value - found[-1].astype(F32)
    return found


def make_bands(band_ref):
    source = lax.broadcasted_iota(jnp.int32, (LANES, 2 * LANES), 0)
    target = lax.broadcasted_iota(jnp.int32, (LANES, 2 * LANES), 1)
    across = jnp.where(target >= LANES + LANES // 2, source + 2 * LANES, source)
    offset = across - target
    distance = jnp.abs(offset)

    def width(index, carry):
        half_width = index + 1
        rim = (distance == half_width + 1).astype(F32)
        edge = (distance == half_width).astype(F32)
        inside = (distance <= half_width).astype(F32)
        both = rim + edge
        for field, value in enumerate((rim - edge, jnp.where(offset > 0, both, -both), inside)):
            band_ref[index, field] = value.astype(BF16)
        return carry

    lax.fori_loop(0, WMAX, width, 0)


def build(k, half_width, first, count, blocks, x_ref, left_ref):
    def row(index):
        return x_ref[k, pl.ds(pl.multiple_of(index * blocks, blocks), blocks), :]

    total = row(first)
    for step in range(1, WMAX + 1):
        total = total + jnp.where(step <= half_width, row(first - step) + row(first + step), 0.0)
    for i in range(count):
        high, low = first + i + half_width, first + i - half_width
        rim_high, edge_high, edge_low, rim_low = row(high + 1), row(high), row(low), row(low - 1)
        values = (total, (rim_high + edge_high) - (edge_low + rim_low),
                  (rim_high - edge_high) - (edge_low - rim_low))
        total = total + (rim_high - edge_low)
        here = slice(i * blocks, (i + 1) * blocks)
        for field, value in enumerate(values):
            for part, piece in enumerate(split(value, PARTS[field])):
                left_ref[field, here, part * LANES:(part + 1) * LANES] = piece


def multiply(half_width, field, length, band_ref, left_ref):
    weight = jnp.concatenate([band_ref[half_width - 1, field]] * PARTS[field], axis=0)
    return jnp.dot(left_ref[field, :length, :PARTS[field] * LANES], weight, preferred_element_type=F32)


def combine(k, field, near, scale, blocks, product, beside_ref, entry_ref):
    pitch = blocks + SUB
    count = product.shape[0] // blocks
    left_lane = lax.broadcasted_iota(jnp.int32, (blocks, LANES), 1) < LANES // 2
    factor = -0.25 * scale if field == 1 else -scale
    for at in range(count):
        beside_ref[field, pl.ds(at * pitch + SUB, blocks), :] = product[at * blocks:(at + 1) * blocks, LANES:]
    for at in range(count):
        beside = jnp.where(left_lane, beside_ref[field, pl.ds(at * pitch + SUB - 1, blocks), :],
                           beside_ref[field, pl.ds(at * pitch + SUB + 1, blocks), :])
        value = factor * (product[at * blocks:(at + 1) * blocks, :LANES] + beside)
        entry_ref[k, field, pl.ds(at * blocks, blocks), :] = value if field == 1 else value + near


def sweep(planes, base, length, near_of, entry_ref, conv_ref, start, finish):
    step = next(count * SUB for count in (4, 3, 2, 1) if length % (count * SUB) == 0)

    def part(index, carry):
        own = pl.ds(pl.multiple_of(index * step, SUB), step)
        where = pl.ds(pl.multiple_of(base + index * step, SUB), step)
        now, then = (None, None) if start is None else start(own)
        for k in range(planes):
            xx, xy, yy = [entry_ref[k, i, where, :] for i in range(3)]
            kept = 1.0 - near_of(k)
            if now is None:
                one, zero = jnp.ones((step, LANES), F32), jnp.zeros((step, LANES), F32)
                now, new = [one, zero, zero, one], [xx + kept, xy, xy, yy + kept]
            else:
                new = [
                    xx * now[0] + xy * now[2],
                    xx * now[1] + xy * now[3],
                    xy * now[0] + yy * now[2],
                    xy * now[1] + yy * now[3],
                ]
                if then is None:
                    new = [new[0] + kept, new[1], new[2], new[3] + kept]
                else:
                    new = [value + kept * old for value, old in zip(new, then)]
            then = now if k or start is not None else None
            now = new
            conv_ref[k, where, :] = 1.0 - 0.5 * (new[0] + new[3])
        if finish is not None:
            finish(own, now + then)
        return carry

    lax.fori_loop(0, length // step, part, 0)


def packed_state(state):
    a00, a01, a10, a11, b00, b01, b10, b11 = state
    p = [a00 + b01, a10 + b11, a01 - b00, a11 - b10]
    q = [a00 - b01, a10 - b11, a01 + b00, a11 + b10]
    most = jnp.maximum(jnp.maximum(jnp.abs(q[0]), jnp.abs(q[1])), jnp.maximum(jnp.abs(q[2]), jnp.abs(q[3])))
    scale = 1.0 / jnp.maximum(most, TINY)
    q = [value * scale for value in q]
    side = q[0] * q[0] + q[1] * q[1] + q[2] * q[2]
    reach = jnp.sqrt(side + q[3] * q[3]) + jnp.abs(q[3])
    ahead = q[3] >= 0.0
    factor = jnp.where(ahead, 1.0, reach) / jnp.where(ahead, jnp.maximum(reach, TINY), jnp.maximum(side, POLE))
    at_pole = jnp.logical_and(jnp.logical_not(ahead), side < POLE)
    u = [value * factor for value in q[:3]]
    return p + [jnp.where(at_pole, FAR, u[0]), u[1], u[2]]


def unpacked_state(values):
    p, u = values[:4], values[4:]
    most = jnp.maximum(jnp.maximum(jnp.abs(p[0]), jnp.abs(p[1])), jnp.maximum(jnp.abs(p[2]), jnp.abs(p[3])))
    bound = jnp.maximum(most, TINY)
    scale = 1.0 / bound
    unit = [value * scale for value in p]
    norm = bound * jnp.sqrt((unit[0] * unit[0] + unit[1] * unit[1]) + (unit[2] * unit[2] + unit[3] * unit[3]))
    square = u[0] * u[0] + u[1] * u[1] + u[2] * u[2]
    share = 1.0 / (1.0 + square)
    q = [norm * (2.0 * share * value) for value in u] + [norm * ((1.0 - square) * share)]
    half = lambda a, b: 0.5 * (a + b)
    now = [half(p[0], q[0]), half(p[2], q[2]), half(p[1], q[1]), half(p[3], q[3])]
    then = [half(q[2], -p[2]), half(p[0], -q[0]), half(q[3], -p[3]), half(p[1], -q[1])]
    return now, then


def writer(state_ref):
    def finish(where, state):
        for i, value in enumerate(packed_state(state)):
            state_ref[i, where, :] = value

    return finish


def steps_of(planes, shares):
    count = planes // SHARES
    per = next(n for n in range(max(1, TOGETHER // len(shares)), 0, -1) if count % n == 0)
    return count // per, per


def group_stage(sizes, part, scalars, x_ref, band_ref, scratch, entry_ref, before_plane=None,
                shares=tuple(range(SHARES))):
    planes, rows, blocks = sizes
    widths, slots, near, lens = scalars
    left_refs, beside_refs = scratch[::2], scratch[1::2]
    first, count = first_row(rows, part) + RIM, group_sizes(rows)[part]
    steps, per = steps_of(planes, shares)
    for beside_ref in beside_refs:
        beside_ref[...] = jnp.zeros(beside_ref.shape, F32)

    def step(index, carry):
        ks = []
        for i in range(per):
            for share in shares:
                place = index * per + i
                ks.append(place * SHARES + share)
                if before_plane is not None:
                    before_plane(share, place, ks[-1])
        for k, left_ref in zip(ks, left_refs):
            build(k, widths[k], first, count, blocks, x_ref, left_ref)
        for field in range(3):
            for k, left_ref, beside_ref in zip(ks, left_refs, beside_refs):
                width = (2 * widths[k] + 1).astype(F32)
                combine(k, field, near[slots[k]], lens[slots[k]] / (width * width), blocks,
                        multiply(widths[k], field, count * blocks, band_ref, left_ref), beside_ref, entry_ref)
        return carry

    lax.fori_loop(0, steps, step, 0)


def is_first():
    return lax.axis_index("depth") == 0


def first_sweep(sizes, part, scalars, entry_ref, conv_ref, state_refs):
    planes, rows, blocks = sizes
    widths, slots, near, lens = scalars
    pieces = [(base, count) for group, base, count in pieces_of(rows) if group == part]

    @pl.when(is_first())
    def _():
        for (base, count), state_ref in zip(pieces, state_refs):
            sweep(planes, base * blocks, count * blocks, lambda k: near[slots[k]], entry_ref, conv_ref, None,
                  writer(state_ref))


def first_kernel(sizes, widths_hbm, slots_hbm, near_hbm, lens_hbm, potential_hbm, x_ref, band_ref, entry_ref, conv_ref,
                 state_ref, *refs):
    planes, rows, blocks = sizes
    sends, scratch = refs[:2 * SHARES], refs[2 * SHARES:]
    scratch, (tiles_ref, widths, slots, near, lens, plane_sems, table_sems) = scratch[:-7], scratch[-7:]
    tables = ((widths_hbm, widths), (slots_hbm, slots), (near_hbm, near), (lens_hbm, lens))
    copies = [pltpu.make_async_copy(*pair, table_sems.at[i]) for i, pair in enumerate(tables)]
    for copy in copies:
        copy.start()

    def plane_copy(k):
        return pltpu.make_async_copy(potential_hbm.at[k], tiles_ref.at[k], plane_sems.at[k])

    for k in range(planes):
        plane_copy(k).start()
    make_bands(band_ref)
    for copy in copies:
        copy.wait()
    sides = [(start + RIM) * blocks for start, _ in side_starts(rows)]

    def arrive(share, place, k):
        plane_copy(k).wait()
        for row in range(rows):
            for half in range(blocks // SUB):
                start = (row // SUB) * SUB * blocks + half * SUB * SUB + row % SUB
                x_ref[k, pl.ds((row + RIM) * blocks + half * SUB, SUB), :] = tiles_ref[
                    k, pl.ds(start, SUB, stride=SUB), :]
        for i, side in enumerate(sides):
            sends[i * SHARES + share][place] = x_ref[k, pl.ds(pl.multiple_of(side, blocks), RIM * blocks), :]

    scalars = (widths, slots, near, lens)

    @pl.when(is_first())
    def _():
        group_stage(sizes, 0, scalars, x_ref, band_ref, scratch, entry_ref, arrive)

    @pl.when(jnp.logical_not(is_first()))
    def _():
        def place(index, carry):
            for share in range(SHARES):
                arrive(share, index, index * SHARES + share)
            return carry

        lax.fori_loop(0, planes // SHARES, place, 0)

    first_sweep(sizes, 0, scalars, entry_ref, conv_ref, [state_ref])


def second_kernel(sizes, widths, slots, near, lens, band_ref, x_ref, entry_ref, conv_ref, state_ref, *scratch):
    scalars = (widths, slots, near, lens)
    group_stage(sizes, 1, scalars, x_ref, band_ref, scratch, entry_ref)
    first_sweep(sizes, 1, scalars, entry_ref, conv_ref, [state_ref])


def border_kernel(sizes, part, shares, counts, widths, slots, near, lens, band_ref, x_in, *refs):
    planes, rows, blocks = sizes
    handed, results, _ = counts
    refs = refs[handed:]
    arrived, refs = refs[:len(shares)], refs[len(shares) + counts[2]:]
    (x_ref, entry_ref, *made), scratch = refs[:results], refs[results:]
    start = side_starts(rows)[part - 2][1] + RIM
    scalars = (widths, slots, near, lens)

    def arrive(share, place, k):
        x_ref[k, pl.ds(pl.multiple_of(start * blocks, blocks), RIM * blocks), :] = arrived[shares.index(share)][place]

    group_stage(sizes, part, scalars, x_ref, band_ref, scratch, entry_ref, arrive, shares)
    if shares[-1] == SHARES - 1:
        first_sweep(sizes, part, scalars, entry_ref, made[0], made[1:])
    elif shares[0] == 0:
        @pl.when(jnp.logical_not(is_first()))
        def _():
            for share in range(SHARES):
                group_stage(sizes, 0, scalars, x_ref, band_ref, scratch, made[0], None, (share,))


def resume(sizes, piece, turn, slots, near, entry_ref, incoming, conv_ref, finish):
    planes, rows, blocks = sizes
    part, base, count = pieces_of(rows)[piece]

    @pl.when(lax.axis_index("depth") == turn)
    def _():
        sweep(planes, base * blocks, count * blocks, lambda k: near[slots[k]], entry_ref, conv_ref,
              lambda where: unpacked_state([incoming[i, where, :] for i in range(SENT)]), finish)


def resume_kernel(sizes, piece, turn, slots, near, entry_ref, incoming, conv_in, behind, conv_ref, *state_ref):
    resume(sizes, piece, turn, slots, near, entry_ref, incoming, conv_ref, writer(state_ref[0]) if state_ref else None)


def place_rows(sizes, piece, k, conv_ref, tiles_ref):
    planes, rows, blocks = sizes
    part, base, count = pieces_of(rows)[piece]
    start = first_row(rows, part) + base
    for i in range(count):
        row = start + i
        for half in range(blocks // SUB):
            to = lax.div(row, SUB) * SUB * blocks + half * SUB * SUB + lax.rem(row, SUB)
            at = (base + i) * blocks + half * SUB
            tiles_ref[k, pl.ds(to, SUB, stride=SUB), :] = conv_ref[k, pl.ds(pl.multiple_of(at, SUB), SUB), :]


def write_out(sizes, late, tiles_ref, out_hbm, sems, before_plane):
    planes, rows, blocks = sizes
    even = is_even()
    tail = -(-FINAL_ROWS // SUB) * SUB
    if late:
        start, count = jnp.where(even, 0, rows - tail), tail
    else:
        start, count = jnp.where(even, tail, 0), rows - tail

    def plane_copy(k):
        where = pl.ds(pl.multiple_of(start * blocks, SUB * blocks), count * blocks)
        return pltpu.make_async_copy(tiles_ref.at[k, where], out_hbm.at[k, where], sems.at[k])

    def plane(k, carry):
        before_plane(k)
        plane_copy(k).start()
        return carry

    lax.fori_loop(0, planes, plane, 0)
    for k in range(planes):
        plane_copy(k).wait()


def early_kernel(sizes, *refs):
    *conv_refs, tiles_ref, out_hbm, sems = refs

    def place(k):
        for piece, (part, _, _) in enumerate(pieces_of(sizes[1])[:-1]):
            place_rows(sizes, piece, k, conv_refs[part], tiles_ref)

    write_out(sizes, False, tiles_ref, out_hbm, sems, place)


def last_kernel(sizes, piece, turn, slots, near, entry_ref, incoming, conv_in, tiles_in, out_in, conv_ref, tiles_ref,
                out_hbm, sems):
    resume(sizes, piece, turn, slots, near, entry_ref, incoming, conv_ref, None)
    write_out(sizes, True, tiles_ref, out_hbm, sems, lambda k: place_rows(sizes, piece, k, conv_ref, tiles_ref))


def per_device(potential, widths, plane_slot, ratio_near, ratio_lens):
    planes, rows, cols = potential.shape
    blocks = cols // LANES
    sizes = (planes, rows, blocks)
    counts = group_sizes(rows)
    parts = len(counts)
    pieces = [(part, count) for part, _, count in pieces_of(rows)]
    depth_count, sky_count = lax.axis_size("depth"), lax.axis_size("sky")
    swaps = [[pair for i in range(first, sky_count - 1, 2) for pair in ((i, i + 1), (i + 1, i))] for first in (0, 1)]
    ahead = [(i, i + 1) for i in range(depth_count - 1)]
    tiled = potential.reshape(planes, rows // SUB, SUB, blocks, LANES).transpose(0, 1, 3, 2, 4)
    tiled = tiled.reshape(planes, rows * blocks, LANES)
    smem = pl.BlockSpec(memory_space=pltpu.SMEM)
    vmem = pl.BlockSpec(memory_space=pltpu.VMEM)
    anywhere = pl.BlockSpec(memory_space=pl.ANY)
    params = pltpu.CompilerParams(vmem_limit_bytes=VMEM_LIMIT)
    scalars = (widths, plane_slot, ratio_near, ratio_lens)
    dma = pltpu.SemaphoreType.DMA
    cost = pl.CostEstimate(flops=1, transcendentals=0, bytes_accessed=1)

    def held(*shape, dtype=F32):
        return pltpu.VMEM(shape, dtype)

    def moved(*shape):
        return jax.ShapeDtypeStruct(shape, F32)

    def in_vmem(array):
        return pltpu.with_memory_space_constraint(array, pltpu.VMEM)

    def in_hbm(array):
        return pltpu.with_memory_space_constraint(array, pltpu.HBM)

    x_shape = held(planes, (rows + 2 * RIM) * blocks, LANES)
    band_shape = held(WMAX, 3, LANES, 2 * LANES, dtype=BF16)

    def entry_shape(part):
        return held(planes, 3, counts[part] * blocks, LANES)

    def conv_shape(part):
        return held(planes, counts[part] * blocks, LANES)

    def state_shape(piece):
        return moved(SENT, pieces[piece][1] * blocks, LANES)

    def group_shapes(part):
        return [conv_shape(part), *[state_shape(piece) for piece, (group, _) in enumerate(pieces) if group == part]]

    def group_scratch(part, shares):
        count = max(counts[0], counts[part]) if part > 1 else counts[part]
        return [held(3, count * blocks, max(PARTS) * LANES, dtype=BF16),
                held(3, (count + 1) * (blocks + SUB), LANES)] * (len(shares) * steps_of(planes, shares)[1])

    side = moved(planes // SHARES, RIM * blocks, LANES)
    x, bands, *rest = pl.pallas_call(
        functools.partial(first_kernel, sizes),
        out_shape=[x_shape, band_shape, entry_shape(0), *group_shapes(0), *[side] * (2 * SHARES)],
        in_specs=[anywhere] * 5,
        out_specs=[vmem] * (5 + 2 * SHARES),
        scratch_shapes=[
            *group_scratch(0, range(SHARES)), held(planes, rows * blocks, LANES),
            *[pltpu.SMEM(array.shape, array.dtype) for array in scalars], dma((planes,)), dma((len(scalars),))],
        compiler_params=params,
        cost_estimate=cost,
        name="first",
    )(*[in_hbm(array) for array in (*scalars, tiled)])
    (entry, conv, state), sends = rest[:3], rest[3:]
    convs, arriving = [conv], [lax.ppermute(state, "depth", ahead)]
    swapped = [[lax.ppermute(piece, "sky", swap) for piece in sends[i * SHARES:(i + 1) * SHARES]]
               for i, swap in enumerate(swaps)]
    entries = [entry]
    entry, conv, state = pl.pallas_call(
        functools.partial(second_kernel, sizes),
        out_shape=[entry_shape(1), *group_shapes(1)],
        in_specs=[smem] * 4 + [vmem] * 2,
        out_specs=[vmem] * 3,
        scratch_shapes=group_scratch(1, range(SHARES)),
        compiler_params=params,
        cost_estimate=cost,
        name="second",
    )(*scalars, in_vmem(bands), in_vmem(x))
    entries.append(entry)
    convs.append(conv)
    arriving.append(lax.ppermute(state, "depth", ahead))
    for part in range(2, parts):
        entry = None
        for shares in BORDER_SHARES[part - 2]:
            last = shares[-1] == SHARES - 1
            behind = [] if part == 2 else [] if last else arriving[:2]
            handed = ([] if entry is None else [entry]) + ([] if last else entries[:1])
            shapes = [x_shape, entry_shape(part), *([] if last else [entry_shape(0)]), *(group_shapes(part) if last else [])]
            x, entry, *group = pl.pallas_call(
                functools.partial(border_kernel, sizes, part, shares, (len(handed), len(shapes), len(behind))),
                out_shape=shapes,
                in_specs=[smem] * 4 + [vmem] * (2 + len(handed) + len(shares)) + [anywhere] * len(behind),
                out_specs=[vmem] * len(shapes),
                scratch_shapes=group_scratch(part, shares),
                input_output_aliases={5: 0} | ({} if entry is None else {6: 1}) | ({} if last else {5 + len(handed): 2}),
                compiler_params=params,
                cost_estimate=cost,
                name="border",
            )(*scalars, in_vmem(bands), in_vmem(x), *map(in_vmem, handed), *[swapped[part - 2][share] for share in shares],
              *behind)
            if not last:
                entries[0] = group[0]
        entries.append(entry)
        convs.append(group[0])
        arriving += [lax.ppermute(state, "depth", ahead) for state in group[1:]]

    for turn in range(1, depth_count):
        last = turn == depth_count - 1
        for piece, (part, _) in enumerate(pieces[:len(pieces) - last]):
            convs[part], *state = pl.pallas_call(
                functools.partial(resume_kernel, sizes, piece, turn),
                out_shape=[conv_shape(part)] + ([] if last else [state_shape(piece)]),
                in_specs=[smem] * 2 + [vmem] * 4,
                out_specs=[vmem] * (1 if last else 2),
                input_output_aliases={4: 0},
                compiler_params=params,
                cost_estimate=cost,
                name="resume",
            )(plane_slot, ratio_near, in_vmem(entries[part]), arriving[piece], in_vmem(convs[part]),
              in_vmem(convs[part - 1]))
            if state:
                arriving[piece] = lax.ppermute(state[0], "depth", ahead)
    out_shape = moved(planes, rows * blocks, LANES)
    tiles, out = pl.pallas_call(
        functools.partial(early_kernel, sizes),
        out_shape=[held(planes, rows * blocks, LANES), out_shape],
        in_specs=[vmem] * parts,
        out_specs=[vmem, anywhere],
        scratch_shapes=[dma((planes,))],
        compiler_params=params,
        cost_estimate=cost,
        name="early",
    )(*[in_vmem(conv) for conv in convs])
    conv, tiles, out = pl.pallas_call(
        functools.partial(last_kernel, sizes, len(pieces) - 1, depth_count - 1),
        out_shape=[conv_shape(parts - 1), held(planes, rows * blocks, LANES), out_shape],
        in_specs=[smem] * 2 + [vmem] * 4 + [anywhere],
        out_specs=[vmem, vmem, anywhere],
        scratch_shapes=[dma((planes,))],
        input_output_aliases={4: 0, 5: 1, 6: 2},
        compiler_params=params,
        cost_estimate=cost,
        name="last",
    )(plane_slot, ratio_near, in_vmem(entries[-1]), arriving[-1], in_vmem(convs[-1]), in_vmem(tiles), out)
    out = out.reshape(planes, rows // SUB, blocks, SUB, LANES).transpose(0, 1, 3, 2, 4)
    return out.reshape(planes, rows, cols)


def solution(mesh):
    return jax.shard_map(
        per_device,
        mesh=mesh,
        in_specs=(P("depth", "sky", None), P("depth"), P("depth"), P(), P()),
        out_specs=P("depth", "sky", None),
        check_vma=False,
    )
```

```python
import functools

import jax
import jax.numpy as jnp
from jax import lax
from jax.experimental import pallas as pl
from jax.experimental.pallas import tpu as pltpu
from jax.sharding import PartitionSpec as P

WMAX = 8
RIM = WMAX + 1
LANES = 128
SUB = 8
INNER_ROWS, FINAL_ROWS = 8, 3
TOGETHER = 4
PARTS = (3, 2, 2)
MADE_UP = {3: 0, 4: 2}
BEHIND = {2: 0, 3: 1}
SHARES = 2
SENT = 7
TINY, POLE, FAR = 1e-30, 1e-20, 1e10
VMEM_LIMIT = 16 * 1024 * 1024
F32, BF16 = jnp.float32, jnp.bfloat16


def group_sizes(row_count):
    return (INNER_ROWS, row_count - 2 * RIM - INNER_ROWS, RIM, RIM - FINAL_ROWS, FINAL_ROWS)


def is_even():
    return lax.rem(lax.axis_index("sky"), 2) == 0


def by_side(paired, low, high):
    return jnp.where(is_even() != paired, low, high)


def first_row(row_count, part):
    if part < 2:
        return (RIM, RIM + INNER_ROWS)[part]
    if part == 2:
        return by_side(True, 0, row_count - RIM)
    if part == 3:
        return by_side(False, FINAL_ROWS, row_count - RIM)
    return by_side(False, 0, row_count - FINAL_ROWS)


def sent_rows(row_count, part):
    near = RIM - FINAL_ROWS
    if part == 2:
        return by_side(True, 0, row_count - RIM), RIM
    if part == 3:
        return by_side(False, 0, row_count - near), near
    return by_side(False, near, row_count - RIM), FINAL_ROWS


def got_rows(row_count, part):
    near = RIM - FINAL_ROWS
    if part == 2:
        return by_side(True, -RIM, row_count), RIM
    if part == 3:
        return by_side(False, -near, row_count), near
    return by_side(False, -RIM, row_count + near), FINAL_ROWS


def split(value, parts):
    found = []
    for part in range(parts):
        found.append(value.astype(BF16))
        if part + 1 < parts:
            value = value - found[-1].astype(F32)
    return found


def make_bands(band_ref):
    source = lax.broadcasted_iota(jnp.int32, (LANES, 2 * LANES), 0)
    target = lax.broadcasted_iota(jnp.int32, (LANES, 2 * LANES), 1)
    across = jnp.where(target >= LANES + LANES // 2, source + 2 * LANES, source)
    offset = across - target
    distance = jnp.abs(offset)

    def width(index, carry):
        half_width = index + 1
        rim = (distance == half_width + 1).astype(F32)
        edge = (distance == half_width).astype(F32)
        inside = (distance <= half_width).astype(F32)
        both = rim + edge
        for field, value in enumerate((rim - edge, jnp.where(offset > 0, both, -both), inside)):
            band_ref[index, field] = value.astype(BF16)
        return carry

    lax.fori_loop(0, WMAX, width, 0)


def build(k, half_width, first, count, blocks, x_ref, left_ref):
    def row(index):
        return x_ref[k, pl.ds(pl.multiple_of(index * blocks, blocks), blocks), :]

    total = row(first)
    for step in range(1, WMAX + 1):
        total = total + jnp.where(step <= half_width, row(first - step) + row(first + step), 0.0)
    for i in range(count):
        high, low = first + i + half_width, first + i - half_width
        rim_high, edge_high, edge_low, rim_low = row(high + 1), row(high), row(low), row(low - 1)
        values = (total, (rim_high + edge_high) - (edge_low + rim_low),
                  (rim_high - edge_high) - (edge_low - rim_low))
        total = total + (rim_high - edge_low)
        here = slice(i * blocks, (i + 1) * blocks)
        for field, value in enumerate(values):
            for part, piece in enumerate(split(value, PARTS[field])):
                left_ref[field, here, part * LANES:(part + 1) * LANES] = piece


def multiply(half_width, field, length, band_ref, left_ref):
    weight = jnp.concatenate([band_ref[half_width - 1, field]] * PARTS[field], axis=0)
    return jnp.dot(left_ref[field, :length, :PARTS[field] * LANES], weight, preferred_element_type=F32)


def combine(k, field, near, scale, blocks, product, beside_ref, entry_ref):
    pitch = blocks + SUB
    count = product.shape[0] // blocks
    left_lane = lax.broadcasted_iota(jnp.int32, (blocks, LANES), 1) < LANES // 2
    factor = -0.25 * scale if field == 1 else -scale
    for at in range(count):
        beside_ref[field, pl.ds(at * pitch + SUB, blocks), :] = product[at * blocks:(at + 1) * blocks, LANES:]
    for at in range(count):
        beside = jnp.where(left_lane, beside_ref[field, pl.ds(at * pitch + SUB - 1, blocks), :],
                           beside_ref[field, pl.ds(at * pitch + SUB + 1, blocks), :])
        value = factor * (product[at * blocks:(at + 1) * blocks, :LANES] + beside)
        entry_ref[k, field, pl.ds(at * blocks, blocks), :] = value if field == 1 else value + near


def sweep(planes, length, near_of, entry_ref, conv_ref, start, finish):
    step = next(count * SUB for count in (4, 3, 2, 1) if length % (count * SUB) == 0)

    def part(index, carry):
        where = pl.ds(pl.multiple_of(index * step, SUB), step)
        now, then = (None, None) if start is None else start(where)
        for k in range(planes):
            xx, xy, yy = [entry_ref[k, i, where, :] for i in range(3)]
            kept = 1.0 - near_of(k)
            if now is None:
                one, zero = jnp.ones((step, LANES), F32), jnp.zeros((step, LANES), F32)
                now, new = [one, zero, zero, one], [xx + kept, xy, xy, yy + kept]
            else:
                new = [
                    xx * now[0] + xy * now[2],
                    xx * now[1] + xy * now[3],
                    xy * now[0] + yy * now[2],
                    xy * now[1] + yy * now[3],
                ]
                if then is None:
                    new = [new[0] + kept, new[1], new[2], new[3] + kept]
                else:
                    new = [value + kept * old for value, old in zip(new, then)]
            then = now if k or start is not None else None
            now = new
            conv_ref[k, where, :] = 1.0 - 0.5 * (new[0] + new[3])
        if finish is not None:
            finish(where, now + then)
        return carry

    lax.fori_loop(0, length // step, part, 0)


def packed_state(state):
    a00, a01, a10, a11, b00, b01, b10, b11 = state
    p = [a00 + b01, a10 + b11, a01 - b00, a11 - b10]
    q = [a00 - b01, a10 - b11, a01 + b00, a11 + b10]
    most = jnp.maximum(jnp.maximum(jnp.abs(q[0]), jnp.abs(q[1])), jnp.maximum(jnp.abs(q[2]), jnp.abs(q[3])))
    scale = 1.0 / jnp.maximum(most, TINY)
    q = [value * scale for value in q]
    side = q[0] * q[0] + q[1] * q[1] + q[2] * q[2]
    reach = jnp.sqrt(side + q[3] * q[3]) + jnp.abs(q[3])
    ahead = q[3] >= 0.0
    factor = jnp.where(ahead, 1.0, reach) / jnp.where(ahead, jnp.maximum(reach, TINY), jnp.maximum(side, POLE))
    at_pole = jnp.logical_and(jnp.logical_not(ahead), side < POLE)
    u = [value * factor for value in q[:3]]
    return p + [jnp.where(at_pole, FAR, u[0]), u[1], u[2]]


def unpacked_state(values):
    p, u = values[:4], values[4:]
    most = jnp.maximum(jnp.maximum(jnp.abs(p[0]), jnp.abs(p[1])), jnp.maximum(jnp.abs(p[2]), jnp.abs(p[3])))
    bound = jnp.maximum(most, TINY)
    scale = 1.0 / bound
    unit = [value * scale for value in p]
    norm = bound * jnp.sqrt((unit[0] * unit[0] + unit[1] * unit[1]) + (unit[2] * unit[2] + unit[3] * unit[3]))
    square = u[0] * u[0] + u[1] * u[1] + u[2] * u[2]
    share = 1.0 / (1.0 + square)
    q = [norm * (2.0 * share * value) for value in u] + [norm * ((1.0 - square) * share)]
    half = lambda a, b: 0.5 * (a + b)
    now = [half(p[0], q[0]), half(p[2], q[2]), half(p[1], q[1]), half(p[3], q[3])]
    then = [half(q[2], -p[2]), half(p[0], -q[0]), half(q[3], -p[3]), half(p[1], -q[1])]
    return now, then


def writer(state_ref):
    def finish(where, state):
        for i, value in enumerate(packed_state(state)):
            state_ref[i, where, :] = value

    return finish


def steps_of(planes, shares):
    count = planes // SHARES
    per = next(n for n in range(max(1, TOGETHER // len(shares)), 0, -1) if count % n == 0)
    return count // per, per


def group_stage(sizes, part, scalars, x_ref, band_ref, scratch, entry_ref, before_plane=None,
                shares=tuple(range(SHARES))):
    planes, rows, blocks = sizes
    widths, slots, near, lens = scalars
    left_refs, beside_refs = scratch[::2], scratch[1::2]
    first, count = first_row(rows, part) + RIM, group_sizes(rows)[part]
    steps, per = steps_of(planes, shares)
    for beside_ref in beside_refs:
        beside_ref[...] = jnp.zeros(beside_ref.shape, F32)

    def step(index, carry):
        ks = []
        for i in range(per):
            for share in shares:
                place = index * per + i
                ks.append(place * SHARES + share)
                if before_plane is not None:
                    before_plane(share, place, ks[-1])
        for k, left_ref in zip(ks, left_refs):
            build(k, widths[k], first, count, blocks, x_ref, left_ref)
        for field in range(3):
            for k, left_ref, beside_ref in zip(ks, left_refs, beside_refs):
                width = (2 * widths[k] + 1).astype(F32)
                combine(k, field, near[slots[k]], lens[slots[k]] / (width * width), blocks,
                        multiply(widths[k], field, count * blocks, band_ref, left_ref), beside_ref, entry_ref)
        return carry

    lax.fori_loop(0, steps, step, 0)


def is_first():
    return lax.axis_index("depth") == 0


def first_sweep(sizes, part, scalars, entry_ref, conv_ref, state_ref):
    planes, rows, blocks = sizes
    widths, slots, near, lens = scalars

    @pl.when(is_first())
    def _():
        sweep(planes, group_sizes(rows)[part] * blocks, lambda k: near[slots[k]], entry_ref, conv_ref, None,
              writer(state_ref))


def each_plane(planes, body):
    def step(place, carry):
        for share in range(SHARES):
            body(share, place, place * SHARES + share)
        return carry

    lax.fori_loop(0, planes // SHARES, step, 0)


def first_kernel(sizes, widths_hbm, slots_hbm, near_hbm, lens_hbm, potential_hbm, x_ref, band_ref, entry_ref, conv_ref,
                 state_ref, near_ref, far_ref, *rest):
    planes, rows, blocks = sizes
    paired_refs, scratch = rest[:SHARES], rest[SHARES:]
    scratch, (tiles_ref, widths, slots, near, lens, plane_sems, table_sems) = scratch[:-7], scratch[-7:]
    tables = ((widths_hbm, widths), (slots_hbm, slots), (near_hbm, near), (lens_hbm, lens))
    copies = [pltpu.make_async_copy(*pair, table_sems.at[i]) for i, pair in enumerate(tables)]
    for copy in copies:
        copy.start()

    def plane_copy(k):
        return pltpu.make_async_copy(potential_hbm.at[k], tiles_ref.at[k], plane_sems.at[k])

    for k in range(planes):
        plane_copy(k).start()
    make_bands(band_ref)
    for copy in copies:
        copy.wait()

    def arrive(share, place, k):
        plane_copy(k).wait()
        for row in range(rows):
            for half in range(blocks // SUB):
                start = (row // SUB) * SUB * blocks + half * SUB * SUB + row % SUB
                x_ref[k, pl.ds((row + RIM) * blocks + half * SUB, SUB), :] = tiles_ref[
                    k, pl.ds(start, SUB, stride=SUB), :]
        for part, ref, at in ((2, paired_refs[share], place), (3, near_ref, k), (4, far_ref, k)):
            start, count = sent_rows(rows, part)
            ref[at] = x_ref[k, pl.ds(pl.multiple_of((start + RIM) * blocks, blocks), count * blocks), :]

    scalars = (widths, slots, near, lens)

    @pl.when(is_first())
    def _():
        group_stage(sizes, 0, scalars, x_ref, band_ref, scratch, entry_ref, arrive)

    @pl.when(jnp.logical_not(is_first()))
    def _():
        each_plane(planes, arrive)

    first_sweep(sizes, 0, scalars, entry_ref, conv_ref, state_ref)


def second_kernel(sizes, widths, slots, near, lens, band_ref, x_ref, entry_ref, conv_ref, state_ref, *scratch):
    scalars = (widths, slots, near, lens)
    group_stage(sizes, 1, scalars, x_ref, band_ref, scratch, entry_ref)
    first_sweep(sizes, 1, scalars, entry_ref, conv_ref, state_ref)


def border_kernel(sizes, part, widths, slots, near, lens, band_ref, x_in, *refs):
    planes, rows, blocks = sizes
    made_up = part in MADE_UP
    arrived, refs = refs[made_up:made_up + (SHARES if part == 2 else 1)], refs[made_up + (SHARES if part == 2 else 1) + (part in BEHIND):]
    x_ref, entry_ref, conv_ref, state_ref, *scratch = refs
    start, count = got_rows(rows, part)
    scalars = (widths, slots, near, lens)

    def arrive(share, place, k):
        rows_in = arrived[share][place] if part == 2 else arrived[0][k]
        x_ref[k, pl.ds(pl.multiple_of((start + RIM) * blocks, blocks), count * blocks), :] = rows_in

    if made_up:
        other_ref, scratch = scratch[0], scratch[1:]
    if part in MADE_UP.values():

        @pl.when(is_first())
        def _():
            group_stage(sizes, part, scalars, x_ref, band_ref, scratch, entry_ref, arrive)

        @pl.when(jnp.logical_not(is_first()))
        def _():
            each_plane(planes, arrive)

    else:
        group_stage(sizes, part, scalars, x_ref, band_ref, scratch, entry_ref, arrive)
    if made_up:

        @pl.when(jnp.logical_not(is_first()))
        def _():
            group_stage(sizes, MADE_UP[part], scalars, x_ref, band_ref, scratch, other_ref)

    first_sweep(sizes, part, scalars, entry_ref, conv_ref, state_ref)


def resume(sizes, part, turn, slots, near, entry_ref, incoming, conv_ref, finish):
    planes, rows, blocks = sizes

    @pl.when(lax.axis_index("depth") == turn)
    def _():
        sweep(planes, group_sizes(rows)[part] * blocks, lambda k: near[slots[k]], entry_ref, conv_ref,
              lambda where: unpacked_state([incoming[i, where, :] for i in range(SENT)]), finish)


def resume_kernel(sizes, part, turn, slots, near, entry_ref, incoming, conv_in, behind, conv_ref, *state_ref):
    resume(sizes, part, turn, slots, near, entry_ref, incoming, conv_ref, writer(state_ref[0]) if state_ref else None)


def place_rows(sizes, part, k, conv_ref, tiles_ref):
    planes, rows, blocks = sizes
    start = first_row(rows, part)
    for i in range(group_sizes(rows)[part]):
        row = start + i
        for half in range(blocks // SUB):
            to = lax.div(row, SUB) * SUB * blocks + half * SUB * SUB + lax.rem(row, SUB)
            tiles_ref[k, pl.ds(to, SUB, stride=SUB), :] = conv_ref[k, pl.ds(i * blocks + half * SUB, SUB), :]


def write_out(sizes, late, tiles_ref, out_hbm, sems, before_plane):
    planes, rows, blocks = sizes
    even = is_even()
    tail = -(-FINAL_ROWS // SUB) * SUB
    if late:
        start, count = jnp.where(even, 0, rows - tail), tail
    else:
        start, count = jnp.where(even, tail, 0), rows - tail

    def plane_copy(k):
        where = pl.ds(pl.multiple_of(start * blocks, SUB * blocks), count * blocks)
        return pltpu.make_async_copy(tiles_ref.at[k, where], out_hbm.at[k, where], sems.at[k])

    def plane(k, carry):
        before_plane(k)
        plane_copy(k).start()
        return carry

    lax.fori_loop(0, planes, plane, 0)
    for k in range(planes):
        plane_copy(k).wait()


def early_kernel(sizes, *refs):
    *conv_refs, tiles_ref, out_hbm, sems = refs

    def place(k):
        for part, conv_ref in enumerate(conv_refs):
            place_rows(sizes, part, k, conv_ref, tiles_ref)

    write_out(sizes, False, tiles_ref, out_hbm, sems, place)


def last_kernel(sizes, part, turn, slots, near, entry_ref, incoming, conv_in, tiles_in, out_in, conv_ref, tiles_ref,
                out_hbm, sems):
    resume(sizes, part, turn, slots, near, entry_ref, incoming, conv_ref, None)
    write_out(sizes, True, tiles_ref, out_hbm, sems, lambda k: place_rows(sizes, part, k, conv_ref, tiles_ref))


def per_device(potential, widths, plane_slot, ratio_near, ratio_lens):
    planes, rows, cols = potential.shape
    blocks = cols // LANES
    sizes = (planes, rows, blocks)
    counts = group_sizes(rows)
    parts = len(counts)
    depth_count, sky_count = lax.axis_size("depth"), lax.axis_size("sky")
    swaps = [[pair for i in range(first, sky_count - 1, 2) for pair in ((i, i + 1), (i + 1, i))] for first in (0, 1)]
    ahead = [(i, i + 1) for i in range(depth_count - 1)]
    tiled = potential.reshape(planes, rows // SUB, SUB, blocks, LANES).transpose(0, 1, 3, 2, 4)
    tiled = tiled.reshape(planes, rows * blocks, LANES)
    smem = pl.BlockSpec(memory_space=pltpu.SMEM)
    vmem = pl.BlockSpec(memory_space=pltpu.VMEM)
    anywhere = pl.BlockSpec(memory_space=pl.ANY)
    params = pltpu.CompilerParams(vmem_limit_bytes=VMEM_LIMIT)
    scalars = (widths, plane_slot, ratio_near, ratio_lens)
    dma = pltpu.SemaphoreType.DMA
    cost = pl.CostEstimate(flops=1, transcendentals=0, bytes_accessed=1)

    def held(*shape, dtype=F32):
        return pltpu.VMEM(shape, dtype)

    def moved(*shape):
        return jax.ShapeDtypeStruct(shape, F32)

    def in_vmem(array):
        return pltpu.with_memory_space_constraint(array, pltpu.VMEM)

    def in_hbm(array):
        return pltpu.with_memory_space_constraint(array, pltpu.HBM)

    x_shape = held(planes, (rows + 2 * RIM) * blocks, LANES)
    band_shape = held(WMAX, 3, LANES, 2 * LANES, dtype=BF16)

    def entry_shape(part):
        return held(planes, 3, counts[part] * blocks, LANES)

    def conv_shape(part):
        return held(planes, counts[part] * blocks, LANES)

    def state_shape(part):
        return moved(SENT, counts[part] * blocks, LANES)

    def group_shapes(part):
        return [entry_shape(part), conv_shape(part), state_shape(part)]

    def group_scratch(part):
        count = max(counts[part], counts[MADE_UP[part]] if part in MADE_UP else 0)
        return [held(3, count * blocks, max(PARTS) * LANES, dtype=BF16),
                held(3, (count + 1) * (blocks + SUB), LANES)] * (SHARES * steps_of(planes, range(SHARES))[1])

    def side_shape(part, shares=1):
        return moved(planes // shares, sent_rows(rows, part)[1] * blocks, LANES)

    x, bands, entry, conv, state, close, far, *paired = pl.pallas_call(
        functools.partial(first_kernel, sizes),
        out_shape=[x_shape, band_shape, *group_shapes(0), side_shape(3), side_shape(4), *[side_shape(2, SHARES)] * SHARES],
        in_specs=[anywhere] * 5,
        out_specs=[vmem] * (7 + SHARES),
        scratch_shapes=[
            *group_scratch(0), held(planes, rows * blocks, LANES),
            *[pltpu.SMEM(array.shape, array.dtype) for array in scalars], dma((planes,)), dma((len(scalars),))],
        compiler_params=params,
        cost_estimate=cost,
        name="first",
    )(*[in_hbm(array) for array in (*scalars, tiled)])
    entries, convs, arriving = [entry], [conv], [lax.ppermute(state, "depth", ahead)]
    entry, conv, state = pl.pallas_call(
        functools.partial(second_kernel, sizes),
        out_shape=group_shapes(1),
        in_specs=[smem] * 4 + [vmem] * 2,
        out_specs=[vmem] * 3,
        scratch_shapes=group_scratch(1),
        compiler_params=params,
        cost_estimate=cost,
        name="second",
    )(*scalars, in_vmem(bands), in_vmem(x))
    entries.append(entry)
    convs.append(conv)
    arriving.append(lax.ppermute(state, "depth", ahead))
    swapped = {part: [lax.ppermute(piece, "sky", swaps[part > 2]) for piece in pieces]
               for part, pieces in ((2, paired), (3, [close]), (4, [far]))}
    for part in range(2, parts):
        other = [entries[MADE_UP[part]]] if part in MADE_UP else []
        x, entry, conv, state, *again = pl.pallas_call(
            functools.partial(border_kernel, sizes, part),
            out_shape=[x_shape, *group_shapes(part), *[entry_shape(MADE_UP[part]) for _ in other]],
            in_specs=[smem] * 4 + [vmem] * (2 + len(other) + len(swapped[part])) + [anywhere] * (part in BEHIND),
            out_specs=[vmem] * (4 + len(other)),
            scratch_shapes=group_scratch(part),
            input_output_aliases={5: 0} | ({6: 4} if other else {}),
            compiler_params=params,
            cost_estimate=cost,
            name="border",
        )(*scalars, in_vmem(bands), in_vmem(x), *map(in_vmem, other), *swapped[part], *[arriving[BEHIND[part]] for _ in range(part in BEHIND)])
        if other:
            entries[MADE_UP[part]], = again
        entries.append(entry)
        convs.append(conv)
        arriving.append(lax.ppermute(state, "depth", ahead))

    for turn in range(1, depth_count):
        last = turn == depth_count - 1
        for part in range(parts - last):
            convs[part], *state = pl.pallas_call(
                functools.partial(resume_kernel, sizes, part, turn),
                out_shape=[conv_shape(part)] + ([] if last else [state_shape(part)]),
                in_specs=[smem] * 2 + [vmem] * 4,
                out_specs=[vmem] * (1 if last else 2),
                input_output_aliases={4: 0},
                compiler_params=params,
                cost_estimate=cost,
                name="resume",
            )(plane_slot, ratio_near, in_vmem(entries[part]), arriving[part], in_vmem(convs[part]),
              in_vmem(convs[part - 1]))
            if state:
                arriving[part] = lax.ppermute(state[0], "depth", ahead)
    out_shape = moved(planes, rows * blocks, LANES)
    tiles, out = pl.pallas_call(
        functools.partial(early_kernel, sizes),
        out_shape=[held(planes, rows * blocks, LANES), out_shape],
        in_specs=[vmem] * (parts - 1),
        out_specs=[vmem, anywhere],
        scratch_shapes=[dma((planes,))],
        compiler_params=params,
        cost_estimate=cost,
        name="early",
    )(*[in_vmem(conv) for conv in convs[:-1]])
    conv, tiles, out = pl.pallas_call(
        functools.partial(last_kernel, sizes, parts - 1, depth_count - 1),
        out_shape=[conv_shape(parts - 1), held(planes, rows * blocks, LANES), out_shape],
        in_specs=[smem] * 2 + [vmem] * 4 + [anywhere],
        out_specs=[vmem, vmem, anywhere],
        scratch_shapes=[dma((planes,))],
        input_output_aliases={4: 0, 5: 1, 6: 2},
        compiler_params=params,
        cost_estimate=cost,
        name="last",
    )(plane_slot, ratio_near, in_vmem(entries[-1]), arriving[-1], in_vmem(convs[-1]), in_vmem(tiles), out)
    out = out.reshape(planes, rows // SUB, blocks, SUB, LANES).transpose(0, 1, 3, 2, 4)
    return out.reshape(planes, rows, cols)


def solution(mesh):
    return jax.shard_map(
        per_device,
        mesh=mesh,
        in_specs=(P("depth", "sky", None), P("depth"), P("depth"), P(), P()),
        out_specs=P("depth", "sky", None),
        check_vma=False,
    )
```

```python
import functools

import jax
import jax.numpy as jnp
from jax import lax
from jax.experimental import pallas as pl
from jax.experimental.pallas import tpu as pltpu
from jax.sharding import PartitionSpec as P

WMAX = 8
RIM = WMAX + 1
LANES = 128
SUB = 8
INNER_ROWS, FINAL_ROWS = 8, 3
TOGETHER = 6
PARTS = (3, 2, 2)
MADE_UP = {3: 0, 4: 2}
BEHIND = {2: 0, 3: 1}
SHARES = 2
SENT = 7
TINY, POLE, FAR = 1e-30, 1e-20, 1e10
VMEM_LIMIT = 16 * 1024 * 1024
F32, BF16 = jnp.float32, jnp.bfloat16


def group_sizes(row_count):
    return (INNER_ROWS, row_count - 2 * RIM - INNER_ROWS, RIM, RIM - FINAL_ROWS, FINAL_ROWS)


def is_even():
    return lax.rem(lax.axis_index("sky"), 2) == 0


def by_side(paired, low, high):
    return jnp.where(is_even() != paired, low, high)


def first_row(row_count, part):
    if part < 2:
        return (RIM, RIM + INNER_ROWS)[part]
    if part == 2:
        return by_side(True, 0, row_count - RIM)
    if part == 3:
        return by_side(False, FINAL_ROWS, row_count - RIM)
    return by_side(False, 0, row_count - FINAL_ROWS)


def sent_rows(row_count, part):
    near = RIM - FINAL_ROWS
    if part == 2:
        return by_side(True, 0, row_count - RIM), RIM
    if part == 3:
        return by_side(False, 0, row_count - near), near
    return by_side(False, near, row_count - RIM), FINAL_ROWS


def got_rows(row_count, part):
    near = RIM - FINAL_ROWS
    if part == 2:
        return by_side(True, -RIM, row_count), RIM
    if part == 3:
        return by_side(False, -near, row_count), near
    return by_side(False, -RIM, row_count + near), FINAL_ROWS


def split(value, parts):
    found = []
    for part in range(parts):
        found.append(value.astype(BF16))
        if part + 1 < parts:
            value = value - found[-1].astype(F32)
    return found


def make_bands(band_ref):
    source = lax.broadcasted_iota(jnp.int32, (LANES, 2 * LANES), 0)
    target = lax.broadcasted_iota(jnp.int32, (LANES, 2 * LANES), 1)
    across = jnp.where(target >= LANES + LANES // 2, source + 2 * LANES, source)
    offset = across - target
    distance = jnp.abs(offset)

    def width(index, carry):
        half_width = index + 1
        rim = (distance == half_width + 1).astype(F32)
        edge = (distance == half_width).astype(F32)
        inside = (distance <= half_width).astype(F32)
        both = rim + edge
        for field, value in enumerate((rim - edge, jnp.where(offset > 0, both, -both), inside)):
            band_ref[index, field] = value.astype(BF16)
        return carry

    lax.fori_loop(0, WMAX, width, 0)


def build(k, half_width, first, count, blocks, x_ref, left_ref):
    def row(index):
        return x_ref[k, pl.ds(pl.multiple_of(index * blocks, blocks), blocks), :]

    total = row(first)
    for step in range(1, WMAX + 1):
        total = total + jnp.where(step <= half_width, row(first - step) + row(first + step), 0.0)
    for i in range(count):
        high, low = first + i + half_width, first + i - half_width
        rim_high, edge_high, edge_low, rim_low = row(high + 1), row(high), row(low), row(low - 1)
        values = (total, (rim_high + edge_high) - (edge_low + rim_low),
                  (rim_high - edge_high) - (edge_low - rim_low))
        total = total + (rim_high - edge_low)
        here = slice(i * blocks, (i + 1) * blocks)
        for field, value in enumerate(values):
            for part, piece in enumerate(split(value, PARTS[field])):
                left_ref[field, here, part * LANES:(part + 1) * LANES] = piece


def multiply(half_width, field, length, band_ref, left_ref):
    weight = jnp.concatenate([band_ref[half_width - 1, field]] * PARTS[field], axis=0)
    return jnp.dot(left_ref[field, :length, :PARTS[field] * LANES], weight, preferred_element_type=F32)


def combine(k, field, near, scale, blocks, product, beside_ref, entry_ref):
    pitch = blocks + SUB
    count = product.shape[0] // blocks
    left_lane = lax.broadcasted_iota(jnp.int32, (blocks, LANES), 1) < LANES // 2
    factor = -0.25 * scale if field == 1 else -scale
    for at in range(count):
        beside_ref[field, pl.ds(at * pitch + SUB, blocks), :] = product[at * blocks:(at + 1) * blocks, LANES:]
    for at in range(count):
        beside = jnp.where(left_lane, beside_ref[field, pl.ds(at * pitch + SUB - 1, blocks), :],
                           beside_ref[field, pl.ds(at * pitch + SUB + 1, blocks), :])
        value = factor * (product[at * blocks:(at + 1) * blocks, :LANES] + beside)
        entry_ref[k, field, pl.ds(at * blocks, blocks), :] = value if field == 1 else value + near


def sweep(planes, length, near_of, entry_ref, conv_ref, start, finish):
    step = next(count * SUB for count in (4, 3, 2, 1) if length % (count * SUB) == 0)

    def part(index, carry):
        where = pl.ds(pl.multiple_of(index * step, SUB), step)
        now, then = (None, None) if start is None else start(where)
        for k in range(planes):
            xx, xy, yy = [entry_ref[k, i, where, :] for i in range(3)]
            kept = 1.0 - near_of(k)
            if now is None:
                one, zero = jnp.ones((step, LANES), F32), jnp.zeros((step, LANES), F32)
                now, new = [one, zero, zero, one], [xx + kept, xy, xy, yy + kept]
            else:
                new = [
                    xx * now[0] + xy * now[2],
                    xx * now[1] + xy * now[3],
                    xy * now[0] + yy * now[2],
                    xy * now[1] + yy * now[3],
                ]
                if then is None:
                    new = [new[0] + kept, new[1], new[2], new[3] + kept]
                else:
                    new = [value + kept * old for value, old in zip(new, then)]
            then = now if k or start is not None else None
            now = new
            conv_ref[k, where, :] = 1.0 - 0.5 * (new[0] + new[3])
        if finish is not None:
            finish(where, now + then)
        return carry

    lax.fori_loop(0, length // step, part, 0)


def packed_state(state):
    a00, a01, a10, a11, b00, b01, b10, b11 = state
    p = [a00 + b01, a10 + b11, a01 - b00, a11 - b10]
    q = [a00 - b01, a10 - b11, a01 + b00, a11 + b10]
    most = jnp.maximum(jnp.maximum(jnp.abs(q[0]), jnp.abs(q[1])), jnp.maximum(jnp.abs(q[2]), jnp.abs(q[3])))
    scale = 1.0 / jnp.maximum(most, TINY)
    q = [value * scale for value in q]
    side = q[0] * q[0] + q[1] * q[1] + q[2] * q[2]
    reach = jnp.sqrt(side + q[3] * q[3]) + jnp.abs(q[3])
    ahead = q[3] >= 0.0
    factor = jnp.where(ahead, 1.0, reach) / jnp.where(ahead, jnp.maximum(reach, TINY), jnp.maximum(side, POLE))
    at_pole = jnp.logical_and(jnp.logical_not(ahead), side < POLE)
    u = [value * factor for value in q[:3]]
    return p + [jnp.where(at_pole, FAR, u[0]), u[1], u[2]]


def unpacked_state(values):
    p, u = values[:4], values[4:]
    most = jnp.maximum(jnp.maximum(jnp.abs(p[0]), jnp.abs(p[1])), jnp.maximum(jnp.abs(p[2]), jnp.abs(p[3])))
    bound = jnp.maximum(most, TINY)
    scale = 1.0 / bound
    unit = [value * scale for value in p]
    norm = bound * jnp.sqrt((unit[0] * unit[0] + unit[1] * unit[1]) + (unit[2] * unit[2] + unit[3] * unit[3]))
    square = u[0] * u[0] + u[1] * u[1] + u[2] * u[2]
    share = 1.0 / (1.0 + square)
    q = [norm * (2.0 * share * value) for value in u] + [norm * ((1.0 - square) * share)]
    half = lambda a, b: 0.5 * (a + b)
    now = [half(p[0], q[0]), half(p[2], q[2]), half(p[1], q[1]), half(p[3], q[3])]
    then = [half(q[2], -p[2]), half(p[0], -q[0]), half(q[3], -p[3]), half(p[1], -q[1])]
    return now, then


def writer(state_ref):
    def finish(where, state):
        for i, value in enumerate(packed_state(state)):
            state_ref[i, where, :] = value

    return finish


def steps_of(planes, shares):
    count = planes // SHARES
    per = next(n for n in range(max(1, TOGETHER // len(shares)), 0, -1) if count % n == 0)
    return count // per, per


def group_stage(sizes, part, scalars, x_ref, band_ref, scratch, entry_ref, before_plane=None,
                shares=tuple(range(SHARES))):
    planes, rows, blocks = sizes
    widths, slots, near, lens = scalars
    left_refs, beside_refs = scratch[::2], scratch[1::2]
    first, count = first_row(rows, part) + RIM, group_sizes(rows)[part]
    steps, per = steps_of(planes, shares)
    for beside_ref in beside_refs:
        beside_ref[...] = jnp.zeros(beside_ref.shape, F32)

    def step(index, carry):
        ks = []
        for i in range(per):
            for share in shares:
                place = index * per + i
                ks.append(place * SHARES + share)
                if before_plane is not None:
                    before_plane(share, place, ks[-1])
        for k, left_ref in zip(ks, left_refs):
            build(k, widths[k], first, count, blocks, x_ref, left_ref)
        for field in range(3):
            for k, left_ref, beside_ref in zip(ks, left_refs, beside_refs):
                width = (2 * widths[k] + 1).astype(F32)
                combine(k, field, near[slots[k]], lens[slots[k]] / (width * width), blocks,
                        multiply(widths[k], field, count * blocks, band_ref, left_ref), beside_ref, entry_ref)
        return carry

    lax.fori_loop(0, steps, step, 0)


def is_first():
    return lax.axis_index("depth") == 0


def first_sweep(sizes, part, scalars, entry_ref, conv_ref, state_ref):
    planes, rows, blocks = sizes
    widths, slots, near, lens = scalars

    @pl.when(is_first())
    def _():
        sweep(planes, group_sizes(rows)[part] * blocks, lambda k: near[slots[k]], entry_ref, conv_ref, None,
              writer(state_ref))


def each_plane(planes, body):
    def step(place, carry):
        for share in range(SHARES):
            body(share, place, place * SHARES + share)
        return carry

    lax.fori_loop(0, planes // SHARES, step, 0)


def first_kernel(sizes, widths_hbm, slots_hbm, near_hbm, lens_hbm, potential_hbm, x_ref, band_ref, entry_ref, conv_ref,
                 state_ref, near_ref, far_ref, *rest):
    planes, rows, blocks = sizes
    paired_refs, scratch = rest[:SHARES], rest[SHARES:]
    scratch, (tiles_ref, widths, slots, near, lens, plane_sems, table_sems) = scratch[:-7], scratch[-7:]
    tables = ((widths_hbm, widths), (slots_hbm, slots), (near_hbm, near), (lens_hbm, lens))
    copies = [pltpu.make_async_copy(*pair, table_sems.at[i]) for i, pair in enumerate(tables)]
    for copy in copies:
        copy.start()

    def plane_copy(k):
        return pltpu.make_async_copy(potential_hbm.at[k], tiles_ref.at[k, pl.ds(0, rows * blocks)], plane_sems.at[k])

    for k in range(planes):
        plane_copy(k).start()
    make_bands(band_ref)
    for copy in copies:
        copy.wait()

    def arrive(share, place, k):
        plane_copy(k).wait()
        for row in range(rows):
            for half in range(blocks // SUB):
                start = (row // SUB) * SUB * blocks + half * SUB * SUB + row % SUB
                x_ref[k, pl.ds((row + RIM) * blocks + half * SUB, SUB), :] = tiles_ref[
                    k, pl.ds(start, SUB, stride=SUB), :]
        for part, ref, at in ((2, paired_refs[share], place), (3, near_ref, k), (4, far_ref, k)):
            start, count = sent_rows(rows, part)
            ref[at] = x_ref[k, pl.ds(pl.multiple_of((start + RIM) * blocks, blocks), count * blocks), :]

    scalars = (widths, slots, near, lens)

    @pl.when(is_first())
    def _():
        group_stage(sizes, 0, scalars, x_ref, band_ref, scratch, entry_ref, arrive)

    @pl.when(jnp.logical_not(is_first()))
    def _():
        each_plane(planes, arrive)

    first_sweep(sizes, 0, scalars, entry_ref, conv_ref, state_ref)


def second_kernel(sizes, widths, slots, near, lens, band_ref, x_ref, entry_ref, conv_ref, state_ref, *scratch):
    scalars = (widths, slots, near, lens)
    group_stage(sizes, 1, scalars, x_ref, band_ref, scratch, entry_ref)
    first_sweep(sizes, 1, scalars, entry_ref, conv_ref, state_ref)


def border_kernel(sizes, part, widths, slots, near, lens, band_ref, x_in, *refs):
    planes, rows, blocks = sizes
    made_up = part in MADE_UP
    arrived, refs = refs[made_up:made_up + (SHARES if part == 2 else 1)], refs[made_up + (SHARES if part == 2 else 1) + (part in BEHIND):]
    x_ref, entry_ref, conv_ref, state_ref, *scratch = refs
    start, count = got_rows(rows, part)
    scalars = (widths, slots, near, lens)

    def arrive(share, place, k):
        rows_in = arrived[share][place] if part == 2 else arrived[0][k]
        x_ref[k, pl.ds(pl.multiple_of((start + RIM) * blocks, blocks), count * blocks), :] = rows_in

    if made_up:
        other_ref, scratch = scratch[0], scratch[1:]
    if part in MADE_UP.values():

        @pl.when(is_first())
        def _():
            group_stage(sizes, part, scalars, x_ref, band_ref, scratch, entry_ref, arrive)

        @pl.when(jnp.logical_not(is_first()))
        def _():
            each_plane(planes, arrive)

    else:
        group_stage(sizes, part, scalars, x_ref, band_ref, scratch, entry_ref, arrive)
    if made_up:

        @pl.when(jnp.logical_not(is_first()))
        def _():
            group_stage(sizes, MADE_UP[part], scalars, x_ref, band_ref, scratch, other_ref)

    first_sweep(sizes, part, scalars, entry_ref, conv_ref, state_ref)


def resume(sizes, part, turn, slots, near, entry_ref, incoming, conv_ref, finish):
    planes, rows, blocks = sizes

    @pl.when(lax.axis_index("depth") == turn)
    def _():
        sweep(planes, group_sizes(rows)[part] * blocks, lambda k: near[slots[k]], entry_ref, conv_ref,
              lambda where: unpacked_state([incoming[i, where, :] for i in range(SENT)]), finish)


def resume_kernel(sizes, part, turn, slots, near, entry_ref, incoming, conv_in, behind, conv_ref, *state_ref):
    resume(sizes, part, turn, slots, near, entry_ref, incoming, conv_ref, writer(state_ref[0]) if state_ref else None)


def place_rows(sizes, part, k, conv_ref, tiles_ref):
    planes, rows, blocks = sizes
    start = first_row(rows, part)
    for i in range(group_sizes(rows)[part]):
        row = start + i
        for half in range(blocks // SUB):
            to = lax.div(row, SUB) * SUB * blocks + half * SUB * SUB + lax.rem(row, SUB)
            tiles_ref[k, pl.ds(to, SUB, stride=SUB), :] = conv_ref[k, pl.ds(i * blocks + half * SUB, SUB), :]


def write_out(sizes, late, tiles_ref, out_hbm, sems, before_plane):
    planes, rows, blocks = sizes
    even = is_even()
    tail = -(-FINAL_ROWS // SUB) * SUB
    if late:
        start, count = jnp.where(even, 0, rows - tail), tail
    else:
        start, count = jnp.where(even, tail, 0), rows - tail

    def plane_copy(k):
        where = pl.ds(pl.multiple_of(start * blocks, SUB * blocks), count * blocks)
        return pltpu.make_async_copy(tiles_ref.at[k, where], out_hbm.at[k, where], sems.at[k])

    def plane(k, carry):
        before_plane(k)
        plane_copy(k).start()
        return carry

    lax.fori_loop(0, planes, plane, 0)
    for k in range(planes):
        plane_copy(k).wait()


def early_kernel(sizes, *refs):
    *conv_refs, tiles_ref, out_hbm, sems = refs

    def place(k):
        for part, conv_ref in enumerate(conv_refs):
            place_rows(sizes, part, k, conv_ref, tiles_ref)

    write_out(sizes, False, tiles_ref, out_hbm, sems, place)


def last_kernel(sizes, part, turn, slots, near, entry_ref, incoming, conv_in, tiles_in, out_in, conv_ref, tiles_ref,
                out_hbm, sems):
    resume(sizes, part, turn, slots, near, entry_ref, incoming, conv_ref, None)
    write_out(sizes, True, tiles_ref, out_hbm, sems, lambda k: place_rows(sizes, part, k, conv_ref, tiles_ref))


def per_device(potential, widths, plane_slot, ratio_near, ratio_lens):
    planes, rows, cols = potential.shape
    blocks = cols // LANES
    sizes = (planes, rows, blocks)
    counts = group_sizes(rows)
    parts = len(counts)
    depth_count, sky_count = lax.axis_size("depth"), lax.axis_size("sky")
    swaps = [[pair for i in range(first, sky_count - 1, 2) for pair in ((i, i + 1), (i + 1, i))] for first in (0, 1)]
    ahead = [(i, i + 1) for i in range(depth_count - 1)]
    tiled = potential.reshape(planes, rows // SUB, SUB, blocks, LANES).transpose(0, 1, 3, 2, 4)
    tiled = tiled.reshape(planes, rows * blocks, LANES)
    smem = pl.BlockSpec(memory_space=pltpu.SMEM)
    vmem = pl.BlockSpec(memory_space=pltpu.VMEM)
    anywhere = pl.BlockSpec(memory_space=pl.ANY)
    params = pltpu.CompilerParams(vmem_limit_bytes=VMEM_LIMIT)
    scalars = (widths, plane_slot, ratio_near, ratio_lens)
    dma = pltpu.SemaphoreType.DMA
    cost = pl.CostEstimate(flops=1, transcendentals=0, bytes_accessed=1)

    def held(*shape, dtype=F32):
        return pltpu.VMEM(shape, dtype)

    tiles_shape = held(planes, rows * blocks + SUB * SUB, LANES)

    def moved(*shape):
        return jax.ShapeDtypeStruct(shape, F32)

    def in_vmem(array):
        return pltpu.with_memory_space_constraint(array, pltpu.VMEM)

    def in_hbm(array):
        return pltpu.with_memory_space_constraint(array, pltpu.HBM)

    x_shape = held(planes, (rows + 2 * RIM) * blocks, LANES)
    band_shape = held(WMAX, 3, LANES, 2 * LANES, dtype=BF16)

    def entry_shape(part):
        return held(planes, 3, counts[part] * blocks, LANES)

    def conv_shape(part):
        return held(planes, counts[part] * blocks, LANES)

    def state_shape(part):
        return moved(SENT, counts[part] * blocks, LANES)

    def group_shapes(part):
        return [entry_shape(part), conv_shape(part), state_shape(part)]

    def group_scratch(part):
        count = max(counts[part], counts[MADE_UP[part]] if part in MADE_UP else 0)
        return [held(3, count * blocks, max(PARTS) * LANES, dtype=BF16),
                held(3, (count + 1) * (blocks + SUB), LANES)] * (SHARES * steps_of(planes, range(SHARES))[1])

    def side_shape(part, shares=1):
        return moved(planes // shares, sent_rows(rows, part)[1] * blocks, LANES)

    x, bands, entry, conv, state, close, far, *paired = pl.pallas_call(
        functools.partial(first_kernel, sizes),
        out_shape=[x_shape, band_shape, *group_shapes(0), side_shape(3), side_shape(4), *[side_shape(2, SHARES)] * SHARES],
        in_specs=[anywhere] * 5,
        out_specs=[vmem] * (7 + SHARES),
        scratch_shapes=[
            *group_scratch(0), tiles_shape,
            *[pltpu.SMEM(array.shape, array.dtype) for array in scalars], dma((planes,)), dma((len(scalars),))],
        compiler_params=params,
        cost_estimate=cost,
        name="first",
    )(*[in_hbm(array) for array in (*scalars, tiled)])
    entries, convs, arriving = [entry], [conv], [lax.ppermute(state, "depth", ahead)]
    entry, conv, state = pl.pallas_call(
        functools.partial(second_kernel, sizes),
        out_shape=group_shapes(1),
        in_specs=[smem] * 4 + [vmem] * 2,
        out_specs=[vmem] * 3,
        scratch_shapes=group_scratch(1),
        compiler_params=params,
        cost_estimate=cost,
        name="second",
    )(*scalars, in_vmem(bands), in_vmem(x))
    entries.append(entry)
    convs.append(conv)
    arriving.append(lax.ppermute(state, "depth", ahead))
    swapped = {part: [lax.ppermute(piece, "sky", swaps[part > 2]) for piece in pieces]
               for part, pieces in ((2, paired), (3, [close]), (4, [far]))}
    for part in range(2, parts):
        other = [entries[MADE_UP[part]]] if part in MADE_UP else []
        x, entry, conv, state, *again = pl.pallas_call(
            functools.partial(border_kernel, sizes, part),
            out_shape=[x_shape, *group_shapes(part), *[entry_shape(MADE_UP[part]) for _ in other]],
            in_specs=[smem] * 4 + [vmem] * (2 + len(other) + len(swapped[part])) + [anywhere] * (part in BEHIND),
            out_specs=[vmem] * (4 + len(other)),
            scratch_shapes=group_scratch(part),
            input_output_aliases={5: 0} | ({6: 4} if other else {}),
            compiler_params=params,
            cost_estimate=cost,
            name="border",
        )(*scalars, in_vmem(bands), in_vmem(x), *map(in_vmem, other), *swapped[part], *[arriving[BEHIND[part]] for _ in range(part in BEHIND)])
        if other:
            entries[MADE_UP[part]], = again
        entries.append(entry)
        convs.append(conv)
        arriving.append(lax.ppermute(state, "depth", ahead))

    for turn in range(1, depth_count):
        last = turn == depth_count - 1
        for part in range(parts - last):
            convs[part], *state = pl.pallas_call(
                functools.partial(resume_kernel, sizes, part, turn),
                out_shape=[conv_shape(part)] + ([] if last else [state_shape(part)]),
                in_specs=[smem] * 2 + [vmem] * 4,
                out_specs=[vmem] * (1 if last else 2),
                input_output_aliases={4: 0},
                compiler_params=params,
                cost_estimate=cost,
                name="resume",
            )(plane_slot, ratio_near, in_vmem(entries[part]), arriving[part], in_vmem(convs[part]),
              in_vmem(convs[part - 1]))
            if state:
                arriving[part] = lax.ppermute(state[0], "depth", ahead)
    out_shape = moved(planes, rows * blocks, LANES)
    tiles, out = pl.pallas_call(
        functools.partial(early_kernel, sizes),
        out_shape=[tiles_shape, out_shape],
        in_specs=[vmem] * (parts - 1),
        out_specs=[vmem, anywhere],
        scratch_shapes=[dma((planes,))],
        compiler_params=params,
        cost_estimate=cost,
        name="early",
    )(*[in_vmem(conv) for conv in convs[:-1]])
    conv, tiles, out = pl.pallas_call(
        functools.partial(last_kernel, sizes, parts - 1, depth_count - 1),
        out_shape=[conv_shape(parts - 1), tiles_shape, out_shape],
        in_specs=[smem] * 2 + [vmem] * 4 + [anywhere],
        out_specs=[vmem, vmem, anywhere],
        scratch_shapes=[dma((planes,))],
        input_output_aliases={4: 0, 5: 1, 6: 2},
        compiler_params=params,
        cost_estimate=cost,
        name="last",
    )(plane_slot, ratio_near, in_vmem(entries[-1]), arriving[-1], in_vmem(convs[-1]), in_vmem(tiles), out)
    out = out.reshape(planes, rows // SUB, blocks, SUB, LANES).transpose(0, 1, 3, 2, 4)
    return out.reshape(planes, rows, cols)


def solution(mesh):
    return jax.shard_map(
        per_device,
        mesh=mesh,
        in_specs=(P("depth", "sky", None), P("depth"), P("depth"), P(), P()),
        out_specs=P("depth", "sky", None),
        check_vma=False,
    )
```

```python
import functools

import jax
import jax.numpy as jnp
from jax import lax
from jax.experimental import pallas as pl
from jax.experimental.pallas import tpu as pltpu
from jax.sharding import PartitionSpec as P

WMAX = 8
RIM = WMAX + 1
LANES = 128
SUB = 8
INNER_ROWS, FINAL_ROWS = 8, 3
TOGETHER = 6
PARTS = (3, 2, 2)
MADE_UP = {3: 0, 4: 2}
BEHIND = {2: 0, 3: 1}
SHARES = 2
SENT = 7
TINY, POLE, FAR = 1e-30, 1e-20, 1e10
VMEM_LIMIT = 16 * 1024 * 1024
F32, BF16 = jnp.float32, jnp.bfloat16


def group_sizes(row_count):
    return (INNER_ROWS, row_count - 2 * RIM - INNER_ROWS, RIM, RIM - FINAL_ROWS, FINAL_ROWS)


def is_even():
    return lax.rem(lax.axis_index("sky"), 2) == 0


def by_side(paired, low, high):
    return jnp.where(is_even() != paired, low, high)


def first_row(row_count, part):
    if part < 2:
        return (RIM, RIM + INNER_ROWS)[part]
    if part == 2:
        return by_side(True, 0, row_count - RIM)
    if part == 3:
        return by_side(False, FINAL_ROWS, row_count - RIM)
    return by_side(False, 0, row_count - FINAL_ROWS)


def sent_rows(row_count, part):
    near = RIM - FINAL_ROWS
    if part == 2:
        return by_side(True, 0, row_count - RIM), RIM
    if part == 3:
        return by_side(False, 0, row_count - near), near
    return by_side(False, near, row_count - RIM), FINAL_ROWS


def got_rows(row_count, part):
    near = RIM - FINAL_ROWS
    if part == 2:
        return by_side(True, -RIM, row_count), RIM
    if part == 3:
        return by_side(False, -near, row_count), near
    return by_side(False, -RIM, row_count + near), FINAL_ROWS


def split(value, parts):
    found = []
    for part in range(parts):
        found.append(value.astype(BF16))
        if part + 1 < parts:
            value = value - found[-1].astype(F32)
    return found


def make_bands(band_ref):
    source = lax.broadcasted_iota(jnp.int32, (LANES, 2 * LANES), 0)
    target = lax.broadcasted_iota(jnp.int32, (LANES, 2 * LANES), 1)
    across = jnp.where(target >= LANES + LANES // 2, source + 2 * LANES, source)
    offset = across - target
    distance = jnp.abs(offset)

    def width(index, carry):
        half_width = index + 1
        rim = (distance == half_width + 1).astype(F32)
        edge = (distance == half_width).astype(F32)
        inside = (distance <= half_width).astype(F32)
        both = rim + edge
        for field, value in enumerate((rim - edge, jnp.where(offset > 0, both, -both), inside)):
            band_ref[index, field] = value.astype(BF16)
        return carry

    lax.fori_loop(0, WMAX, width, 0)


def build(k, half_width, first, count, blocks, x_ref, left_ref):
    def row(index):
        return x_ref[k, pl.ds(pl.multiple_of(index * blocks, blocks), blocks), :]

    total = row(first)
    for step in range(1, WMAX + 1):
        total = total + jnp.where(step <= half_width, row(first - step) + row(first + step), 0.0)
    for i in range(count):
        high, low = first + i + half_width, first + i - half_width
        rim_high, edge_high, edge_low, rim_low = row(high + 1), row(high), row(low), row(low - 1)
        values = (total, (rim_high + edge_high) - (edge_low + rim_low),
                  (rim_high - edge_high) - (edge_low - rim_low))
        total = total + (rim_high - edge_low)
        here = slice(i * blocks, (i + 1) * blocks)
        for field, value in enumerate(values):
            for part, piece in enumerate(split(value, PARTS[field])):
                left_ref[field, here, part * LANES:(part + 1) * LANES] = piece


def multiply(half_width, field, length, band_ref, left_ref):
    weight = jnp.concatenate([band_ref[half_width - 1, field]] * PARTS[field], axis=0)
    return jnp.dot(left_ref[field, :length, :PARTS[field] * LANES], weight, preferred_element_type=F32)


def combine(k, field, near, scale, blocks, product, beside_ref, entry_ref):
    pitch = blocks + SUB
    count = product.shape[0] // blocks
    left_lane = lax.broadcasted_iota(jnp.int32, (blocks, LANES), 1) < LANES // 2
    factor = -0.25 * scale if field == 1 else -scale
    for at in range(count):
        beside_ref[field, pl.ds(at * pitch + SUB, blocks), :] = product[at * blocks:(at + 1) * blocks, LANES:]
    for at in range(count):
        beside = jnp.where(left_lane, beside_ref[field, pl.ds(at * pitch + SUB - 1, blocks), :],
                           beside_ref[field, pl.ds(at * pitch + SUB + 1, blocks), :])
        value = factor * (product[at * blocks:(at + 1) * blocks, :LANES] + beside)
        entry_ref[k, field, pl.ds(at * blocks, blocks), :] = value if field == 1 else value + near


def sweep(planes, length, near_of, entry_ref, conv_ref, start, finish):
    step = next(count * SUB for count in (4, 3, 2, 1) if length % (count * SUB) == 0)

    def part(index, carry):
        where = pl.ds(pl.multiple_of(index * step, SUB), step)
        now, then = (None, None) if start is None else start(where)
        for k in range(planes):
            xx, xy, yy = [entry_ref[k, i, where, :] for i in range(3)]
            kept = 1.0 - near_of(k)
            if now is None:
                one, zero = jnp.ones((step, LANES), F32), jnp.zeros((step, LANES), F32)
                now, new = [one, zero, zero, one], [xx + kept, xy, xy, yy + kept]
            else:
                new = [
                    xx * now[0] + xy * now[2],
                    xx * now[1] + xy * now[3],
                    xy * now[0] + yy * now[2],
                    xy * now[1] + yy * now[3],
                ]
                if then is None:
                    new = [new[0] + kept, new[1], new[2], new[3] + kept]
                else:
                    new = [value + kept * old for value, old in zip(new, then)]
            then = now if k or start is not None else None
            now = new
            conv_ref[k, where, :] = 1.0 - 0.5 * (new[0] + new[3])
        if finish is not None:
            finish(where, now + then)
        return carry

    lax.fori_loop(0, length // step, part, 0)


def packed_state(state):
    a00, a01, a10, a11, b00, b01, b10, b11 = state
    p = [a00 + b01, a10 + b11, a01 - b00, a11 - b10]
    q = [a00 - b01, a10 - b11, a01 + b00, a11 + b10]
    most = jnp.maximum(jnp.maximum(jnp.abs(q[0]), jnp.abs(q[1])), jnp.maximum(jnp.abs(q[2]), jnp.abs(q[3])))
    scale = 1.0 / jnp.maximum(most, TINY)
    q = [value * scale for value in q]
    side = q[0] * q[0] + q[1] * q[1] + q[2] * q[2]
    reach = jnp.sqrt(side + q[3] * q[3]) + jnp.abs(q[3])
    ahead = q[3] >= 0.0
    factor = jnp.where(ahead, 1.0, reach) / jnp.where(ahead, jnp.maximum(reach, TINY), jnp.maximum(side, POLE))
    at_pole = jnp.logical_and(jnp.logical_not(ahead), side < POLE)
    u = [value * factor for value in q[:3]]
    return p + [jnp.where(at_pole, FAR, u[0]), u[1], u[2]]


def unpacked_state(values):
    p, u = values[:4], values[4:]
    most = jnp.maximum(jnp.maximum(jnp.abs(p[0]), jnp.abs(p[1])), jnp.maximum(jnp.abs(p[2]), jnp.abs(p[3])))
    bound = jnp.maximum(most, TINY)
    scale = 1.0 / bound
    unit = [value * scale for value in p]
    norm = bound * jnp.sqrt((unit[0] * unit[0] + unit[1] * unit[1]) + (unit[2] * unit[2] + unit[3] * unit[3]))
    square = u[0] * u[0] + u[1] * u[1] + u[2] * u[2]
    share = 1.0 / (1.0 + square)
    q = [norm * (2.0 * share * value) for value in u] + [norm * ((1.0 - square) * share)]
    half = lambda a, b: 0.5 * (a + b)
    now = [half(p[0], q[0]), half(p[2], q[2]), half(p[1], q[1]), half(p[3], q[3])]
    then = [half(q[2], -p[2]), half(p[0], -q[0]), half(q[3], -p[3]), half(p[1], -q[1])]
    return now, then


def writer(state_ref):
    def finish(where, state):
        for i, value in enumerate(packed_state(state)):
            state_ref[i, where, :] = value

    return finish


def steps_of(planes, shares):
    count = planes // SHARES
    per = next(n for n in range(max(1, TOGETHER // len(shares)), 0, -1) if count % n == 0)
    return count // per, per


def group_stage(sizes, part, scalars, x_ref, band_ref, scratch, entry_ref, before_plane=None,
                shares=tuple(range(SHARES))):
    planes, rows, blocks = sizes
    widths, slots, near, lens = scalars
    left_refs, beside_refs = scratch[::2], scratch[1::2]
    first, count = first_row(rows, part) + RIM, group_sizes(rows)[part]
    steps, per = steps_of(planes, shares)
    for beside_ref in beside_refs:
        for at in range(count + 1):
            beside_ref[:, pl.ds(at * (blocks + SUB), SUB), :] = jnp.zeros((3, SUB, LANES), F32)

    def step(index, carry):
        ks = []
        for i in range(per):
            for share in shares:
                place = index * per + i
                ks.append(place * SHARES + share)
                if before_plane is not None:
                    before_plane(share, place, ks[-1])
        for k, left_ref in zip(ks, left_refs):
            build(k, widths[k], first, count, blocks, x_ref, left_ref)
        for field in range(3):
            for k, left_ref, beside_ref in zip(ks, left_refs, beside_refs):
                width = (2 * widths[k] + 1).astype(F32)
                combine(k, field, near[slots[k]], lens[slots[k]] / (width * width), blocks,
                        multiply(widths[k], field, count * blocks, band_ref, left_ref), beside_ref, entry_ref)
        return carry

    lax.fori_loop(0, steps, step, 0)


def is_first():
    return lax.axis_index("depth") == 0


def first_sweep(sizes, part, scalars, entry_ref, conv_ref, state_ref):
    planes, rows, blocks = sizes
    widths, slots, near, lens = scalars

    @pl.when(is_first())
    def _():
        sweep(planes, group_sizes(rows)[part] * blocks, lambda k: near[slots[k]], entry_ref, conv_ref, None,
              writer(state_ref))


def each_plane(planes, body):
    def step(place, carry):
        for share in range(SHARES):
            body(share, place, place * SHARES + share)
        return carry

    lax.fori_loop(0, planes // SHARES, step, 0)


def first_kernel(sizes, widths_hbm, slots_hbm, near_hbm, lens_hbm, potential_hbm, x_ref, band_ref, entry_ref, conv_ref,
                 state_ref, near_ref, far_ref, *rest):
    planes, rows, blocks = sizes
    paired_refs, scratch = rest[:SHARES], rest[SHARES:]
    scratch, (tiles_ref, widths, slots, near, lens, plane_sems, table_sems) = scratch[:-7], scratch[-7:]
    tables = ((widths_hbm, widths), (slots_hbm, slots), (near_hbm, near), (lens_hbm, lens))
    copies = [pltpu.make_async_copy(*pair, table_sems.at[i]) for i, pair in enumerate(tables)]
    for copy in copies:
        copy.start()

    def plane_copy(k):
        return pltpu.make_async_copy(potential_hbm.at[k], tiles_ref.at[k, pl.ds(0, rows * blocks)], plane_sems.at[k])

    for k in range(planes):
        plane_copy(k).start()
    make_bands(band_ref)
    for copy in copies:
        copy.wait()

    def arrive(share, place, k):
        plane_copy(k).wait()
        for row in range(rows):
            for half in range(blocks // SUB):
                start = (row // SUB) * SUB * blocks + half * SUB * SUB + row % SUB
                x_ref[k, pl.ds((row + RIM) * blocks + half * SUB, SUB), :] = tiles_ref[
                    k, pl.ds(start, SUB, stride=SUB), :]
        for part, ref, at in ((2, paired_refs[share], place), (3, near_ref, k), (4, far_ref, k)):
            start, count = sent_rows(rows, part)
            ref[at] = x_ref[k, pl.ds(pl.multiple_of((start + RIM) * blocks, blocks), count * blocks), :]

    scalars = (widths, slots, near, lens)

    @pl.when(is_first())
    def _():
        group_stage(sizes, 0, scalars, x_ref, band_ref, scratch, entry_ref, arrive)

    @pl.when(jnp.logical_not(is_first()))
    def _():
        each_plane(planes, arrive)

    first_sweep(sizes, 0, scalars, entry_ref, conv_ref, state_ref)


def second_kernel(sizes, widths, slots, near, lens, band_ref, x_ref, entry_ref, conv_ref, state_ref, *scratch):
    scalars = (widths, slots, near, lens)
    group_stage(sizes, 1, scalars, x_ref, band_ref, scratch, entry_ref)
    first_sweep(sizes, 1, scalars, entry_ref, conv_ref, state_ref)


def border_kernel(sizes, part, widths, slots, near, lens, band_ref, x_in, *refs):
    planes, rows, blocks = sizes
    made_up = part in MADE_UP
    arrived, refs = refs[made_up:made_up + (SHARES if part == 2 else 1)], refs[made_up + (SHARES if part == 2 else 1) + (part in BEHIND):]
    x_ref, entry_ref, conv_ref, state_ref, *scratch = refs
    start, count = got_rows(rows, part)
    scalars = (widths, slots, near, lens)

    def arrive(share, place, k):
        rows_in = arrived[share][place] if part == 2 else arrived[0][k]
        x_ref[k, pl.ds(pl.multiple_of((start + RIM) * blocks, blocks), count * blocks), :] = rows_in

    if made_up:
        other_ref, scratch = scratch[0], scratch[1:]
    if part in MADE_UP.values():

        @pl.when(is_first())
        def _():
            group_stage(sizes, part, scalars, x_ref, band_ref, scratch, entry_ref, arrive)

        @pl.when(jnp.logical_not(is_first()))
        def _():
            each_plane(planes, arrive)

    else:
        group_stage(sizes, part, scalars, x_ref, band_ref, scratch, entry_ref, arrive)
    if made_up:

        @pl.when(jnp.logical_not(is_first()))
        def _():
            group_stage(sizes, MADE_UP[part], scalars, x_ref, band_ref, scratch, other_ref)

    first_sweep(sizes, part, scalars, entry_ref, conv_ref, state_ref)


def resume(sizes, part, turn, slots, near, entry_ref, incoming, conv_ref, finish):
    planes, rows, blocks = sizes

    @pl.when(lax.axis_index("depth") == turn)
    def _():
        sweep(planes, group_sizes(rows)[part] * blocks, lambda k: near[slots[k]], entry_ref, conv_ref,
              lambda where: unpacked_state([incoming[i, where, :] for i in range(SENT)]), finish)


def resume_kernel(sizes, part, turn, slots, near, entry_ref, incoming, conv_in, behind, conv_ref, *state_ref):
    resume(sizes, part, turn, slots, near, entry_ref, incoming, conv_ref, writer(state_ref[0]) if state_ref else None)


def place_rows(sizes, part, k, conv_ref, tiles_ref):
    planes, rows, blocks = sizes
    start = first_row(rows, part)
    for i in range(group_sizes(rows)[part]):
        row = start + i
        for half in range(blocks // SUB):
            to = lax.div(row, SUB) * SUB * blocks + half * SUB * SUB + lax.rem(row, SUB)
            tiles_ref[k, pl.ds(to, SUB, stride=SUB), :] = conv_ref[k, pl.ds(i * blocks + half * SUB, SUB), :]


def write_out(sizes, late, tiles_ref, out_hbm, sems, before_plane):
    planes, rows, blocks = sizes
    even = is_even()
    tail = -(-FINAL_ROWS // SUB) * SUB
    if late:
        start, count = jnp.where(even, 0, rows - tail), tail
    else:
        start, count = jnp.where(even, tail, 0), rows - tail

    def plane_copy(k):
        where = pl.ds(pl.multiple_of(start * blocks, SUB * blocks), count * blocks)
        return pltpu.make_async_copy(tiles_ref.at[k, where], out_hbm.at[k, where], sems.at[k])

    def plane(k, carry):
        before_plane(k)
        plane_copy(k).start()
        return carry

    lax.fori_loop(0, planes, plane, 0)
    for k in range(planes):
        plane_copy(k).wait()


def early_kernel(sizes, *refs):
    *conv_refs, tiles_ref, out_hbm, sems = refs

    def place(k):
        for part, conv_ref in enumerate(conv_refs):
            place_rows(sizes, part, k, conv_ref, tiles_ref)

    write_out(sizes, False, tiles_ref, out_hbm, sems, place)


def last_kernel(sizes, part, turn, slots, near, entry_ref, incoming, conv_in, tiles_in, out_in, conv_ref, tiles_ref,
                out_hbm, sems):
    resume(sizes, part, turn, slots, near, entry_ref, incoming, conv_ref, None)
    write_out(sizes, True, tiles_ref, out_hbm, sems, lambda k: place_rows(sizes, part, k, conv_ref, tiles_ref))


def per_device(potential, widths, plane_slot, ratio_near, ratio_lens):
    planes, rows, cols = potential.shape
    blocks = cols // LANES
    sizes = (planes, rows, blocks)
    counts = group_sizes(rows)
    parts = len(counts)
    depth_count, sky_count = lax.axis_size("depth"), lax.axis_size("sky")
    swaps = [[pair for i in range(first, sky_count - 1, 2) for pair in ((i, i + 1), (i + 1, i))] for first in (0, 1)]
    ahead = [(i, i + 1) for i in range(depth_count - 1)]
    tiled = potential.reshape(planes, rows // SUB, SUB, blocks, LANES).transpose(0, 1, 3, 2, 4)
    tiled = tiled.reshape(planes, rows * blocks, LANES)
    smem = pl.BlockSpec(memory_space=pltpu.SMEM)
    vmem = pl.BlockSpec(memory_space=pltpu.VMEM)
    anywhere = pl.BlockSpec(memory_space=pl.ANY)
    params = pltpu.CompilerParams(vmem_limit_bytes=VMEM_LIMIT)
    scalars = (widths, plane_slot, ratio_near, ratio_lens)
    dma = pltpu.SemaphoreType.DMA
    cost = pl.CostEstimate(flops=1, transcendentals=0, bytes_accessed=1)

    def held(*shape, dtype=F32):
        return pltpu.VMEM(shape, dtype)

    tiles_shape = held(planes, rows * blocks + SUB * SUB, LANES)

    def moved(*shape):
        return jax.ShapeDtypeStruct(shape, F32)

    def in_vmem(array):
        return pltpu.with_memory_space_constraint(array, pltpu.VMEM)

    def in_hbm(array):
        return pltpu.with_memory_space_constraint(array, pltpu.HBM)

    x_shape = held(planes, (rows + 2 * RIM) * blocks, LANES)
    band_shape = held(WMAX, 3, LANES, 2 * LANES, dtype=BF16)

    def entry_shape(part):
        return held(planes, 3, counts[part] * blocks, LANES)

    def conv_shape(part):
        return held(planes, counts[part] * blocks, LANES)

    def state_shape(part):
        return moved(SENT, counts[part] * blocks, LANES)

    def group_shapes(part):
        return [entry_shape(part), conv_shape(part), state_shape(part)]

    def group_scratch(part):
        count = max(counts[part], counts[MADE_UP[part]] if part in MADE_UP else 0)
        return [held(3, count * blocks, max(PARTS) * LANES, dtype=BF16),
                held(3, (count + 1) * (blocks + SUB), LANES)] * (SHARES * steps_of(planes, range(SHARES))[1])

    def side_shape(part, shares=1):
        return moved(planes // shares, sent_rows(rows, part)[1] * blocks, LANES)

    x, bands, entry, conv, state, close, far, *paired = pl.pallas_call(
        functools.partial(first_kernel, sizes),
        out_shape=[x_shape, band_shape, *group_shapes(0), side_shape(3), side_shape(4), *[side_shape(2, SHARES)] * SHARES],
        in_specs=[anywhere] * 5,
        out_specs=[vmem] * (7 + SHARES),
        scratch_shapes=[
            *group_scratch(0), tiles_shape,
            *[pltpu.SMEM(array.shape, array.dtype) for array in scalars], dma((planes,)), dma((len(scalars),))],
        compiler_params=params,
        cost_estimate=cost,
        name="first",
    )(*[in_hbm(array) for array in (*scalars, tiled)])
    entries, convs, arriving = [entry], [conv], [lax.ppermute(state, "depth", ahead)]
    entry, conv, state = pl.pallas_call(
        functools.partial(second_kernel, sizes),
        out_shape=group_shapes(1),
        in_specs=[smem] * 4 + [vmem] * 2,
        out_specs=[vmem] * 3,
        scratch_shapes=group_scratch(1),
        compiler_params=params,
        cost_estimate=cost,
        name="second",
    )(*scalars, in_vmem(bands), in_vmem(x))
    entries.append(entry)
    convs.append(conv)
    arriving.append(lax.ppermute(state, "depth", ahead))
    swapped = {part: [lax.ppermute(piece, "sky", swaps[part > 2]) for piece in pieces]
               for part, pieces in ((2, paired), (3, [close]), (4, [far]))}
    for part in range(2, parts):
        other = [entries[MADE_UP[part]]] if part in MADE_UP else []
        x, entry, conv, state, *again = pl.pallas_call(
            functools.partial(border_kernel, sizes, part),
            out_shape=[x_shape, *group_shapes(part), *[entry_shape(MADE_UP[part]) for _ in other]],
            in_specs=[smem] * 4 + [vmem] * (2 + len(other) + len(swapped[part])) + [anywhere] * (part in BEHIND),
            out_specs=[vmem] * (4 + len(other)),
            scratch_shapes=group_scratch(part),
            input_output_aliases={5: 0} | ({6: 4} if other else {}),
            compiler_params=params,
            cost_estimate=cost,
            name="border",
        )(*scalars, in_vmem(bands), in_vmem(x), *map(in_vmem, other), *swapped[part], *[arriving[BEHIND[part]] for _ in range(part in BEHIND)])
        if other:
            entries[MADE_UP[part]], = again
        entries.append(entry)
        convs.append(conv)
        arriving.append(lax.ppermute(state, "depth", ahead))

    for turn in range(1, depth_count):
        last = turn == depth_count - 1
        for part in range(parts - last):
            convs[part], *state = pl.pallas_call(
                functools.partial(resume_kernel, sizes, part, turn),
                out_shape=[conv_shape(part)] + ([] if last else [state_shape(part)]),
                in_specs=[smem] * 2 + [vmem] * 4,
                out_specs=[vmem] * (1 if last else 2),
                input_output_aliases={4: 0},
                compiler_params=params,
                cost_estimate=cost,
                name="resume",
            )(plane_slot, ratio_near, in_vmem(entries[part]), arriving[part], in_vmem(convs[part]),
              in_vmem(convs[part - 1]))
            if state:
                arriving[part] = lax.ppermute(state[0], "depth", ahead)
    out_shape = moved(planes, rows * blocks, LANES)
    tiles, out = pl.pallas_call(
        functools.partial(early_kernel, sizes),
        out_shape=[tiles_shape, out_shape],
        in_specs=[vmem] * (parts - 1),
        out_specs=[vmem, anywhere],
        scratch_shapes=[dma((planes,))],
        compiler_params=params,
        cost_estimate=cost,
        name="early",
    )(*[in_vmem(conv) for conv in convs[:-1]])
    conv, tiles, out = pl.pallas_call(
        functools.partial(last_kernel, sizes, parts - 1, depth_count - 1),
        out_shape=[conv_shape(parts - 1), tiles_shape, out_shape],
        in_specs=[smem] * 2 + [vmem] * 4 + [anywhere],
        out_specs=[vmem, vmem, anywhere],
        scratch_shapes=[dma((planes,))],
        input_output_aliases={4: 0, 5: 1, 6: 2},
        compiler_params=params,
        cost_estimate=cost,
        name="last",
    )(plane_slot, ratio_near, in_vmem(entries[-1]), arriving[-1], in_vmem(convs[-1]), in_vmem(tiles), out)
    out = out.reshape(planes, rows // SUB, blocks, SUB, LANES).transpose(0, 1, 3, 2, 4)
    return out.reshape(planes, rows, cols)


def solution(mesh):
    return jax.shard_map(
        per_device,
        mesh=mesh,
        in_specs=(P("depth", "sky", None), P("depth"), P("depth"), P(), P()),
        out_specs=P("depth", "sky", None),
        check_vma=False,
    )
```
